128 devices in a mesh: section: 4 (over x), ctx: 32 (over z, y, core).
Axes of the slice: x: 4, y: 4, z: 4, core: 2. Of those that a mesh axis runs over, the one named last changes fastest.
Arguments:
- inputs: bfloat16 [2, 1, 2048, 1024], P(None, None, 'ctx'), may hold values from -6 to 6
- cotangent: bfloat16 [2, 1, 2048, 1024], P(None, None, 'ctx'), may hold values from -6 to 6
- segment_ids: int32 [2, 1, 2048], replicated, may hold values from 0 to 2, as said below
- gains: bfloat16 [4, 1024], P('section', 'ctx'), may hold values from 0.25 to 1.75
- wq1: bfloat16 [1024, 1024], P('ctx', 'section'), may hold values from -0.1875 to 0.1875
- wk1: bfloat16 [1024, 1024], P('ctx', 'section'), may hold values from -0.1875 to 0.1875
- wv1: bfloat16 [1024, 1024], P('ctx', 'section'), may hold values from -0.1875 to 0.1875
- wo1: bfloat16 [1024, 1024], P('ctx', 'section'), may hold values from -3 to 3
- wg1: bfloat16 [1024, 2816], P('ctx', 'section'), may hold values from -0.1875 to 0.1875
- wu1: bfloat16 [1024, 2816], P('ctx', 'section'), may hold values from -0.1875 to 0.1875
- wd1: bfloat16 [2816, 1024], P('ctx', 'section'), may hold values from -0.109375 to 0.109375
- wq2: bfloat16 [1024, 1024], P('ctx', 'section'), may hold values from -0.1875 to 0.1875
- wk2: bfloat16 [1024, 1024], P('ctx', 'section'), may hold values from -0.1875 to 0.1875
- wv2: bfloat16 [1024, 1024], P('ctx', 'section'), may hold values from -0.1875 to 0.1875
- wo2: bfloat16 [1024, 1024], P('ctx', 'section'), may hold values from -3 to 3
- wg2: bfloat16 [1024, 2816], P('ctx', 'section'), may hold values from -0.1875 to 0.1875
- wu2: bfloat16 [1024, 2816], P('ctx', 'section'), may hold values from -0.1875 to 0.1875
- wd2: bfloat16 [2816, 1024], P('ctx', 'section'), may hold values from -0.109375 to 0.109375
Outputs:
- outputs: bfloat16 [2, 1, 2048, 1024], P(None, None, 'ctx', 'section')
- input_grads: bfloat16 [2, 1, 2048, 1024], P(None, None, 'ctx', 'section')
- gain_grads: float32 [4, 1024], P('section', 'ctx')
- grad_wq1: float32 [1024, 1024], P('ctx', 'section')
- grad_wk1: float32 [1024, 1024], P('ctx', 'section')
- grad_wv1: float32 [1024, 1024], P('ctx', 'section')
- grad_wo1: float32 [1024, 1024], P('ctx', 'section')
- grad_wg1: float32 [1024, 2816], P('ctx', 'section')
- grad_wu1: float32 [1024, 2816], P('ctx', 'section')
- grad_wd1: float32 [2816, 1024], P('ctx', 'section')
- grad_wq2: float32 [1024, 1024], P('ctx', 'section')
- grad_wk2: float32 [1024, 1024], P('ctx', 'section')
- grad_wv2: float32 [1024, 1024], P('ctx', 'section')
- grad_wo2: float32 [1024, 1024], P('ctx', 'section')
- grad_wg2: float32 [1024, 2816], P('ctx', 'section')
- grad_wu2: float32 [1024, 2816], P('ctx', 'section')
- grad_wd2: float32 [2816, 1024], P('ctx', 'section')
The draws below stay inside these ranges and needn't reach their ends.
Inputs may be any that keep to these rules, and one draw needn't show every extreme that they name: `segment_ids`: along each sequence the ids never fall, and each sequence holds each of the values 0, 1 and 2.
All inputs are finite; a program needn't handle non-finite values.
Results may differ from the reference program's by a relative error of at most 0.028.
Values may be sent and summed in bfloat16 or wider, within the bound.
A program may use at most 256 MiB of HBM per device.

```python
import math
import jax
import jax.numpy as jnp
from jax import lax

D = 1024
H = 16
HD = 64
FF = 2816
SEQ = 2048
MICRO = 2
SEQS_MB = 1
N_CTX = 32


def draw_segment_ids(key, part):
    key = jax.random.fold_in(key, 7)
    first_key, last_key, wide_first, wide_last, pick_key = jax.random.split(key, 5)
    shard_len = SEQ // N_CTX
    half_len = SEQ // 2
    near_open = jax.random.randint(first_key, (MICRO, SEQS_MB, 1), 1, shard_len)
    near_close = SEQ - jax.random.randint(last_key, (MICRO, SEQS_MB, 1), 1, shard_len)
    wide_open = jax.random.randint(wide_first, (MICRO, SEQS_MB, 1), 1, half_len)
    wide_close = jax.random.randint(wide_last, (MICRO, SEQS_MB, 1), half_len, SEQ)
    chosen = jax.random.randint(pick_key, (), 0, MICRO * SEQS_MB)
    number = jnp.arange(MICRO * SEQS_MB, dtype=jnp.int32).reshape(MICRO, SEQS_MB, 1)
    spanning = number == chosen
    opening = jnp.where(spanning, near_open, wide_open)
    closing = jnp.where(spanning, near_close, wide_close)
    positions = jnp.arange(SEQ, dtype=jnp.int32)[None, None, :]
    return (positions >= opening).astype(jnp.int32) + (positions >= closing).astype(jnp.int32)


def block_scale(rng, extent, cuts, low, high):
    factor_of, own = 1.0, jax.random.fold_in(rng, 6)
    for position, parts in cuts:
        heights = jnp.exp(jax.random.uniform(jax.random.fold_in(own, position), (parts,), jnp.float32, low / len(cuts), high / len(cuts)))
        factor_of = factor_of * jnp.repeat(heights, extent[position] // parts).reshape([-1 if axis == position else 1 for axis in range(len(extent))])
    return factor_of


def normal_values(rng, shape, scale, limit, cuts=(), kind=jnp.bfloat16):
    entries = jax.random.normal(rng, shape, jnp.float32) * scale
    if len(cuts) > 0:
        entries = block_scale(rng, shape, cuts, -0.22, 0.18) * entries
    return jnp.clip(entries, min=-limit, max=limit).astype(kind)


def setup_inputs(seed: int = 0) -> dict:
    key_of = jax.random.split(jax.random.key(seed), 19)
    return {
        "inputs": normal_values(key_of[0], (MICRO, SEQS_MB, SEQ, D), 1.0, 6.0, ((2, 32),)),
        "cotangent": normal_values(key_of[1], (MICRO, SEQS_MB, SEQ, D), 1.0, 6.0, ((2, 32),)),
        "segment_ids": draw_segment_ids(jax.random.fold_in(key_of[18], 71), 0),
        "gains": jnp.clip(1.0 + 0.15 * jax.random.normal(key_of[3], (4, D), jnp.float32), 0.25, 1.75).astype(jnp.bfloat16),
        "wq1": normal_values(key_of[4], (D, D), D ** -0.5, 0.1875, ((0, 32), (1, 4))),
        "wk1": normal_values(key_of[5], (D, D), D ** -0.5, 0.1875, ((0, 32), (1, 4))),
        "wv1": normal_values(key_of[6], (D, D), D ** -0.5, 0.1875, ((0, 32), (1, 4))),
        "wo1": normal_values(key_of[7], (D, D), (max(D // 256, 1)) ** -0.5, 3.0, ((0, 32), (1, 4))),
        "wg1": normal_values(key_of[8], (D, FF), D ** -0.5, 0.1875, ((0, 32), (1, 4))),
        "wu1": normal_values(key_of[9], (D, FF), D ** -0.5, 0.1875, ((0, 32), (1, 4))),
        "wd1": normal_values(key_of[10], (FF, D), FF ** -0.5, 0.109375, ((0, 32), (1, 4))),
        "wq2": normal_values(key_of[11], (D, D), D ** -0.5, 0.1875, ((0, 32), (1, 4))),
        "wk2": normal_values(key_of[12], (D, D), D ** -0.5, 0.1875, ((0, 32), (1, 4))),
        "wv2": normal_values(key_of[13], (D, D), D ** -0.5, 0.1875, ((0, 32), (1, 4))),
        "wo2": normal_values(key_of[14], (D, D), (max(D // 256, 1)) ** -0.5, 3.0, ((0, 32), (1, 4))),
        "wg2": normal_values(key_of[15], (D, FF), D ** -0.5, 0.1875, ((0, 32), (1, 4))),
        "wu2": normal_values(key_of[16], (D, FF), D ** -0.5, 0.1875, ((0, 32), (1, 4))),
        "wd2": normal_values(key_of[17], (FF, D), FF ** -0.5, 0.109375, ((0, 32), (1, 4))),
    }


norm_eps = 1e-06
masked_score = -1e+30

@jax.custom_vjp
def low(v):
    return lax.optimization_barrier(v.astype(jnp.bfloat16)).astype(jnp.float32)

@jax.custom_vjp
def low_back(v):
    return v

def low_keep(v):
    return (low(v), None)

def low_pass(kept, grad):
    return (grad,)

def back_keep(v):
    return (v, None)

def back_low(kept, grad):
    return (low(grad),)
low.defvjp(low_keep, low_pass)
low_back.defvjp(back_keep, back_low)

def product(left_side, right_side):
    return jnp.dot(left_side, right_side, precision=lax.Precision.HIGHEST)

def normalize(stream_rows, gain_vector):
    inverse = lax.rsqrt(lax.optimization_barrier(jnp.mean(stream_rows * stream_rows, axis=-1, keepdims=True)) + norm_eps)
    return low(stream_rows * inverse * gain_vector)

def sequence_attention(operand):
    query_rows, key_rows, value_rows, segments = operand
    query_heads = query_rows.reshape(SEQ, H, HD)
    key_heads = key_rows.reshape(SEQ, H, HD)
    value_heads = value_rows.reshape(SEQ, H, HD)
    raw_scores = jnp.einsum('qhd,khd->hqk', query_heads, key_heads, precision=lax.Precision.HIGHEST) * (1.0 / math.sqrt(HD))
    scores = low_back(raw_scores)
    positions = jnp.arange(SEQ, dtype=jnp.int32)
    allowed = (segments[:, None] == segments[None, :]) & (positions[None, :] <= positions[:, None])
    weights = low(jax.nn.softmax(jnp.where(allowed[None], scores, masked_score), axis=-1))
    mixed = jnp.einsum('hqk,khd->qhd', weights, value_heads, precision=lax.Precision.HIGHEST)
    return mixed.reshape(SEQ, D)

def attention_block(stream_rows, gain_vector, weight_set, segments, earlier_values, mix_share):
    query_w, key_w, value_w, out_w = weight_set
    activations = normalize(stream_rows, gain_vector)
    queries = low_back(low(product(activations, query_w)))
    key_rows = low_back(low(product(activations, key_w)))
    values = low_back(low((1.0 - mix_share) * product(activations, value_w) + mix_share * earlier_values))
    context = lax.map(jax.checkpoint(sequence_attention), (queries.reshape(-1, SEQ, D), key_rows.reshape(-1, SEQ, D), values.reshape(-1, SEQ, D), segments))
    context = low_back(low(context.reshape(-1, D)))
    branch_out = low_back(product(context, out_w))
    return (low_back(low(stream_rows + branch_out)), values)

def feedforward_block(stream_rows, gain_vector, weight_set):
    gate_w, up_w, down_w = weight_set
    activations = normalize(stream_rows, gain_vector)
    gate_rows = low_back(product(activations, gate_w))
    up_rows = low_back(product(activations, up_w))
    hidden = low(jax.nn.silu(gate_rows) * up_rows)
    return stream_rows + low_back(product(hidden, down_w))

def forward(stream_rows, gain_rows, weight_set, segments):
    first_out, first_values = attention_block(stream_rows, gain_rows[0], weight_set[0:4], segments, jnp.zeros_like(stream_rows), 0.0)
    second_out = low_back(low(feedforward_block(first_out, gain_rows[1], weight_set[4:7])))
    third_out, later_values = attention_block(second_out, gain_rows[2], weight_set[7:11], segments, first_values, 0.5)
    return feedforward_block(third_out, gain_rows[3], weight_set[11:14])

def reference(inputs, cotangent, segment_ids, gains, wq1, wk1, wv1, wo1, wg1, wu1, wd1, wq2, wk2, wv2, wo2, wg2, wu2, wd2):
    weight_set = tuple((matrix.astype(jnp.float32) for matrix in (wq1, wk1, wv1, wo1, wg1, wu1, wd1, wq2, wk2, wv2, wo2, wg2, wu2, wd2)))
    segments = segment_ids.reshape(-1, SEQ)
    stream_rows = inputs.astype(jnp.float32).reshape(-1, D)

    def run_layers(rows_in, gain_rows, weights_in):
        return forward(rows_in, gain_rows, weights_in, segments)
    result, pullback = jax.vjp(run_layers, stream_rows, gains.astype(jnp.float32), weight_set)
    grad_rows, grad_gains, grad_weights = pullback(cotangent.astype(jnp.float32).reshape(-1, D))
    return (result.astype(jnp.bfloat16).reshape(inputs.shape), grad_rows.astype(jnp.bfloat16).reshape(inputs.shape), grad_gains, grad_weights[0], grad_weights[1], grad_weights[2], grad_weights[3], grad_weights[4], grad_weights[5], grad_weights[6], grad_weights[7], grad_weights[8], grad_weights[9], grad_weights[10], grad_weights[11], grad_weights[12], grad_weights[13])
```

```python
from types import SimpleNamespace

import jax
import jax.numpy as jnp
from jax import lax
from jax.experimental import pallas as pl
from jax.experimental.pallas import tpu as pltpu
from jax.sharding import PartitionSpec as P

MESH = pl.DeviceIdType.MESH
BF = jnp.bfloat16
F32 = jnp.float32
I32 = jnp.int32
EPS = 1e-06
MASKED = -1e30


def spec(dtype, *shape):
    return shape, dtype


LAYER_IN = dict(
    wq=spec(BF, 32, 256),
    wk=spec(BF, 32, 256),
    wv=spec(BF, 32, 256),
    wo=spec(BF, 32, 256),
    gus=spec(BF, 2, 32, 768),
    wd=spec(BF, 88, 256),
)
COMMON_IN = dict(
    xin=spec(BF, 2, 2, 32, 1024), cot=spec(BF, 2, 2, 32, 1024), gst=spec(F32, 8, 128), startq=spec(I32, 8, 512)
)
LAYER_OUT = dict(
    oq=spec(F32, 32, 256),
    ok=spec(F32, 32, 256),
    ov=spec(F32, 32, 256),
    oo=spec(F32, 32, 256),
    ogu=spec(F32, 2, 32, 768),
    od=spec(F32, 96, 256),
)
COMMON_OUT = dict(out=spec(BF, 2, 2, 32, 256), ing=spec(BF, 2, 2, 32, 256), ogg=spec(F32, 8, 128))
COMMON = dict(
    hin=spec(BF, 8, 32, 1024),
    gx=spec(F32, 3, 8, 128),
    g1=spec(F32, 8, 128),
    gyr=spec(F32, 8, 8, 128),
    gz=spec(F32, 4, 2, 8, 128),
    gains=spec(F32, 8, 1024),
    gg=spec(F32, 8, 1024),
    ggx=spec(F32, 3, 8, 1024),
    ggz=spec(F32, 4, 8, 256),
    ggzr=spec(F32, 3, 8, 256),
    ggy=spec(F32, 2, 8, 128),
    ggyr=spec(F32, 8, 8, 128),
    scores=spec(F32, 16, 128, 512),
    dkvf=spec(F32, 2, 256, 256),
    outst=spec(BF, 4, 32, 256),
    ingst=spec(BF, 4, 32, 256),
    outrv=spec(BF, 2, 2, 32, 256),
    ingrv=spec(BF, 2, 2, 32, 256),
    dmh=spec(BF, 256, 128),
)
LAYER = dict(
    wst=spec(BF, 2, 32, 384),
    wds=spec(BF, 96, 256),
    wqkv=spec(BF, 4, 8, 32, 384),
    wout=spec(BF, 4, 4, 32, 256),
    wgu=spec(BF, 4, 4, 2, 32, 768),
    wdn=spec(BF, 4, 4, 96, 256),
    kv=spec(BF, 4, 2, 256, 256),
    q2=spec(BF, 512, 128),
    prob=spec(BF, 16, 128, 512),
    ot=spec(F32, 128, 256),
    gu=spec(F32, 256, 768),
    hid=spec(BF, 256, 384),
    dkv=spec(BF, 4, 2, 256, 256),
    dkvr=spec(BF, 3, 2, 256, 256),
    dkvs=spec(BF, 256, 256),
    dkvy=spec(BF, 256, 256),
    gwqkv=spec(BF, 4, 8, 32, 384),
    gwout=spec(BF, 4, 4, 32, 256),
    gwgu=spec(BF, 4, 4, 2, 32, 768),
    gwdn=spec(BF, 4, 4, 96, 256),
    rzqkv=spec(BF, 3, 8, 32, 384),
    rzout=spec(BF, 3, 4, 32, 256),
    rygu=spec(BF, 3, 4, 2, 32, 768),
    rzdn=spec(BF, 3, 4, 96, 256),
    sqkv=spec(BF, 8, 32, 384),
    sout=spec(BF, 4, 32, 256),
    sgu=spec(BF, 4, 2, 32, 768),
    sdn=spec(BF, 4, 96, 256),
    fqkv=spec(BF, 8, 32, 384),
    fout=spec(BF, 4, 32, 256),
    fgu=spec(BF, 8, 32, 768),
    fdn=spec(BF, 4, 96, 256),
)
SUB = dict(
    a=spec(BF, 8, 32, 1024),
    h=spec(BF, 32, 1024),
    gr=spec(BF, 32, 1024),
    gb=spec(BF, 8, 32, 1024),
)
EXCHANGE = dict(
    pb=spec(BF, 2, 4, 32, 1024),
    sib=spec(BF, 4, 32, 1024),
    xs=spec(BF, 3, 32, 1024),
    xr=spec(BF, 3, 32, 1024),
)
N_SEM = 480
N_LAYERS, N_SUB, N_EXCHANGE = 2, 4, 8


def groups():
    arguments = [(0, 0, COMMON_IN)] + [(1, l, LAYER_IN) for l in range(N_LAYERS)]
    results = [(0, 0, COMMON_OUT)] + [(1, l, LAYER_OUT) for l in range(N_LAYERS)]
    scratch = [(0, 0, COMMON)] + [(1, l, LAYER) for l in range(N_LAYERS)]
    scratch += [(2, i, SUB) for i in range(N_SUB)] + [(3, n, EXCHANGE) for n in range(N_EXCHANGE)]
    return arguments, results, scratch


def named(refs):
    spaces = [[SimpleNamespace() for _ in range(n)] for n in (1, N_LAYERS, N_SUB, N_EXCHANGE)]
    left = list(refs)
    for group in groups():
        for kind, index, specs in group:
            for name in specs:
                setattr(spaces[kind][index], name, left.pop(0))
    return spaces[0][0], spaces[1], spaces[2], spaces[3]


def specs_of(group):
    return [entry for _, _, specs in group for entry in specs.values()]


def nn(a, b):
    return lax.dot_general(a, b, (((1,), (0,)), ((), ())), preferred_element_type=F32)


def nt(a, b):
    return lax.dot_general(a, b, (((1,), (1,)), ((), ())), preferred_element_type=F32)


def tn(a, b):
    return lax.dot_general(a, b, (((0,), (0,)), ((), ())), preferred_element_type=F32)


def normalize(h):
    inverse = lax.rsqrt(jnp.mean(h * h, axis=-1, keepdims=True) + EPS)
    return h * inverse, inverse


def kernel(*refs):
    R, L, S, X = named(refs[:-1])
    sems = refs[-1]
    used = [0]
    pending = []

    def new():
        used[0] += 1
        return sems.at[used[0] - 1]

    x = lax.axis_index("section")
    c = lax.axis_index("ctx")
    z, y, k = lax.div(c, 8), lax.rem(lax.div(c, 2), 4), lax.rem(c, 2)
    t = 2 * x + k
    s = lax.div(y, 2)
    yy = lax.rem(y, 2)
    other = 1 - k

    def plus(v, j):
        return lax.rem(v + j, 4)

    def dev(xd, zd, yd, kd):
        return {"section": xd, "ctx": zd * 8 + yd * 2 + kd}

    def flip(j):
        return k if j % 2 == 0 else other

    sibling = dev(x, z, y, other)

    def put(src, dst, to, rsem):
        copy = pltpu.make_async_remote_copy(
            src_ref=src, dst_ref=dst, send_sem=new(), recv_sem=rsem, device_id=to, device_id_type=MESH
        )
        copy.start()
        pending.append((None, copy))

    def put_or_keep(mine, src, dst, to, rsem):
        copy = pltpu.make_async_remote_copy(
            src_ref=src, dst_ref=dst, send_sem=new(), recv_sem=rsem, device_id=to, device_id_type=MESH
        )

        @pl.when(mine)
        def _():
            pltpu.make_async_copy(src, dst, rsem).start()

        @pl.when(jnp.logical_not(mine))
        def _():
            copy.start()

        pending.append((mine, copy))

    def arrived(ref, sem):
        pltpu.make_async_copy(ref, ref, sem).wait()

    barrier = pltpu.get_barrier_semaphore()

    def greet(d):
        pl.semaphore_signal(barrier, inc=1, device_id=d, device_id_type=MESH)

    count = 0
    for j in range(4):
        for i in range(2):
            if (j, i) != (0, 0):
                greet(dev(plus(x, j), z, y, flip(i)))
                count += 1
            if j:
                greet(dev(x, z, plus(y, j), flip(i)))
                greet(dev(x, plus(z, j), y, flip(i)))
                count += 2
            greet(dev(plus(x, j), 3 - z, 3 - y, flip(i)))
            count += 1
    crossing = jnp.where(x == z, 0, 1)

    @pl.when(x != z)
    def _():
        for j in range(4):
            for i in range(2):
                greet(dev(z, x, plus(y, j), flip(i)))

    pl.semaphore_wait(barrier, count + 8 * crossing)

    W = [SimpleNamespace(), SimpleNamespace()]

    def weights_att_first(l):
        wst = L[l].wst
        for i in range(2):
            for n, w in enumerate((L[l].wq, L[l].wk, L[l].wv)):
                wst[i, :, 128 * n : 128 * n + 128] = w[:, 128 * i : 128 * i + 128]
        w = L[l].wqkv
        sem = W[l].q1 = new()
        pltpu.make_async_copy(wst.at[k], w.at[z, 2 * y + k], sem).start()
        for j in range(1, 8):
            put(wst.at[flip(j)], w.at[z, 2 * y + k], dev(x, z, plus(y, j // 2), flip(j)), sem)
        wo, w = L[l].wo, L[l].wout
        sem = W[l].o1 = new()
        crossed(wo, w, sem)

    def crossed(src, w, sem):
        slot = w.at[x, 2 * yy + k]
        mine = (x == z) & (s == k)
        put_or_keep(mine, src, slot, dev(z, x, y, s), sem)
        for j in range(1, 4):
            put(src, slot, dev(z, x, plus(y, j), s), sem)

    def weights_ff_first(l):
        src, w = L[l].gus, L[l].wgu
        sem = W[l].g1 = new()
        pltpu.make_async_copy(src.at[k], w.at[z, y, k], sem).start()
        for j in range(1, 8):
            put(src.at[flip(j)], w.at[z, y, k], dev(x, plus(z, j // 2), y, flip(j)), sem)
        wds = L[l].wds
        wds[0:88, :] = L[l].wd[...]
        wds[88:96, :] = jnp.zeros((8, 256), BF)
        sem = W[l].d1 = new()
        crossed(wds, L[l].wdn, sem)

    def along_z(w):
        sem = new()
        for j in (1, 3, 2):
            put(w.at[z], w.at[z], dev(x, plus(z, j), y, k), sem)
        return sem

    def weights_att_second(l):
        w, wo = L[l].wqkv, L[l].wout
        arrived(w.at[z], W[l].q1)
        W[l].q2 = along_z(w)
        arrived(wo.at[z], W[l].o1)
        W[l].o2 = along_z(wo)

    def weights_ff_second(l):
        w, wd = L[l].wgu, L[l].wdn
        arrived(w.at[z], W[l].g1)
        sem = W[l].g2 = new()
        for j in (1, 3, 2):
            put(w.at[:, y], w.at[:, y], dev(x, z, plus(y, j), k), sem)
        arrived(wd.at[z], W[l].d1)
        W[l].d2 = along_z(wd)

    def rs_start(n, part):
        pb, sib = X[n].pb, X[n].sib
        for i in range(8):
            pb[i % 2, i // 2] = part[32 * i : 32 * i + 32].astype(BF)
        sem = [new() for _ in range(4)]
        for j in (1, 3, 2, 0):
            xd = plus(x, j)
            put(pb.at[other, xd], sib.at[xd], sibling, sem[j])
        return sem

    def rs_mid(n, sem):
        pb, sib, xs, xr = X[n].pb, X[n].sib, X[n].xs, X[n].xr
        out = []
        for j in (1, 3, 2):
            xd = plus(x, j)
            arrived(sib.at[xd], sem[j])
            xs[j - 1] = (pb[k, xd].astype(F32) + sib[xd].astype(F32)).astype(BF)
            out.append(new())
            put(xs.at[j - 1], xr.at[j - 1], dev(xd, z, y, k), out[-1])
        return sem[0], out

    def rs_end(n, sems_):
        pb, sib, xr = X[n].pb, X[n].sib, X[n].xr
        own, out = sems_
        arrived(sib.at[x], own)
        total = pb[k, x].astype(F32) + sib[x].astype(F32)
        for j, sem in zip((1, 3, 2), out):
            arrived(xr.at[j - 1], sem)
            total += xr[j - 1].astype(F32)
        return total

    def gather(buf, block):
        buf[t] = block
        rx = [new() for _ in range(4)]
        rk = [new() for _ in range(4)]
        for j in (1, 3, 2):
            put(buf.at[t], buf.at[t], dev(plus(x, j), z, y, k), rx[j])
        put(buf.at[t], buf.at[t], sibling, rk[0])
        for j in (1, 3, 2):
            slot = buf.at[2 * plus(x, 4 - j) + k]
            arrived(slot, rx[j])
            put(slot, slot, sibling, rk[j])
        for j in range(4):
            arrived(buf.at[0], rk[j])

    def to_owners(rows, stage, landing):
        for i in range(4):
            stage[i] = rows[:, 256 * i : 256 * i + 256]
        near = x < 2
        zd, yd = jnp.where(near, z, 3 - z), jnp.where(near, y, 3 - y)
        kd = lax.rem(x, 2)
        sem = new()
        put_or_keep(near & (kd == k), stage.at[x], landing.at[s, k], dev(x, zd, yd, kd), sem)
        for j in range(1, 4):
            xd = plus(x, j)
            put(stage.at[xd], landing.at[s, k], dev(xd, zd, yd, kd), sem)
        return sem

    def spread_tokens(src, dst):
        sem = new()
        near, far = pl.ds(2 * k, 2), pl.ds(4 + 2 * k, 2)
        dst[near] = src[s]
        put(src.at[s], dst.at[near], sibling, sem)
        put(src.at[1 - s], dst.at[far], dev(x, 3 - z, 3 - y, k), sem)
        put(src.at[1 - s], dst.at[far], dev(x, 3 - z, 3 - y, other), sem)
        return sem

    lane = lax.rem(lax.broadcasted_iota(I32, (1, 512), 1), 256)
    own_block = 4 * z + y
    query_pos = jnp.where(lane < 128, 128 * own_block + lane, 128 * (15 - own_block) + lane - 128)
    query_start = R.startq[0:1, :]
    head_lane = lax.broadcasted_iota(I32, (256, 128), 1) < 64

    def two_heads(v):
        zero = jnp.zeros_like(v)
        return jnp.concatenate([jnp.where(head_lane, v, zero), jnp.where(head_lane, zero, v)], axis=0)

    def own_heads(vt):
        return jnp.concatenate([vt[0:64, 0:256], vt[64:128, 256:512]], axis=0)

    def gain_row(i):
        return R.gains[i : i + 1, :]

    def full(ref):
        return ref[...].reshape(256, 1024)

    def keys_of(l, zz):
        return L[l].kv[zz, :, :, 0:128].reshape(512, 128)

    def values_of(l, zz):
        return L[l].kv[zz, :, :, 128:256].reshape(512, 128)

    def attention_forward(l, hook):
        arrived(L[l].wqkv.at[0:3], W[l].q2)
        qkv = nn(full(S[2 * l].a), L[l].wqkv[...].reshape(1024, 384))
        q = (qkv[:, 0:128].astype(BF) * 0.125).astype(BF)
        keys = qkv[:, 128:256].astype(BF)
        u = qkv[:, 256:384]
        if l == 0:
            values = u.astype(BF)
        else:
            values = (0.5 * u + 0.5 * L[0].kv[z, yy, :, 128:256].astype(F32)).astype(BF)
        kv = L[l].kv
        kv[z, yy, :, 0:128] = keys
        kv[z, yy, :, 128:256] = values
        q2 = two_heads(q)
        L[l].q2[...] = q2
        sem = new()
        put(kv.at[z, yy], kv.at[z, yy], dev(x, z, y + 1 - 2 * yy, k), sem)
        arrived(kv.at[z, yy], sem)
        zsem = [new() for _ in range(4)]
        for j in (1, 3, 2):
            put(kv.at[z], kv.at[z], dev(x, plus(z, j), y, k), zsem[j])
        hook()
        scores = R.scores
        top = jnp.full((1, 512), MASKED, F32)
        for j in (0, 3, 1, 2):
            zz = plus(z, j)
            if j:
                arrived(kv.at[zz], zsem[4 - j])
            scores[4 * j : 4 * j + 4] = nt(keys_of(l, zz), L[l].q2[...]).reshape(4, 128, 512)

            def mask(i, top, j=j, zz=zz):
                block = 4 * zz + 2 * s + lax.div(i, 2)
                base = 128 * (block + lax.rem(i, 2) * (15 - 2 * block))
                row = lax.broadcasted_iota(I32, (128, 512), 0)
                seen = (row >= query_start - base) & (row <= query_pos - base)
                v = jnp.where(seen, scores[4 * j + i], MASKED)
                scores[4 * j + i] = v
                return jnp.maximum(top, jnp.max(v, axis=0, keepdims=True))

            top = lax.fori_loop(0, 4, mask, top)

        def expo(i, total):
            v = jnp.exp(scores[i] - top)
            scores[i] = v
            return total + jnp.sum(v, axis=0, keepdims=True)

        total = lax.fori_loop(0, 16, expo, jnp.zeros((1, 512), F32))
        share = 1.0 / total
        prob = L[l].prob

        def norm(i, carry):
            prob[i] = (scores[i] * share).astype(BF)
            return carry

        lax.fori_loop(0, 16, norm, 0)
        ot = jnp.zeros((128, 512), F32)
        for j in range(4):
            ot += tn(values_of(l, plus(z, j)), prob[4 * j : 4 * j + 4].reshape(512, 512))
        ot = own_heads(ot)
        L[l].ot[...] = ot
        o = jnp.transpose(ot).astype(BF)
        arrived(L[l].wout.at[0:3], W[l].o2)
        return jnp.concatenate([nn(o, L[l].wout[i].reshape(128, 256)) for i in range(4)], axis=1)

    def feedforward_forward(l, hook):
        arrived(L[l].wgu.at[0:3], W[l].g2)
        gu = nn(full(S[2 * l + 1].a), L[l].wgu[...].reshape(1024, 768))
        L[l].gu[...] = gu
        gate, up = gu[:, 0:384], gu[:, 384:768]
        hidden = (gate * jax.nn.sigmoid(gate) * up).astype(BF)
        L[l].hid[...] = hidden
        hook()
        arrived(L[l].wdn.at[0:3], W[l].d2)
        return jnp.concatenate([nn(hidden, L[l].wdn[i].reshape(384, 256)) for i in range(4)], axis=1)

    def next_rows(i, part):
        total = rs_end(i, rs_mid(i, rs_start(i, part)))
        rows = (S[i].h[...].astype(F32) + total).astype(BF)
        S[i + 1].h[...] = rows
        normed, _ = normalize(rows.astype(F32))
        gather(S[i + 1].a, (normed * gain_row(i + 1)).astype(BF))

    def norm_backward(i, da):
        normed, inverse = normalize(S[i].h[...].astype(F32))
        R.gg[i : i + 1, :] = jnp.sum(da * normed, axis=0, keepdims=True)
        scaled = da * gain_row(i)
        mixed = scaled - normed * jnp.mean(scaled * normed, axis=-1, keepdims=True)
        return (S[i].gr[...].astype(F32) + inverse * mixed).astype(BF)

    G = [SimpleNamespace(), SimpleNamespace()]

    def send_z(g, landing):
        sem = new()
        for j in (1, 3, 2):
            zd = plus(z, j)
            put(g.at[zd], landing.at[j - 1], dev(x, zd, y, k), sem)
        return sem

    def attention_backward(l, hook1, hook2):
        i0 = 2 * l
        gb = full(S[i0].gb)
        wo = L[l].wout
        dot_ = nt(wo[0].reshape(128, 256), gb[:, 0:256])
        for i in range(1, 4):
            dot_ += nt(wo[i].reshape(128, 256), gb[:, 256 * i : 256 * i + 256])
        dot_ = dot_.astype(BF).astype(F32)
        do2 = two_heads(jnp.transpose(dot_).astype(BF))
        prod = dot_ * L[l].ot[...]
        delta = jnp.concatenate(
            [jnp.sum(prod[0:64], axis=0, keepdims=True), jnp.sum(prod[64:128], axis=0, keepdims=True)], axis=1
        )
        dkv, prob = L[l].dkv, L[l].prob
        dq = jnp.zeros((128, 512), F32)
        zsem = G[l].kv = new()
        for j in (1, 3, 2, 0):
            zz = plus(z, j)
            p = prob[4 * j : 4 * j + 4].reshape(512, 512)
            dp = nt(values_of(l, zz), do2)
            ds = (p.astype(F32) * (dp - delta)).astype(BF)
            dkv[zz, :, :, 0:128] = nn(ds, L[l].q2[...]).astype(BF).reshape(2, 256, 128)
            dkv[zz, :, :, 128:256] = nn(p, do2).astype(BF).reshape(2, 256, 128)
            if j:
                put(dkv.at[zz], L[l].dkvr.at[j - 1], dev(x, zz, y, k), zsem)
            dq += tn(keys_of(l, zz), ds)
        dq = jnp.transpose(own_heads(dq) * 0.125).astype(BF)
        hook1()
        got = L[l].dkvr
        arrived(got, zsem)
        tot = dkv[z].astype(F32) + got[0].astype(F32) + got[1].astype(F32) + got[2].astype(F32)
        R.dkvf[...] = tot
        mate = 1 - yy
        L[l].dkvs[...] = R.dkvf[mate].astype(BF)
        sem = new()
        put(L[l].dkvs, L[l].dkvy, dev(x, z, y + 1 - 2 * yy, k), sem)
        arrived(L[l].dkvy, sem)
        tot = R.dkvf[yy] + L[l].dkvy[...].astype(F32)
        dk = tot[:, 0:128].astype(BF)
        dvals = tot[:, 128:256]
        if l == 1:
            half = 0.5 * dvals.astype(BF).astype(F32)
            du = half.astype(BF)
            R.dmh[...] = du
        else:
            du = (dvals + R.dmh[...].astype(F32)).astype(BF)
        dqkv = jnp.concatenate([dq, dk, du], axis=1)
        rs = rs_start(4 + i0, nt(dqkv, L[l].wqkv[...].reshape(1024, 384)))
        rs = rs_mid(4 + i0, rs)
        at = jnp.transpose(full(S[i0].a))
        gw = L[l].gwqkv
        gw[...] = nn(at, dqkv).astype(BF).reshape(4, 8, 32, 384)
        G[l].q = send_z(gw, L[l].rzqkv)
        otb = L[l].ot[...].astype(BF)
        gw = L[l].gwout
        for i in range(4):
            gw[i] = nn(otb, gb[:, 256 * i : 256 * i + 256]).astype(BF).reshape(4, 32, 256)
        G[l].o = send_z(gw, L[l].rzout)
        hook2()
        return norm_backward(i0, rs_end(4 + i0, rs))

    def feedforward_backward(l, hook1, hook2):
        i0 = 2 * l + 1
        gb = full(S[i0].gb)
        wd = L[l].wdn
        dhid = nt(gb[:, 0:256], wd[0].reshape(384, 256))
        for i in range(1, 4):
            dhid += nt(gb[:, 256 * i : 256 * i + 256], wd[i].reshape(384, 256))
        gu = L[l].gu[...]
        gate, up = gu[:, 0:384], gu[:, 384:768]
        sig = jax.nn.sigmoid(gate)
        dgate = dhid * up * sig * (1.0 + gate * (1.0 - sig))
        dup = dhid * (gate * sig)
        dgu = jnp.concatenate([dgate.astype(BF), dup.astype(BF)], axis=1)
        rs = rs_start(4 + i0, nt(dgu, L[l].wgu[...].reshape(1024, 768)))
        hook1()
        rs = rs_mid(4 + i0, rs)
        at = jnp.transpose(full(S[i0].a))
        gw = L[l].gwgu
        gw[...] = nn(at, dgu).astype(BF).reshape(4, 4, 2, 32, 768)
        sem = G[l].g = new()
        for j in (1, 3, 2):
            yd = plus(y, j)
            put(gw.at[:, yd], L[l].rygu.at[j - 1], dev(x, z, yd, k), sem)
        ht = jnp.transpose(L[l].hid[...])
        gw = L[l].gwdn
        for i in range(4):
            gw[i] = nn(ht, gb[:, 256 * i : 256 * i + 256]).astype(BF).reshape(4, 96, 256)
        G[l].d = send_z(gw, L[l].rzdn)
        hook2()
        return norm_backward(i0, rs_end(4 + i0, rs))

    def summed(own, got):
        return own.astype(F32) + got[0].astype(F32) + got[1].astype(F32) + got[2].astype(F32)

    def owners_crossed(src, landing):
        sem = new()
        first = 2 * yy + k
        for j in range(4):
            m = plus(first, j)
            to = dev(z, x, 2 * k + lax.div(m, 2), lax.rem(m, 2))
            if j == 0:
                put_or_keep((x == z) & (s == k), src.at[m], landing.at[y], to, sem)
            else:
                put(src.at[m], landing.at[y], to, sem)
        return sem

    def grads_att_second(l):
        gw, got, st, land = L[l].gwqkv, L[l].rzqkv, L[l].sqkv, L[l].fqkv
        arrived(got, G[l].q)
        st[...] = summed(gw[z], got).astype(BF)
        sem = G[l].q2 = new()
        land[0] = st[2 * y + k]
        for j in range(1, 8):
            yd, kd = plus(y, j // 2), flip(j)
            put(st.at[2 * yd + kd], land.at[j], dev(x, z, yd, kd), sem)
        gw, got, st = L[l].gwout, L[l].rzout, L[l].sout
        arrived(got, G[l].o)
        st[...] = summed(gw[z], got).astype(BF)
        G[l].o2 = owners_crossed(st, L[l].fout)

    def halves(land):
        own = land[0].astype(F32) + land[2].astype(F32) + land[4].astype(F32) + land[6].astype(F32)
        far = land[1].astype(F32) + land[3].astype(F32) + land[5].astype(F32) + land[7].astype(F32)
        return own, far

    def four(land):
        return land[0].astype(F32) + land[1].astype(F32) + land[2].astype(F32) + land[3].astype(F32)

    def grads_att_end(l):
        land = L[l].fqkv
        arrived(land.at[1:8], G[l].q2)
        own, far = halves(land)
        first = k == 0
        low, high = jnp.where(first, own, far), jnp.where(first, far, own)
        for n, result in enumerate((L[l].oq, L[l].ok, L[l].ov)):
            result[:, 0:128] = low[:, 128 * n : 128 * n + 128]
            result[:, 128:256] = high[:, 128 * n : 128 * n + 128]
        land = L[l].fout
        arrived(land, G[l].o2)
        L[l].oo[...] = four(land)

    def grads_ff_second(l):
        gw, got, st, land = L[l].gwgu, L[l].rygu, L[l].sgu, L[l].fgu
        arrived(got, G[l].g)
        for i in range(4):
            st[i] = (
                gw[i, y].astype(F32) + got[0, i].astype(F32) + got[1, i].astype(F32) + got[2, i].astype(F32)
            ).astype(BF)
        sem = G[l].g2 = new()
        land[0] = st[z, k]
        for j in range(1, 8):
            zd, kd = plus(z, j // 2), flip(j)
            put(st.at[zd, kd], land.at[j], dev(x, zd, y, kd), sem)
        gw, got, st = L[l].gwdn, L[l].rzdn, L[l].sdn
        arrived(got, G[l].d)
        st[...] = summed(gw[z], got).astype(BF)
        G[l].d2 = owners_crossed(st, L[l].fdn)

    def grads_ff_end(l):
        land = L[l].fgu
        arrived(land.at[1:8], G[l].g2)
        own, far = halves(land)
        L[l].ogu[k] = own
        L[l].ogu[other] = far
        land = L[l].fdn
        arrived(land, G[l].d2)
        L[l].od[...] = four(land)

    def nothing():
        pass

    weights_att_first(0)
    in_sem = spread_tokens(R.xin, R.hin)
    gx_sem = new()
    for j in (1, 3, 2):
        put(R.gst, R.gx.at[j - 1], dev(plus(x, j), z, y, k), gx_sem)
    weights_ff_first(0)
    arrived(R.gx, gx_sem)
    R.g1[...] = R.gst[...] + R.gx[0] + R.gx[1] + R.gx[2]
    gy_sem = new()
    R.gyr[2 * y + k] = R.g1[...]
    for j in range(1, 8):
        put(R.g1, R.gyr.at[2 * y + k], dev(x, z, plus(y, j // 2), flip(j)), gy_sem)
    weights_att_second(0)
    arrived(R.gyr.at[0:7], gy_sem)
    for i in range(2):
        R.gz[z, i] = R.gyr[4 * i] + R.gyr[4 * i + 1] + R.gyr[4 * i + 2] + R.gyr[4 * i + 3]
    gz_sem = new()
    for j in (1, 3, 2):
        put(R.gz.at[z], R.gz.at[z], dev(x, plus(z, j), y, k), gz_sem)
    R.gg[...] = jnp.zeros((8, 1024), F32)
    arrived(R.hin.at[0:6], in_sem)
    arrived(R.gz.at[0:3], gz_sem)
    R.gains[...] = jnp.concatenate([R.gz[i // 2, i % 2] for i in range(8)], axis=1)
    normed, _ = normalize(full(R.hin).astype(F32))
    S[0].a[...] = (normed * gain_row(0)).astype(BF).reshape(8, 32, 1024)
    S[0].h[...] = R.hin[t]
    cot_sem = []

    def after_keys_0():
        weights_ff_second(0)
        weights_att_first(1)
        weights_ff_first(1)

    def after_keys_1():
        weights_ff_second(1)
        cot_sem.append(spread_tokens(R.cot, S[3].gb))

    next_rows(0, attention_forward(0, after_keys_0))
    next_rows(1, feedforward_forward(0, lambda: weights_att_second(1)))
    next_rows(2, attention_forward(1, after_keys_1))
    last = rs_mid(3, rs_start(3, feedforward_forward(1, nothing)))
    arrived(S[3].gb.at[0:6], cot_sem[0])
    S[3].gr[...] = S[3].gb[t]
    out_sem = []

    def finish_outputs():
        rows = (S[3].h[...].astype(F32) + rs_end(3, last)).astype(BF)
        out_sem.append(to_owners(rows, R.outst, R.outrv))

    def hand_back(i, rows):
        S[i].gr[...] = rows
        gather(S[i].gb, rows)

    hand_back(2, feedforward_backward(1, finish_outputs, nothing))
    hand_back(1, attention_backward(1, lambda: grads_ff_second(1), nothing))
    hand_back(0, feedforward_backward(0, lambda: grads_att_second(1), lambda: grads_ff_end(1)))
    rows = attention_backward(0, lambda: grads_ff_second(0), lambda: grads_att_end(1))
    in_grad_sem = to_owners(rows, R.ingst, R.ingrv)
    gg_sem = new()
    for j in (1, 3, 2):
        put(R.gg, R.ggx.at[j - 1], dev(plus(x, j), z, y, k), gg_sem)
    grads_att_second(0)
    arrived(R.ggx, gg_sem)
    gg = R.gg[...] + R.ggx[0] + R.ggx[1] + R.ggx[2]
    for i in range(4):
        R.ggz[i] = gg[:, 256 * i : 256 * i + 256]
    gg_sem = new()
    for j in (1, 3, 2):
        zd = plus(z, j)
        put(R.ggz.at[zd], R.ggzr.at[j - 1], dev(x, zd, y, k), gg_sem)
    grads_ff_end(0)
    arrived(R.outrv, out_sem[0])
    R.out[...] = R.outrv[...]
    arrived(R.ggzr, gg_sem)
    gg = R.ggz[z] + R.ggzr[0] + R.ggzr[1] + R.ggzr[2]
    R.ggy[0] = gg[:, 0:128]
    R.ggy[1] = gg[:, 128:256]
    gg_sem = new()
    R.ggyr[0] = R.ggy[s]
    for j in range(1, 8):
        yd = plus(y, j // 2)
        put(R.ggy.at[lax.div(yd, 2)], R.ggyr.at[j], dev(x, z, yd, flip(j)), gg_sem)
    arrived(R.ingrv, in_grad_sem)
    R.ing[...] = R.ingrv[...]
    arrived(R.ggyr.at[1:8], gg_sem)
    gg = R.ggyr[0]
    for j in range(1, 8):
        gg = gg + R.ggyr[j]
    R.ogg[...] = gg
    grads_att_end(0)
    for mine, copy in pending:
        if mine is None:
            copy.wait_send()
        else:

            @pl.when(jnp.logical_not(mine))
            def _(copy=copy):
                copy.wait_send()

    assert used[0] <= N_SEM, used


def call(*args):
    whole = pl.BlockSpec(memory_space=pltpu.VMEM)
    arguments, results, scratch = (specs_of(group) for group in groups())
    return pl.pallas_call(
        kernel,
        out_shape=[jax.ShapeDtypeStruct(shape, dtype) for shape, dtype in results],
        in_specs=[whole] * len(arguments),
        out_specs=[whole] * len(results),
        scratch_shapes=[pltpu.VMEM(shape, dtype) for shape, dtype in scratch]
        + [pltpu.SemaphoreType.DMA((N_SEM,))],
        compiler_params=pltpu.CompilerParams(
            collective_id=0, has_side_effects=True, vmem_limit_bytes=62 * 1024 * 1024
        ),
    )(*args)


def packed(w):
    rows = w.shape[0]
    groups = w.reshape(rows, 2, 4, 88)
    return jnp.pad(groups, ((0, 0), (0, 0), (0, 0), (0, 8))).reshape(rows, 2, 384).swapaxes(0, 1)


def unpacked(g):
    rows = g.shape[1]
    return g.swapaxes(0, 1).reshape(rows, 2, 4, 96)[..., :88].reshape(rows, 704)


def body(inputs, cotangent, segment_ids, gains, *weights):
    x = lax.axis_index("section")
    c = lax.axis_index("ctx")
    z, y = c // 8, (c // 2) % 4
    segments = lax.dynamic_index_in_dim(segment_ids.reshape(2, 2048), y // 2, 0, keepdims=False)
    first = jnp.sum(segments == 0).astype(I32)
    second = jnp.sum(segments <= 1).astype(I32)
    row = jnp.arange(512, dtype=I32) % 256
    block = 4 * z + y
    pos = jnp.where(row < 128, 128 * block + row, 128 * (15 - block) + row - 128)
    start = jnp.where(pos < first, 0, jnp.where(pos < second, first, second)).astype(I32)
    startq = jnp.broadcast_to(start[None], (8, 512))
    at_row = lax.broadcasted_iota(I32, (8, 128), 0) == x
    at_lane = lax.broadcasted_iota(I32, (8, 128), 1) // 32 == c % 4
    piece = jnp.tile(gains.astype(F32), (1, 4))
    gst = jnp.where(at_row & at_lane, piece, 0.0)
    args = [inputs.reshape(2, 2, 32, 1024), cotangent.reshape(2, 2, 32, 1024), gst, startq]
    for l in range(2):
        wq, wk, wv, wo, wg, wu, wd = weights[7 * l : 7 * l + 7]
        args += [wq, wk, wv, wo, jnp.concatenate([packed(wg), packed(wu)], axis=2), wd]
    outs = call(*args)
    out, ing, ogg = outs[:3]
    gain = lax.dynamic_slice(ogg, (x, (c % 4) * 32), (1, 32))
    results = [out.reshape(2, 1, 64, 256), ing.reshape(2, 1, 64, 256), gain]
    for l in range(2):
        oq, ok, ov, oo, ogu, od = outs[3 + 6 * l : 9 + 6 * l]
        results += [oq, ok, ov, oo, unpacked(ogu[:, :, :384]), unpacked(ogu[:, :, 384:])]
        results += [od[:88]]
    return tuple(results)


def solution(mesh):
    tokens = P(None, None, "ctx", None)
    weight = P("ctx", "section")
    return jax.shard_map(
        body,
        mesh=mesh,
        in_specs=(tokens, tokens, P(), P("section", "ctx")) + (weight,) * 14,
        out_specs=(P(None, None, "ctx", "section"),) * 2 + (P("section", "ctx"),) + (weight,) * 14,
        check_vma=False,
    )
```

```python
from types import SimpleNamespace

import jax
import jax.numpy as jnp
from jax import lax
from jax.experimental import pallas as pl
from jax.experimental.pallas import tpu as pltpu
from jax.sharding import PartitionSpec as P

MESH = pl.DeviceIdType.MESH
BF = jnp.bfloat16
F32 = jnp.float32
I32 = jnp.int32
EPS = 1e-06
MASKED = -1e30


def spec(dtype, *shape):
    return shape, dtype


LAYER_IN = dict(
    wq=spec(BF, 32, 256),
    wk=spec(BF, 32, 256),
    wv=spec(BF, 32, 256),
    wo=spec(BF, 32, 256),
    wg=spec(BF, 32, 704),
    wu=spec(BF, 32, 704),
    wd=spec(BF, 88, 256),
)
COMMON_IN = dict(
    xin=spec(BF, 2, 2, 32, 1024), cot=spec(BF, 2, 2, 32, 1024), seg=spec(I32, 2, 1, 2048), gains_in=spec(BF, 1, 32)
)
LAYER_OUT = dict(
    oq=spec(F32, 32, 256),
    ok=spec(F32, 32, 256),
    ov=spec(F32, 32, 256),
    oo=spec(F32, 32, 256),
    og=spec(F32, 32, 704),
    ou=spec(F32, 32, 704),
    od=spec(F32, 88, 256),
)
COMMON_OUT = dict(out=spec(BF, 2, 1, 64, 256), ing=spec(BF, 2, 1, 64, 256), ogg=spec(F32, 1, 32))
COMMON = dict(
    hin=spec(BF, 8, 32, 1024),
    pick=spec(BF, 704, 768),
    gst=spec(F32, 8, 128),
    gx=spec(F32, 3, 8, 128),
    g1=spec(F32, 8, 128),
    gyr=spec(F32, 8, 8, 128),
    gz=spec(F32, 4, 2, 8, 128),
    gains=spec(F32, 8, 1024),
    gg=spec(F32, 8, 1024),
    ggx=spec(F32, 3, 8, 1024),
    ggz=spec(F32, 4, 8, 256),
    ggzr=spec(F32, 3, 8, 256),
    ggy=spec(F32, 2, 8, 128),
    ggyr=spec(F32, 8, 8, 128),
    scores=spec(F32, 16, 128, 512),
    dkvf=spec(F32, 2, 256, 256),
    outst=spec(BF, 4, 32, 256),
    ingst=spec(BF, 4, 32, 256),
    outrv=spec(BF, 2, 64, 256),
    ingrv=spec(BF, 2, 64, 256),
    dmh=spec(BF, 256, 128),
)
LAYER = dict(
    qkst=spec(BF, 2, 32, 256),
    vst=spec(BF, 2, 32, 128),
    gus=spec(BF, 2, 32, 768),
    wds=spec(BF, 96, 256),
    cwo=spec(BF, 32, 256),
    cwd=spec(BF, 96, 256),
    wqk=spec(BF, 4, 8, 32, 256),
    wval=spec(BF, 4, 4, 2, 32, 128),
    wout=spec(BF, 4, 4, 32, 256),
    wgu=spec(BF, 4, 4, 2, 32, 768),
    wdn=spec(BF, 4, 4, 96, 256),
    kv=spec(BF, 4, 2, 256, 256),
    q2=spec(BF, 512, 128),
    prob=spec(BF, 16, 128, 512),
    ot=spec(F32, 128, 256),
    gu=spec(F32, 256, 768),
    hid=spec(BF, 256, 384),
    dkv=spec(BF, 4, 2, 256, 256),
    dkvab=spec(BF, 2, 2, 256, 256),
    dkvc=spec(BF, 256, 256),
    dkvds=spec(BF, 256, 256),
    dkvd=spec(BF, 256, 256),
    dkves=spec(BF, 256, 256),
    dkve=spec(BF, 256, 256),
    gwq=spec(BF, 4, 8, 32, 128),
    gwk=spec(BF, 4, 8, 32, 128),
    gwv=spec(BF, 4, 4, 2, 32, 128),
    gwout=spec(BF, 4, 4, 32, 256),
    gwgu=spec(BF, 4, 4, 2, 32, 768),
    gwdn=spec(BF, 4, 4, 96, 256),
    rzq=spec(BF, 3, 8, 32, 128),
    rzk=spec(BF, 3, 8, 32, 128),
    ryv=spec(BF, 3, 4, 2, 32, 128),
    rzout=spec(BF, 3, 4, 32, 256),
    rygu=spec(BF, 3, 4, 2, 32, 768),
    rzdn=spec(BF, 3, 4, 96, 256),
    sq=spec(BF, 8, 32, 128),
    sk=spec(BF, 8, 32, 128),
    sv=spec(BF, 4, 2, 32, 128),
    sout=spec(BF, 4, 32, 256),
    sgu=spec(BF, 4, 2, 32, 768),
    sdn=spec(BF, 4, 96, 256),
    fq=spec(BF, 8, 32, 128),
    fk=spec(BF, 8, 32, 128),
    fv=spec(BF, 8, 32, 128),
    fgu=spec(BF, 8, 32, 768),
    yout=spec(BF, 4, 32, 256),
    ydn=spec(BF, 4, 96, 256),
    cout=spec(BF, 32, 256),
    cdn=spec(BF, 96, 256),
    fout=spec(BF, 32, 256),
    fdn=spec(BF, 96, 256),
)
SUB = dict(
    a=spec(BF, 8, 32, 1024),
    h=spec(BF, 32, 1024),
    gr=spec(BF, 32, 1024),
    gb=spec(BF, 8, 32, 1024),
)
EXCHANGE = dict(
    pb=spec(BF, 2, 4, 32, 1024),
    sib=spec(BF, 4, 32, 1024),
    xs=spec(BF, 3, 32, 1024),
    xr=spec(BF, 3, 32, 1024),
)
N_SEM = 640
N_LAYERS, N_SUB, N_EXCHANGE = 2, 4, 8


def groups():
    arguments = [(0, 0, COMMON_IN)] + [(1, l, LAYER_IN) for l in range(N_LAYERS)]
    results = [(0, 0, COMMON_OUT)] + [(1, l, LAYER_OUT) for l in range(N_LAYERS)]
    scratch = [(0, 0, COMMON)] + [(1, l, LAYER) for l in range(N_LAYERS)]
    scratch += [(2, i, SUB) for i in range(N_SUB)] + [(3, n, EXCHANGE) for n in range(N_EXCHANGE)]
    return arguments, results, scratch


def named(refs):
    spaces = [[SimpleNamespace() for _ in range(n)] for n in (1, N_LAYERS, N_SUB, N_EXCHANGE)]
    left = list(refs)
    for group in groups():
        for kind, index, specs in group:
            for name in specs:
                setattr(spaces[kind][index], name, left.pop(0))
    return spaces[0][0], spaces[1], spaces[2], spaces[3]


def specs_of(group):
    return [entry for _, _, specs in group for entry in specs.values()]


def nn(a, b):
    return lax.dot_general(a, b, (((1,), (0,)), ((), ())), preferred_element_type=F32)


def nt(a, b):
    return lax.dot_general(a, b, (((1,), (1,)), ((), ())), preferred_element_type=F32)


def tn(a, b):
    return lax.dot_general(a, b, (((0,), (0,)), ((), ())), preferred_element_type=F32)


def normalize(h):
    inverse = lax.rsqrt(jnp.mean(h * h, axis=-1, keepdims=True) + EPS)
    return h * inverse, inverse


def kernel(*refs):
    R, L, S, X = named(refs[:-1])
    sems = refs[-1]
    used = [0]
    pending = []

    def new():
        used[0] += 1
        return sems.at[used[0] - 1]

    x = lax.axis_index("section")
    c = lax.axis_index("ctx")
    z, y, k = lax.div(c, 8), lax.rem(lax.div(c, 2), 4), lax.rem(c, 2)
    t = 2 * x + k
    s = lax.div(y, 2)
    yy = lax.rem(y, 2)
    other = 1 - k

    def plus(v, j):
        return lax.rem(v + j, 4)

    def dev(xd, zd, yd, kd):
        return {"section": xd, "ctx": zd * 8 + yd * 2 + kd}

    def flip(j):
        return k if j % 2 == 0 else other

    sibling = dev(x, z, y, other)

    def put(src, dst, to, rsem):
        copy = pltpu.make_async_remote_copy(
            src_ref=src, dst_ref=dst, send_sem=new(), recv_sem=rsem, device_id=to, device_id_type=MESH
        )
        copy.start()
        pending.append((None, copy))

    def put_or_keep(mine, src, dst, to, rsem):
        copy = pltpu.make_async_remote_copy(
            src_ref=src, dst_ref=dst, send_sem=new(), recv_sem=rsem, device_id=to, device_id_type=MESH
        )

        @pl.when(mine)
        def _():
            pltpu.make_async_copy(src, dst, rsem).start()

        @pl.when(jnp.logical_not(mine))
        def _():
            copy.start()

        pending.append((mine, copy))

    def arrived(ref, sem):
        pltpu.make_async_copy(ref, ref, sem).wait()

    barrier = pltpu.get_barrier_semaphore()

    def greet(d):
        pl.semaphore_signal(barrier, inc=1, device_id=d, device_id_type=MESH)

    count = 0
    for j in range(4):
        for i in range(2):
            if (j, i) != (0, 0):
                greet(dev(plus(x, j), z, y, flip(i)))
                count += 1
            if j:
                greet(dev(x, z, plus(y, j), flip(i)))
                greet(dev(x, plus(z, j), y, flip(i)))
                count += 2
            greet(dev(plus(x, j), 3 - z, 3 - y, flip(i)))
            count += 1
    crossing = jnp.where(x == z, 0, 1)

    @pl.when(x != z)
    def _():
        greet(dev(z, x, y, k))

    lane = lax.broadcasted_iota(I32, (1, 768), 1)
    half = (lane >= 384).astype(I32)
    place = lane - 384 * half
    group = (place >= 96).astype(I32) + (place >= 192).astype(I32) + (place >= 288).astype(I32)
    place = place - 96 * group
    unit = jnp.where(place < 88, 352 * half + 88 * group + place, -1)
    R.pick[...] = (lax.broadcasted_iota(I32, (704, 768), 0) == unit).astype(F32).astype(BF)
    stacked = jnp.concatenate([w[...] for l in range(2) for w in (L[l].wg, L[l].wu)], axis=0)
    stacked = nn(stacked, R.pick[...]).astype(BF)
    for l in range(2):
        for i in range(2):
            L[l].qkst[i, :, 0:128] = L[l].wq[:, 128 * i : 128 * i + 128]
            L[l].qkst[i, :, 128:256] = L[l].wk[:, 128 * i : 128 * i + 128]
            L[l].vst[i] = L[l].wv[:, 128 * i : 128 * i + 128]
            for n in range(2):
                rows = stacked[64 * l + 32 * n : 64 * l + 32 * n + 32, 384 * i : 384 * i + 384]
                L[l].gus[i, :, 384 * n : 384 * n + 384] = rows
        L[l].wds[0:88, :] = L[l].wd[...]
        L[l].wds[88:96, :] = jnp.zeros((8, 256), BF)
    column = lax.broadcasted_iota(I32, (32, 128), 1) - 32 * lax.rem(c, 4)
    spot = (lax.broadcasted_iota(I32, (32, 128), 0) == column).astype(F32).astype(BF)
    piece = nn(jnp.broadcast_to(R.gains_in[...].astype(F32), (8, 32)).astype(BF), spot)
    R.gst[...] = jnp.where(lax.broadcasted_iota(I32, (8, 128), 0) == x, piece, 0.0)
    R.gg[...] = jnp.zeros((8, 1024), F32)
    pl.semaphore_wait(barrier, count + crossing)

    W = [SimpleNamespace(), SimpleNamespace()]
    G = [SimpleNamespace(), SimpleNamespace()]
    partner = dev(x, z, y + 1 - 2 * yy, k)
    mate = 1 - yy
    slot_m = 2 * yy + k

    def keep(src, dst, sem):
        pltpu.make_async_copy(src, dst, sem).start()

    def to_z(src, dst, js=(1, 3, 2)):
        sem = new()
        for j in js:
            put(src, dst, dev(x, plus(z, j), y, k), sem)
        return sem

    def to_y(src, dst, js=(1, 3, 2)):
        sem = new()
        for j in js:
            put(src, dst, dev(x, z, plus(y, j), k), sem)
        return sem

    def qk_first(l):
        src, dst = L[l].qkst, L[l].wqk.at[z, 2 * y + k]
        sem = W[l].qk = new()
        keep(src.at[k], dst, sem)
        for j in (2, 6, 4, 3, 7, 5, 1):
            put(src.at[flip(j)], dst, dev(x, z, plus(y, j // 2), flip(j)), sem)

    def qk_second(l):
        w = L[l].wqk
        arrived(w.at[z], W[l].qk)
        W[l].qk = to_z(w.at[z], w.at[z])

    def z_first(src, w):
        sem, dst = new(), w.at[z, y, k]
        keep(src.at[k], dst, sem)
        for j in (2, 6, 4, 3, 7, 5, 1):
            put(src.at[flip(j)], dst, dev(x, plus(z, j // 2), y, flip(j)), sem)
        return sem

    def v_second(l):
        w = L[l].wval
        arrived(w.at[:, y], W[l].v)
        W[l].v = to_y(w.at[:, y], w.at[:, y])

    def gate_second(l):
        arrived(L[l].wgu.at[:, y], W[l].gu)
        w = L[l].wgu.at[:, y, :, :, 0:384]
        W[l].gate = to_y(w, w)

    def up_second(l):
        w = L[l].wgu.at[:, y, :, :, 384:768]
        W[l].up = to_y(w, w)

    def cross_first(src, dst):
        sem = new()
        put_or_keep(x == z, src, dst, dev(z, x, y, k), sem)
        return sem

    def cross_second(src, w, sem):
        arrived(src, sem)
        sem, dst = new(), w.at[z, slot_m]
        put_or_keep(s == k, src, dst, dev(x, z, y, s), sem)
        for j in (1, 3, 2):
            put(src, dst, dev(x, z, plus(y, j), s), sem)
        return sem

    def cross_third(w, sem):
        arrived(w.at[z], sem)
        return to_z(w.at[z], w.at[z])

    def rs_start(n, part):
        pb, sib = X[n].pb, X[n].sib
        for i in range(8):
            pb[i % 2, i // 2] = part[32 * i : 32 * i + 32].astype(BF)
        sem = [new() for _ in range(4)]
        for j in (1, 3, 2, 0):
            xd = plus(x, j)
            put(pb.at[other, xd], sib.at[xd], sibling, sem[j])
        return sem

    def rs_mid(n, sem):
        pb, sib, xs, xr = X[n].pb, X[n].sib, X[n].xs, X[n].xr
        out = []
        for j in (1, 3, 2):
            xd = plus(x, j)
            arrived(sib.at[xd], sem[j])
            xs[j - 1] = (pb[k, xd].astype(F32) + sib[xd].astype(F32)).astype(BF)
            out.append(new())
            put(xs.at[j - 1], xr.at[j - 1], dev(xd, z, y, k), out[-1])
        return sem[0], out

    def rs_end(n, sems_):
        pb, sib, xr = X[n].pb, X[n].sib, X[n].xr
        own, out = sems_
        arrived(sib.at[x], own)
        total = pb[k, x].astype(F32) + sib[x].astype(F32)
        for j, sem in zip((1, 3, 2), out):
            arrived(xr.at[j - 1], sem)
            total += xr[j - 1].astype(F32)
        return total

    def gather(buf, block):
        buf[t] = block
        rx = [new() for _ in range(4)]
        rk = [new() for _ in range(4)]
        for j in (1, 3, 2):
            put(buf.at[t], buf.at[t], dev(plus(x, j), z, y, k), rx[j])
        put(buf.at[t], buf.at[t], sibling, rk[0])
        for j in (1, 3, 2):
            slot = buf.at[2 * plus(x, 4 - j) + k]
            arrived(slot, rx[j])
            put(slot, slot, sibling, rk[j])
        for j in range(4):
            arrived(buf.at[0], rk[j])

    def to_owners(rows, stage, landing):
        for i in range(4):
            stage[i] = rows[:, 256 * i : 256 * i + 256]
        near = x < 2
        zd, yd = jnp.where(near, z, 3 - z), jnp.where(near, y, 3 - y)
        kd = lax.rem(x, 2)
        sem = new()
        dst = landing.at[s, pl.ds(pl.multiple_of(32 * k, 32), 32)]
        put_or_keep(near & (kd == k), stage.at[x], dst, dev(x, zd, yd, kd), sem)
        for j in range(1, 4):
            xd = plus(x, j)
            put(stage.at[xd], dst, dev(xd, zd, yd, kd), sem)
        return sem

    def spread_tokens(src, dst):
        near, far = pl.ds(2 * k, 2), pl.ds(4 + 2 * k, 2)
        close, mirrored = new(), new()
        put(src.at[1 - s], dst.at[far], dev(x, 3 - z, 3 - y, k), mirrored)
        put(src.at[s], dst.at[near], sibling, close)
        dst[near] = src[s]
        return close, mirrored

    def spread_rest(dst, sems_):
        close, mirrored = sems_
        far = pl.ds(4 + 2 * k, 2)
        arrived(dst.at[far], mirrored)
        put(dst.at[far], dst.at[far], sibling, close)
        arrived(dst.at[0:4], close)

    lane = lax.rem(lax.broadcasted_iota(I32, (1, 512), 1), 256)
    own_block = 4 * z + y
    query_pos = jnp.where(lane < 128, 128 * own_block + lane, 128 * (15 - own_block) + lane - 128)
    ids = R.seg[s]

    def tokens_to(n):
        return jnp.sum(jnp.where(ids <= n, 1.0, 0.0), axis=1, keepdims=True).astype(I32)

    first, second = tokens_to(0), tokens_to(1)
    query_start = jnp.where(query_pos < first, 0, jnp.where(query_pos < second, first, second))
    head_lane = lax.broadcasted_iota(I32, (256, 128), 1) < 64

    def two_heads(v):
        zero = jnp.zeros_like(v)
        return jnp.concatenate([jnp.where(head_lane, v, zero), jnp.where(head_lane, zero, v)], axis=0)

    def own_heads(vt):
        return jnp.concatenate([vt[0:64, 0:256], vt[64:128, 256:512]], axis=0)

    def gain_row(i):
        return R.gains[i : i + 1, :]

    def full(ref):
        return ref[...].reshape(256, 1024)

    def keys_of(l, zz):
        return L[l].kv[zz, :, :, 0:128].reshape(512, 128)

    def values_of(l, zz):
        return L[l].kv[zz, :, :, 128:256].reshape(512, 128)

    def attention_forward(l, hook):
        w = L[l].wqk
        arrived(w.at[0:3], W[l].qk)
        a = full(S[2 * l].a)
        qk = nn(a, w[...].reshape(1024, 256))
        w = L[l].wval
        arrived(w.at[0:3], W[l].v)
        u = nn(a, w[...].reshape(1024, 128))
        q = (qk[:, 0:128].astype(BF) * 0.125).astype(BF)
        keys = qk[:, 128:256].astype(BF)
        if l == 0:
            values = u.astype(BF)
        else:
            values = (0.5 * u + 0.5 * L[0].kv[z, yy, :, 128:256].astype(F32)).astype(BF)
        kv = L[l].kv
        kv[z, yy, :, 0:128] = keys
        kv[z, yy, :, 128:256] = values
        q2 = two_heads(q)
        L[l].q2[...] = q2
        own, near = kv.at[z, yy], kv.at[z, mate]
        direct, relayed, from_mate = [new() for _ in range(4)], [new() for _ in range(4)], new()
        for j in (1, 3):
            put(own, own, dev(x, plus(z, j), y, k), direct[j])
        put(own, own, partner, from_mate)
        put(own, own, dev(x, plus(z, 2), y, k), direct[2])
        arrived(near, from_mate)
        for j in (1, 3):
            put(near, near, dev(x, plus(z, j), y, k), relayed[j])
        scores = R.scores
        top = jnp.full((1, 512), MASKED, F32)
        for j in (0, 3, 1, 2):
            zz = plus(z, j)
            if j % 2:
                arrived(kv.at[zz, yy], direct[4 - j])
                arrived(kv.at[zz, mate], relayed[4 - j])
            elif j:
                arrived(kv.at[zz, mate], relayed[2])
            scores[4 * j : 4 * j + 4] = nt(keys_of(l, zz), L[l].q2[...]).reshape(4, 128, 512)

            def mask(i, top, j=j, zz=zz):
                block = 4 * zz + 2 * s + lax.div(i, 2)
                base = 128 * (block + lax.rem(i, 2) * (15 - 2 * block))
                row = lax.broadcasted_iota(I32, (128, 512), 0)
                seen = (row >= query_start - base) & (row <= query_pos - base)
                v = jnp.where(seen, scores[4 * j + i], MASKED)
                scores[4 * j + i] = v
                return jnp.maximum(top, jnp.max(v, axis=0, keepdims=True))

            top = lax.fori_loop(0, 4, mask, top)
            if j == 0:
                opposite = kv.at[plus(z, 2), yy]
                arrived(opposite, direct[2])
                put(opposite, opposite, partner, relayed[2])
        hook()

        def expo(i, total):
            v = jnp.exp(scores[i] - top)
            scores[i] = v
            return total + jnp.sum(v, axis=0, keepdims=True)

        total = lax.fori_loop(0, 16, expo, jnp.zeros((1, 512), F32))
        share = 1.0 / total
        prob = L[l].prob

        def norm(i, carry):
            prob[i] = (scores[i] * share).astype(BF)
            return carry

        lax.fori_loop(0, 16, norm, 0)
        ot = jnp.zeros((128, 512), F32)
        for j in range(4):
            ot += tn(values_of(l, plus(z, j)), prob[4 * j : 4 * j + 4].reshape(512, 512))
        ot = own_heads(ot)
        L[l].ot[...] = ot
        o = jnp.transpose(ot).astype(BF)
        arrived(L[l].wout.at[0:3], W[l].o)
        return jnp.concatenate([nn(o, L[l].wout[i].reshape(128, 256)) for i in range(4)], axis=1)

    def feedforward_forward(l, hook):
        a, w = full(S[2 * l + 1].a), L[l].wgu
        arrived(w.at[0:3, :, :, :, 0:384], W[l].gate)
        gate = nn(a, w[:, :, :, :, 0:384].reshape(1024, 384))
        arrived(w.at[0:3, :, :, :, 384:768], W[l].up)
        up = nn(a, w[:, :, :, :, 384:768].reshape(1024, 384))
        L[l].gu[:, 0:384] = gate
        L[l].gu[:, 384:768] = up
        hidden = (gate * jax.nn.sigmoid(gate) * up).astype(BF)
        L[l].hid[...] = hidden
        hook()
        arrived(L[l].wdn.at[0:3], W[l].d)
        return jnp.concatenate([nn(hidden, L[l].wdn[i].reshape(384, 256)) for i in range(4)], axis=1)

    def next_rows(i, part, hook=None):
        sems_ = rs_mid(i, rs_start(i, part))
        if hook is not None:
            hook()
        total = rs_end(i, sems_)
        rows = (S[i].h[...].astype(F32) + total).astype(BF)
        S[i + 1].h[...] = rows
        normed, _ = normalize(rows.astype(F32))
        gather(S[i + 1].a, (normed * gain_row(i + 1)).astype(BF))

    def norm_backward(i, da):
        normed, inverse = normalize(S[i].h[...].astype(F32))
        R.gg[i : i + 1, :] = jnp.sum(da * normed, axis=0, keepdims=True)
        scaled = da * gain_row(i)
        mixed = scaled - normed * jnp.mean(scaled * normed, axis=-1, keepdims=True)
        return (S[i].gr[...].astype(F32) + inverse * mixed).astype(BF)

    def send_z(g, landing):
        sem = new()
        for j in (1, 3, 2):
            zd = plus(z, j)
            put(g.at[zd], landing.at[j - 1], dev(x, zd, y, k), sem)
        return sem

    def send_y(g, landing):
        sem = new()
        for j in (1, 3, 2):
            yd = plus(y, j)
            put(g.at[:, yd], landing.at[j - 1], dev(x, z, yd, k), sem)
        return sem

    def attention_backward(l, hook1, hook2):
        i0 = 2 * l
        gb = full(S[i0].gb)
        wo = L[l].wout
        dot_ = nt(wo[0].reshape(128, 256), gb[:, 0:256])
        for i in range(1, 4):
            dot_ += nt(wo[i].reshape(128, 256), gb[:, 256 * i : 256 * i + 256])
        dot_ = dot_.astype(BF).astype(F32)
        do2 = two_heads(jnp.transpose(dot_).astype(BF))
        prod = dot_ * L[l].ot[...]
        delta = jnp.concatenate(
            [jnp.sum(prod[0:64], axis=0, keepdims=True), jnp.sum(prod[64:128], axis=0, keepdims=True)], axis=1
        )
        dkv, prob = L[l].dkv, L[l].prob
        dq = jnp.zeros((128, 512), F32)
        ab, c_sem = [new() for _ in range(4)], new()
        for j in (2, 1, 3, 0):
            zz = plus(z, j)
            p = prob[4 * j : 4 * j + 4].reshape(512, 512)
            dp = nt(values_of(l, zz), do2)
            ds = (p.astype(F32) * (dp - delta)).astype(BF)
            dkv[zz, :, :, 0:128] = nn(ds, L[l].q2[...]).astype(BF).reshape(2, 256, 128)
            dkv[zz, :, :, 128:256] = nn(p, do2).astype(BF).reshape(2, 256, 128)
            if j % 2:
                put(dkv.at[zz], L[l].dkvab.at[j // 2], dev(x, zz, y, k), ab[j])
            elif j:
                put(dkv.at[zz, mate], L[l].dkvc, partner, c_sem)
            dq += tn(keys_of(l, zz), ds)
        dq = jnp.transpose(own_heads(dq) * 0.125).astype(BF)
        gw = L[l].gwout
        otb = L[l].ot[...].astype(BF)
        for i in range(4):
            gw[i] = nn(otb, gb[:, 256 * i : 256 * i + 256]).astype(BF).reshape(4, 32, 256)
        at = jnp.transpose(full(S[i0].a))
        L[l].gwq[...] = nn(at, dq).astype(BF).reshape(4, 8, 32, 128)
        arrived(L[l].dkvc, c_sem)
        far = plus(z, 2)
        L[l].dkvds[...] = (dkv[far, yy].astype(F32) + L[l].dkvc[...].astype(F32)).astype(BF)
        d_sem, e_sem = new(), new()
        put(L[l].dkvds, L[l].dkvd, dev(x, far, y, k), d_sem)
        got = L[l].dkvab
        arrived(got.at[0], ab[1])
        arrived(got.at[1], ab[3])
        R.dkvf[...] = dkv[z].astype(F32) + got[0].astype(F32) + got[1].astype(F32)
        L[l].dkves[...] = R.dkvf[mate].astype(BF)
        put(L[l].dkves, L[l].dkve, partner, e_sem)
        G[l].o = send_z(gw, L[l].rzout)
        G[l].q = send_z(L[l].gwq, L[l].rzq)
        arrived(L[l].dkvd, d_sem)
        arrived(L[l].dkve, e_sem)
        tot = R.dkvf[yy] + L[l].dkvd[...].astype(F32) + L[l].dkve[...].astype(F32)
        dk = tot[:, 0:128].astype(BF)
        dvals = tot[:, 128:256]
        if l == 1:
            half = 0.5 * dvals.astype(BF).astype(F32)
            du = half.astype(BF)
            R.dmh[...] = du
        else:
            du = (dvals + R.dmh[...].astype(F32)).astype(BF)
        da = nt(jnp.concatenate([dq, dk], axis=1), L[l].wqk[...].reshape(1024, 256))
        da += nt(du, L[l].wval[...].reshape(1024, 128))
        rs = rs_start(4 + i0, da)
        grads = nn(at, jnp.concatenate([dk, du], axis=1)).astype(BF)
        L[l].gwk[...] = grads[:, 0:128].reshape(4, 8, 32, 128)
        L[l].gwv[...] = grads[:, 128:256].reshape(4, 4, 2, 32, 128)
        rs = rs_mid(4 + i0, rs)
        G[l].k = send_z(L[l].gwk, L[l].rzk)
        G[l].v = send_y(L[l].gwv, L[l].ryv)
        hook1()
        hook2()
        return norm_backward(i0, rs_end(4 + i0, rs))

    def feedforward_backward(l, hook1, hook2):
        i0 = 2 * l + 1
        gb = full(S[i0].gb)
        wd = L[l].wdn
        dhid = nt(gb[:, 0:256], wd[0].reshape(384, 256))
        for i in range(1, 4):
            dhid += nt(gb[:, 256 * i : 256 * i + 256], wd[i].reshape(384, 256))
        gu = L[l].gu[...]
        gate, up = gu[:, 0:384], gu[:, 384:768]
        sig = jax.nn.sigmoid(gate)
        dgate = dhid * up * sig * (1.0 + gate * (1.0 - sig))
        dup = dhid * (gate * sig)
        dgu = jnp.concatenate([dgate.astype(BF), dup.astype(BF)], axis=1)
        rs = rs_start(4 + i0, nt(dgu, L[l].wgu[...].reshape(1024, 768)))
        hook1()
        rs = rs_mid(4 + i0, rs)
        at = jnp.transpose(full(S[i0].a))
        gw = L[l].gwgu
        gw[...] = nn(at, dgu).astype(BF).reshape(4, 4, 2, 32, 768)
        G[l].g = send_y(gw, L[l].rygu)
        ht = jnp.transpose(L[l].hid[...])
        gw = L[l].gwdn
        for i in range(4):
            gw[i] = nn(ht, gb[:, 256 * i : 256 * i + 256]).astype(BF).reshape(4, 96, 256)
        G[l].d = send_z(gw, L[l].rzdn)
        hook2()
        return norm_backward(i0, rs_end(4 + i0, rs))

    def summed(own, got):
        return own.astype(F32) + got[0].astype(F32) + got[1].astype(F32) + got[2].astype(F32)

    def rows_back(st, land):
        sem = new()
        for j in range(4):
            m = plus(slot_m, j)
            to = dev(x, z, 2 * k + lax.div(m, 2), lax.rem(m, 2))
            if j == 0:
                put_or_keep(s == k, st.at[m], land.at[y], to, sem)
            else:
                put(st.at[m], land.at[y], to, sem)
        return sem

    def four(land):
        return land[0].astype(F32) + land[1].astype(F32) + land[2].astype(F32) + land[3].astype(F32)

    def out_second(l):
        arrived(L[l].rzout, G[l].o)
        L[l].sout[...] = summed(L[l].gwout[z], L[l].rzout).astype(BF)
        G[l].o = rows_back(L[l].sout, L[l].yout)

    def out_third(l):
        arrived(L[l].yout, G[l].o)
        L[l].cout[...] = four(L[l].yout).astype(BF)
        G[l].o = cross_first(L[l].cout, L[l].fout)

    def out_end(l):
        arrived(L[l].fout, G[l].o)
        L[l].oo[...] = L[l].fout[...].astype(F32)

    def down_second(l):
        arrived(L[l].rzdn, G[l].d)
        L[l].sdn[...] = summed(L[l].gwdn[z], L[l].rzdn).astype(BF)
        G[l].d = rows_back(L[l].sdn, L[l].ydn)

    def down_third(l):
        arrived(L[l].ydn, G[l].d)
        L[l].cdn[...] = four(L[l].ydn).astype(BF)
        G[l].d = cross_first(L[l].cdn, L[l].fdn)

    def down_end(l):
        arrived(L[l].fdn, G[l].d)
        L[l].od[...] = L[l].fdn[0:88, :].astype(F32)

    def rows_y(g, got, st, land, sem):
        arrived(got, sem)
        st[...] = summed(g[z], got).astype(BF)
        sem = new()
        land[0] = st[2 * y + k]
        for j in (2, 6, 4, 3, 7, 5, 1):
            yd, kd = plus(y, j // 2), flip(j)
            put(st.at[2 * yd + kd], land.at[j], dev(x, z, yd, kd), sem)
        return sem

    def rows_z(g, got, st, land, sem):
        arrived(got, sem)
        for i in range(4):
            own = g[i, y].astype(F32) + got[0, i].astype(F32) + got[1, i].astype(F32) + got[2, i].astype(F32)
            st[i] = own.astype(BF)
        sem = new()
        land[0] = st[z, k]
        for j in (2, 6, 4, 3, 7, 5, 1):
            zd, kd = plus(z, j // 2), flip(j)
            put(st.at[zd, kd], land.at[j], dev(x, zd, y, kd), sem)
        return sem

    def halves(land, sem):
        arrived(land.at[1:8], sem)
        own = land[0].astype(F32) + land[2].astype(F32) + land[4].astype(F32) + land[6].astype(F32)
        far = land[1].astype(F32) + land[3].astype(F32) + land[5].astype(F32) + land[7].astype(F32)
        return jnp.where(k == 0, own, far), jnp.where(k == 0, far, own)

    def q_second(l):
        G[l].q = rows_y(L[l].gwq, L[l].rzq, L[l].sq, L[l].fq, G[l].q)

    def k_second(l):
        G[l].k = rows_y(L[l].gwk, L[l].rzk, L[l].sk, L[l].fk, G[l].k)

    def v_grad_second(l):
        G[l].v = rows_z(L[l].gwv, L[l].ryv, L[l].sv, L[l].fv, G[l].v)

    def gu_grad_second(l):
        G[l].g = rows_z(L[l].gwgu, L[l].rygu, L[l].sgu, L[l].fgu, G[l].g)

    def att_end(l):
        for land, result, sem in ((L[l].fq, L[l].oq, G[l].q), (L[l].fk, L[l].ok, G[l].k), (L[l].fv, L[l].ov, G[l].v)):
            low, high = halves(land, sem)
            result[:, 0:128] = low
            result[:, 128:256] = high

    def gu_end(l):
        low, high = halves(L[l].fgu, G[l].g)
        both = jnp.concatenate(
            [
                jnp.concatenate([low[:, 0:384], high[:, 0:384]], axis=1),
                jnp.concatenate([low[:, 384:768], high[:, 384:768]], axis=1),
            ],
            axis=0,
        )
        main = both.astype(BF)
        rest = (both - main.astype(F32)).astype(BF)
        both = nt(main, R.pick[...]) + nt(rest, R.pick[...])
        L[l].og[...] = both[0:32]
        L[l].ou[...] = both[32:64]

    def nothing():
        pass

    def att_first(l):
        qk_first(l)
        W[l].v = z_first(L[l].vst, L[l].wval)
        W[l].o = cross_first(L[l].wo, L[l].cwo)

    def ff_first(l):
        W[l].gu = z_first(L[l].gus, L[l].wgu)
        W[l].d = cross_first(L[l].wds, L[l].cwd)

    qk_first(0)
    W[0].v = z_first(L[0].vst, L[0].wval)
    in_sems = spread_tokens(R.xin, R.hin)
    gx_sem = new()
    for j in (1, 3, 2):
        put(R.gst, R.gx.at[j - 1], dev(plus(x, j), z, y, k), gx_sem)
    W[0].o = cross_first(L[0].wo, L[0].cwo)
    arrived(R.gx, gx_sem)
    R.g1[...] = R.gst[...] + R.gx[0] + R.gx[1] + R.gx[2]
    gy_sem = new()
    R.gyr[2 * y + k] = R.g1[...]
    for j in range(1, 8):
        put(R.g1, R.gyr.at[2 * y + k], dev(x, z, plus(y, j // 2), flip(j)), gy_sem)
    qk_second(0)
    v_second(0)
    ff_first(0)
    W[0].o = cross_second(L[0].cwo, L[0].wout, W[0].o)
    arrived(R.gyr.at[0:7], gy_sem)
    for i in range(2):
        R.gz[z, i] = R.gyr[4 * i] + R.gyr[4 * i + 1] + R.gyr[4 * i + 2] + R.gyr[4 * i + 3]
    gz_sem = to_z(R.gz.at[z], R.gz.at[z])
    spread_rest(R.hin, in_sems)
    normed, _ = normalize(full(R.hin).astype(F32))
    S[0].h[...] = R.hin[t]
    arrived(R.gz.at[0:3], gz_sem)
    R.gains[...] = jnp.concatenate([R.gz[i // 2, i % 2] for i in range(8)], axis=1)
    S[0].a[...] = (normed * gain_row(0)).astype(BF).reshape(8, 32, 1024)
    W[0].o = cross_third(L[0].wout, W[0].o)
    gate_second(0)
    W[0].d = cross_second(L[0].cwd, L[0].wdn, W[0].d)
    cot_sems = []

    def after_keys_0():
        up_second(0)
        W[0].d = cross_third(L[0].wdn, W[0].d)
        att_first(1)
        ff_first(1)

    def in_ff_0():
        qk_second(1)
        v_second(1)
        W[1].o = cross_second(L[1].cwo, L[1].wout, W[1].o)

    def after_sum_1():
        W[1].o = cross_third(L[1].wout, W[1].o)
        gate_second(1)
        W[1].d = cross_second(L[1].cwd, L[1].wdn, W[1].d)

    def after_keys_1():
        up_second(1)
        W[1].d = cross_third(L[1].wdn, W[1].d)
        cot_sems.append(spread_tokens(R.cot, S[3].gb))

    def nothing():
        pass

    next_rows(0, attention_forward(0, after_keys_0))
    next_rows(1, feedforward_forward(0, in_ff_0), after_sum_1)
    next_rows(2, attention_forward(1, after_keys_1))
    last = rs_mid(3, rs_start(3, feedforward_forward(1, lambda: spread_rest(S[3].gb, cot_sems[0]))))
    S[3].gr[...] = S[3].gb[t]
    out_sem = []

    def finish_outputs():
        rows = (S[3].h[...].astype(F32) + rs_end(3, last)).astype(BF)
        out_sem.append(to_owners(rows, R.outst, R.outrv))

    def hand_back(i, rows):
        S[i].gr[...] = rows
        gather(S[i].gb, rows)

    def ff_grads(l):
        gu_grad_second(l)
        down_second(l)

    def att_grads():
        out_second(1)
        q_second(1)
        k_second(1)
        v_grad_second(1)

    def last_grads():
        out_second(0)
        q_second(0)
        ff_grads(0)

    hand_back(2, feedforward_backward(1, finish_outputs, nothing))
    hand_back(1, attention_backward(1, lambda: ff_grads(1), nothing))
    down_third(1)
    hand_back(0, feedforward_backward(0, att_grads, lambda: gu_end(1)))
    out_third(1)
    rows = attention_backward(0, last_grads, lambda: att_end(1))
    in_grad_sem = to_owners(rows, R.ingst, R.ingrv)
    gg_sem = new()
    for j in (1, 3, 2):
        put(R.gg, R.ggx.at[j - 1], dev(plus(x, j), z, y, k), gg_sem)
    k_second(0)
    v_grad_second(0)
    out_third(0)
    down_third(0)
    arrived(R.ggx, gg_sem)
    gg = R.gg[...] + R.ggx[0] + R.ggx[1] + R.ggx[2]
    for i in range(4):
        R.ggz[i] = gg[:, 256 * i : 256 * i + 256]
    gg_sem = new()
    for j in (1, 3, 2):
        zd = plus(z, j)
        put(R.ggz.at[zd], R.ggzr.at[j - 1], dev(x, zd, y, k), gg_sem)
    out_end(1)
    down_end(1)
    gu_end(0)
    arrived(R.outrv, out_sem[0])
    R.out[...] = R.outrv[...].reshape(2, 1, 64, 256)
    arrived(R.ggzr, gg_sem)
    gg = R.ggz[z] + R.ggzr[0] + R.ggzr[1] + R.ggzr[2]
    R.ggy[0] = gg[:, 0:128]
    R.ggy[1] = gg[:, 128:256]
    gg_sem = new()
    R.ggyr[0] = R.ggy[s]
    for j in range(1, 8):
        yd = plus(y, j // 2)
        put(R.ggy.at[lax.div(yd, 2)], R.ggyr.at[j], dev(x, z, yd, flip(j)), gg_sem)
    arrived(R.ingrv, in_grad_sem)
    R.ing[...] = R.ingrv[...].reshape(2, 1, 64, 256)
    att_end(0)
    out_end(0)
    down_end(0)
    arrived(R.ggyr.at[1:8], gg_sem)
    gg = R.ggyr[0]
    for j in range(1, 8):
        gg = gg + R.ggyr[j]
    gg = jnp.sum(jnp.where(lax.broadcasted_iota(I32, (8, 128), 0) == x, gg, 0.0), axis=0, keepdims=True)
    part = lax.rem(c, 4)
    gain = jnp.zeros((1, 32), F32)
    for i in range(4):
        gain += jnp.where(part == i, gg[:, 32 * i : 32 * i + 32], 0.0)
    R.ogg[...] = gain
    for mine, copy in pending:
        if mine is None:
            copy.wait_send()
        else:

            @pl.when(jnp.logical_not(mine))
            def _(copy=copy):
                copy.wait_send()

    assert used[0] <= N_SEM, used


def call(*args):
    whole = pl.BlockSpec(memory_space=pltpu.VMEM)
    arguments, results, scratch = (specs_of(group) for group in groups())
    return pl.pallas_call(
        kernel,
        out_shape=[jax.ShapeDtypeStruct(shape, dtype) for shape, dtype in results],
        in_specs=[whole] * len(arguments),
        out_specs=[whole] * len(results),
        scratch_shapes=[pltpu.VMEM(shape, dtype) for shape, dtype in scratch]
        + [pltpu.SemaphoreType.DMA((N_SEM,))],
        compiler_params=pltpu.CompilerParams(
            collective_id=0, has_side_effects=True, vmem_limit_bytes=62 * 1024 * 1024
        ),
    )(*args)


def hand_out(*refs):
    n = len(refs) // 2
    copies = [pltpu.make_async_copy(refs[i], refs[n + i], refs[-1].at[i]) for i in range(n)]
    for copy in copies:
        copy.start()
    for copy in copies:
        copy.wait()


def body(inputs, cotangent, segment_ids, gains, *weights):
    first = (inputs.reshape(2, 2, 32, 1024), cotangent.reshape(2, 2, 32, 1024), segment_ids, gains)
    results = call(*first, *weights)
    anywhere = pl.BlockSpec(memory_space=pl.ANY)
    return tuple(
        pl.pallas_call(
            hand_out,
            out_shape=[jax.ShapeDtypeStruct(r.shape, r.dtype) for r in results],
            in_specs=[pl.BlockSpec(memory_space=pltpu.VMEM)] * len(results),
            out_specs=[anywhere] * len(results),
            scratch_shapes=[pltpu.SemaphoreType.DMA((len(results),))],
        )(*results)
    )


def solution(mesh):
    tokens = P(None, None, "ctx", None)
    weight = P("ctx", "section")
    return jax.shard_map(
        body,
        mesh=mesh,
        in_specs=(tokens, tokens, P(), P("section", "ctx")) + (weight,) * 14,
        out_specs=(P(None, None, "ctx", "section"),) * 2 + (P("section", "ctx"),) + (weight,) * 14,
        check_vma=False,
    )
```

```python
from types import SimpleNamespace

import jax
import jax.numpy as jnp
from jax import lax
from jax.experimental import pallas as pl
from jax.experimental.pallas import tpu as pltpu
from jax.sharding import PartitionSpec as P

MESH = pl.DeviceIdType.MESH
BF = jnp.bfloat16
F32 = jnp.float32
I32 = jnp.int32
EPS = 1e-06
MASKED = -1e30


def spec(dtype, *shape):
    return shape, dtype


LAYER_IN = dict(
    wq=spec(BF, 32, 256),
    wk=spec(BF, 32, 256),
    wv=spec(BF, 32, 256),
    wo=spec(BF, 32, 256),
    wg=spec(BF, 32, 704),
    wu=spec(BF, 32, 704),
    wd=spec(BF, 88, 256),
)
COMMON_IN = dict(
    xin=spec(BF, 2, 4, 16, 1024), cot=spec(BF, 2, 4, 16, 1024), seg=spec(I32, 2, 1, 2048), gains_in=spec(BF, 1, 32)
)
LAYER_OUT = dict(
    oq=spec(F32, 32, 256),
    ok=spec(F32, 32, 256),
    ov=spec(F32, 32, 256),
    oo=spec(F32, 32, 256),
    og=spec(F32, 32, 704),
    ou=spec(F32, 32, 704),
    od=spec(F32, 88, 256),
)
COMMON_OUT = dict(out=spec(BF, 2, 1, 64, 256), ing=spec(BF, 2, 1, 64, 256), ogg=spec(F32, 1, 32))
COMMON = dict(
    hin=spec(BF, 2, 8, 16, 1024),
    pick=spec(BF, 704, 768),
    gst=spec(F32, 8, 128),
    gx=spec(F32, 3, 8, 128),
    g1=spec(F32, 8, 128),
    gyr=spec(F32, 8, 8, 128),
    gz=spec(F32, 4, 2, 8, 128),
    gains=spec(F32, 8, 1024),
    gg=spec(F32, 8, 1024),
    ggx=spec(F32, 3, 8, 1024),
    ggz=spec(F32, 4, 8, 256),
    ggzr=spec(F32, 3, 8, 256),
    ggy=spec(F32, 2, 8, 128),
    ggyr=spec(F32, 8, 8, 128),
    scores=spec(F32, 16, 128, 512),
    dkvf=spec(F32, 2, 256, 256),
    outst=spec(BF, 2, 4, 16, 256),
    ingst=spec(BF, 2, 4, 16, 256),
    outrv=spec(BF, 2, 64, 256),
    ingrv=spec(BF, 2, 64, 256),
    dmh=spec(BF, 256, 128),
    ds=spec(BF, 4, 512, 512),
    do2=spec(BF, 512, 128),
    dgu=spec(BF, 2, 128, 768),
)
LAYER = dict(
    qkst=spec(BF, 2, 32, 256),
    vst=spec(BF, 2, 32, 128),
    gus=spec(BF, 2, 32, 768),
    wds=spec(BF, 96, 256),
    cwo=spec(BF, 32, 256),
    cwd=spec(BF, 96, 256),
    wqk=spec(BF, 4, 8, 32, 256),
    wval=spec(BF, 4, 4, 2, 32, 128),
    wout=spec(BF, 4, 4, 32, 256),
    wgu=spec(BF, 4, 4, 2, 32, 768),
    wdn=spec(BF, 4, 4, 96, 256),
    kv=spec(BF, 4, 2, 2, 128, 256),
    q2=spec(BF, 512, 128),
    prob=spec(BF, 16, 128, 512),
    ot=spec(F32, 128, 256),
    gu=spec(F32, 256, 768),
    hid=spec(BF, 256, 384),
    dkv=spec(BF, 4, 2, 256, 256),
    dkvab=spec(BF, 2, 2, 256, 256),
    dkvc=spec(BF, 256, 256),
    dkvds=spec(BF, 256, 256),
    dkvd=spec(BF, 256, 256),
    dkves=spec(BF, 256, 256),
    dkve=spec(BF, 256, 256),
    gwq=spec(BF, 4, 8, 32, 128),
    gwk=spec(BF, 4, 8, 32, 128),
    gwv=spec(BF, 4, 4, 2, 32, 128),
    gwout=spec(BF, 4, 4, 32, 256),
    gwgu=spec(BF, 4, 4, 2, 32, 768),
    gwdn=spec(BF, 4, 4, 96, 256),
    rzq=spec(BF, 3, 8, 32, 128),
    rzk=spec(BF, 3, 8, 32, 128),
    ryv=spec(BF, 3, 4, 2, 32, 128),
    rzout=spec(BF, 3, 4, 32, 256),
    hygu=spec(BF, 2, 2, 2, 32, 768),
    bygu=spec(BF, 2, 4, 2, 32, 768),
    hzdn=spec(BF, 2, 2, 96, 256),
    bzdn=spec(BF, 2, 4, 96, 256),
    share=spec(F32, 8, 512),
    sq=spec(BF, 8, 32, 128),
    sk=spec(BF, 8, 32, 128),
    sv=spec(BF, 4, 2, 32, 128),
    sout=spec(BF, 4, 32, 256),
    sgu=spec(BF, 4, 2, 32, 768),
    sdn=spec(BF, 4, 96, 256),
    fq=spec(BF, 8, 32, 128),
    fk=spec(BF, 8, 32, 128),
    fv=spec(BF, 8, 32, 128),
    fgu=spec(BF, 8, 32, 768),
    yout=spec(BF, 4, 32, 256),
    ydn=spec(BF, 4, 96, 256),
    cout=spec(BF, 32, 256),
    cdn=spec(BF, 96, 256),
    fout=spec(BF, 32, 256),
    fdn=spec(BF, 96, 256),
)
SUB = dict(
    a=spec(BF, 2, 8, 16, 1024),
    h=spec(BF, 2, 16, 1024),
    gr=spec(BF, 2, 16, 1024),
    gb=spec(BF, 2, 8, 16, 1024),
)
EXCHANGE = dict(
    pb=spec(BF, 2, 2, 4, 16, 1024),
    sib=spec(BF, 2, 4, 16, 1024),
    xs=spec(BF, 2, 3, 16, 1024),
    xr=spec(BF, 2, 3, 16, 1024),
)
N_SEM = 960
N_LAYERS, N_SUB, N_EXCHANGE = 2, 4, 8


def groups():
    arguments = [(0, 0, COMMON_IN)] + [(1, l, LAYER_IN) for l in range(N_LAYERS)]
    results = [(0, 0, COMMON_OUT)] + [(1, l, LAYER_OUT) for l in range(N_LAYERS)]
    scratch = [(0, 0, COMMON)] + [(1, l, LAYER) for l in range(N_LAYERS)]
    scratch += [(2, i, SUB) for i in range(N_SUB)] + [(3, n, EXCHANGE) for n in range(N_EXCHANGE)]
    return arguments, results, scratch


def named(refs):
    spaces = [[SimpleNamespace() for _ in range(n)] for n in (1, N_LAYERS, N_SUB, N_EXCHANGE)]
    left = list(refs)
    for group in groups():
        for kind, index, specs in group:
            for name in specs:
                setattr(spaces[kind][index], name, left.pop(0))
    return spaces[0][0], spaces[1], spaces[2], spaces[3]


def specs_of(group):
    return [entry for _, _, specs in group for entry in specs.values()]


def nn(a, b):
    return lax.dot_general(a, b, (((1,), (0,)), ((), ())), preferred_element_type=F32)


def nt(a, b):
    return lax.dot_general(a, b, (((1,), (1,)), ((), ())), preferred_element_type=F32)


def tn(a, b):
    return lax.dot_general(a, b, (((0,), (0,)), ((), ())), preferred_element_type=F32)


def normalize(h):
    inverse = lax.rsqrt(jnp.mean(h * h, axis=-1, keepdims=True) + EPS)
    return h * inverse, inverse


def kernel(*refs):
    R, L, S, X = named(refs[:-1])
    sems = refs[-1]
    used = [0]
    pending = []

    def new():
        used[0] += 1
        return sems.at[used[0] - 1]

    x = lax.axis_index("section")
    c = lax.axis_index("ctx")
    z, y, k = lax.div(c, 8), lax.rem(lax.div(c, 2), 4), lax.rem(c, 2)
    t = 2 * x + k
    s = lax.div(y, 2)
    yy = lax.rem(y, 2)
    other = 1 - k

    def plus(v, j):
        return lax.rem(v + j, 4)

    def dev(xd, zd, yd, kd):
        return {"section": xd, "ctx": zd * 8 + yd * 2 + kd}

    def flip(j):
        return k if j % 2 == 0 else other

    sibling = dev(x, z, y, other)

    def put(src, dst, to, rsem):
        copy = pltpu.make_async_remote_copy(
            src_ref=src, dst_ref=dst, send_sem=new(), recv_sem=rsem, device_id=to, device_id_type=MESH
        )
        copy.start()
        pending.append((None, copy))

    def put_or_keep(mine, src, dst, to, rsem):
        copy = pltpu.make_async_remote_copy(
            src_ref=src, dst_ref=dst, send_sem=new(), recv_sem=rsem, device_id=to, device_id_type=MESH
        )

        @pl.when(mine)
        def _():
            pltpu.make_async_copy(src, dst, rsem).start()

        @pl.when(jnp.logical_not(mine))
        def _():
            copy.start()

        pending.append((mine, copy))

    def arrived(ref, sem):
        pltpu.make_async_copy(ref, ref, sem).wait()

    barrier = pltpu.get_barrier_semaphore()

    def greet(d):
        pl.semaphore_signal(barrier, inc=1, device_id=d, device_id_type=MESH)

    count = 0
    for j in range(4):
        for i in range(2):
            if (j, i) != (0, 0):
                greet(dev(plus(x, j), z, y, flip(i)))
                count += 1
            if j:
                greet(dev(x, z, plus(y, j), flip(i)))
                greet(dev(x, plus(z, j), y, flip(i)))
                count += 2
            greet(dev(plus(x, j), 3 - z, 3 - y, flip(i)))
            count += 1
    crossing = jnp.where(x == z, 0, 1)

    @pl.when(x != z)
    def _():
        greet(dev(z, x, y, k))

    def pack_att(l):
        for i in range(2):
            L[l].qkst[i, :, 0:128] = L[l].wq[:, 128 * i : 128 * i + 128]
            L[l].qkst[i, :, 128:256] = L[l].wk[:, 128 * i : 128 * i + 128]
            L[l].vst[i] = L[l].wv[:, 128 * i : 128 * i + 128]

    def pack_rest():
        lane = lax.broadcasted_iota(I32, (1, 768), 1)
        half = (lane >= 384).astype(I32)
        place = lane - 384 * half
        group = (place >= 96).astype(I32) + (place >= 192).astype(I32) + (place >= 288).astype(I32)
        place = place - 96 * group
        unit = jnp.where(place < 88, 352 * half + 88 * group + place, -1)
        R.pick[...] = (lax.broadcasted_iota(I32, (704, 768), 0) == unit).astype(F32).astype(BF)
        stacked = jnp.concatenate([w[...] for l in range(2) for w in (L[l].wg, L[l].wu)], axis=0)
        stacked = nn(stacked, R.pick[...]).astype(BF)
        for l in range(2):
            for i in range(2):
                for n in range(2):
                    rows = stacked[64 * l + 32 * n : 64 * l + 32 * n + 32, 384 * i : 384 * i + 384]
                    L[l].gus[i, :, 384 * n : 384 * n + 384] = rows
            L[l].wds[0:88, :] = L[l].wd[...]
            L[l].wds[88:96, :] = jnp.zeros((8, 256), BF)
        pack_att(1)
        R.gg[...] = jnp.zeros((8, 1024), F32)

    pack_att(0)
    column = lax.broadcasted_iota(I32, (32, 128), 1) - 32 * lax.rem(c, 4)
    spot = (lax.broadcasted_iota(I32, (32, 128), 0) == column).astype(F32).astype(BF)
    piece = nn(jnp.broadcast_to(R.gains_in[...].astype(F32), (8, 32)).astype(BF), spot)
    R.gst[...] = jnp.where(lax.broadcasted_iota(I32, (8, 128), 0) == x, piece, 0.0)
    pl.semaphore_wait(barrier, count + crossing)

    W = [SimpleNamespace(), SimpleNamespace()]
    G = [SimpleNamespace(), SimpleNamespace()]
    partner = dev(x, z, y + 1 - 2 * yy, k)
    mate = 1 - yy
    slot_m = 2 * yy + k

    def keep(src, dst, sem):
        pltpu.make_async_copy(src, dst, sem).start()

    def to_z(src, dst, js=(1, 3, 2)):
        sem = new()
        for j in js:
            put(src, dst, dev(x, plus(z, j), y, k), sem)
        return sem

    def to_y(src, dst, js=(1, 3, 2)):
        sem = new()
        for j in js:
            put(src, dst, dev(x, z, plus(y, j), k), sem)
        return sem

    def qk_first(l):
        src, dst = L[l].qkst, L[l].wqk.at[z, 2 * y + k]
        sem = W[l].qk = new()
        keep(src.at[k], dst, sem)
        for j in (2, 6, 4, 3, 7, 5, 1):
            put(src.at[flip(j)], dst, dev(x, z, plus(y, j // 2), flip(j)), sem)

    def qk_second(l):
        w = L[l].wqk
        arrived(w.at[z], W[l].qk)
        W[l].qk = to_z(w.at[z], w.at[z])

    def z_first(src, w):
        sem, dst = new(), w.at[z, y, k]
        keep(src.at[k], dst, sem)
        for j in (2, 6, 4, 3, 7, 5, 1):
            put(src.at[flip(j)], dst, dev(x, plus(z, j // 2), y, flip(j)), sem)
        return sem

    def v_second(l):
        w = L[l].wval
        arrived(w.at[:, y], W[l].v)
        W[l].v = to_y(w.at[:, y], w.at[:, y])

    def at_y(j):
        return dev(x, z, plus(y, j), k)

    def at_z(j):
        return dev(x, plus(z, j), y, k)

    def ring_start(block, v, at):
        sems_ = [new() for _ in range(4)]
        put(block(v), block(v), at(1), sems_[0])
        put(block(v), block(v), at(3), sems_[1])
        return block, v, at, sems_

    def ring_relay(state):
        block, v, at, sems_ = state
        before, after = plus(v, 3), plus(v, 1)
        arrived(block(before), sems_[0])
        put(block(before, 0), block(before, 0), at(1), sems_[2])
        arrived(block(after), sems_[1])
        put(block(after, 1), block(after, 1), at(3), sems_[3])

    def ring_end(state):
        block, v, at, sems_ = state
        far = plus(v, 2)
        arrived(block(far, 0), sems_[2])
        arrived(block(far, 1), sems_[3])

    def halved(h):
        return slice(None) if h is None else slice(2 * h, 2 * h + 2)

    def gate_start(l):
        arrived(L[l].wgu.at[:, y], W[l].gu)
        W[l].gate = ring_start(lambda v, h=None: L[l].wgu.at[halved(h), v, :, :, 0:384], y, at_y)

    def up_start(l):
        W[l].up = ring_start(lambda v, h=None: L[l].wgu.at[halved(h), v, :, :, 384:768], y, at_y)

    def down_start(l):
        arrived(L[l].wdn.at[z], W[l].d)
        W[l].d = ring_start(lambda v, h=None: L[l].wdn.at[v, halved(h)], z, at_z)

    def cross_first(src, dst):
        sem = new()
        put_or_keep(x == z, src, dst, dev(z, x, y, k), sem)
        return sem

    def cross_second(src, w, sem):
        arrived(src, sem)
        sem, dst = new(), w.at[z, slot_m]
        put_or_keep(s == k, src, dst, dev(x, z, y, s), sem)
        for j in (1, 3, 2):
            put(src, dst, dev(x, z, plus(y, j), s), sem)
        return sem

    def cross_third(w, sem):
        arrived(w.at[z], sem)
        return to_z(w.at[z], w.at[z])

    streams = (0, 1)
    sums = {}

    def rs_start(n, i, part):
        pb, sib = X[n].pb, X[n].sib
        for r in range(8):
            pb[i, r % 2, r // 2] = part[16 * r : 16 * r + 16].astype(BF)
        sem = sums[n, i] = [new() for _ in range(4)]
        for j in (1, 3, 2, 0):
            xd = plus(x, j)
            put(pb.at[i, other, xd], sib.at[i, xd], sibling, sem[j])

    def rs_mid(n, i):
        pb, sib, xs, xr = X[n].pb, X[n].sib, X[n].xs, X[n].xr
        sem, out = sums[n, i], []
        for j in (1, 3, 2):
            xd = plus(x, j)
            arrived(sib.at[i, xd], sem[j])
            xs[i, j - 1] = (pb[i, k, xd].astype(F32) + sib[i, xd].astype(F32)).astype(BF)
            out.append(new())
            put(xs.at[i, j - 1], xr.at[i, j - 1], dev(xd, z, y, k), out[-1])
        sums[n, i] = sem[0], out

    def rs_end(n, i):
        pb, sib, xr = X[n].pb, X[n].sib, X[n].xr
        own, out = sums[n, i]
        arrived(sib.at[i, x], own)
        total = pb[i, k, x].astype(F32) + sib[i, x].astype(F32)
        for j, sem in zip((1, 3, 2), out):
            arrived(xr.at[i, j - 1], sem)
            total += xr[i, j - 1].astype(F32)
        return total

    def gather_start(buf, i, block):
        buf[i, t] = block
        mine = buf.at[i, t]
        rx = [new() for _ in range(4)]
        rk = [new() for _ in range(4)]
        for j in (1, 3, 2):
            put(mine, mine, dev(plus(x, j), z, y, k), rx[j])
        put(mine, mine, sibling, rk[0])
        return buf, i, rx, rk

    def gather_forward(state):
        if state is not None:
            buf, i, rx, rk = state
            for j in (1, 3, 2):
                slot = buf.at[i, 2 * plus(x, 4 - j) + k]
                arrived(slot, rx[j])
                put(slot, slot, sibling, rk[j])

    def gather_finish(state):
        if state is not None:
            buf, i, rx, rk = state
            for j in range(4):
                arrived(buf.at[i, 0], rk[j])

    def nothing():
        pass

    def opened(states, n, work, early=nothing):
        gather_finish(states[0])
        work(0)
        gather_forward(states[1])
        rs_mid(n, 0)
        early()
        gather_finish(states[1])
        work(1)
        rs_mid(n, 1)

    def closed(rows_of, buf, between):
        first = gather_start(buf, 0, rows_of(0))
        second = gather_start(buf, 1, rows_of(1))
        between()
        gather_forward(first)
        return first, second

    def to_owners(i, rows, stage, landing, sem):
        for r in range(4):
            stage[i, r] = rows[:, 256 * r : 256 * r + 256]
        zd, yd = (z, y) if i == 0 else (3 - z, 3 - y)
        kd = lax.div(x, 2)
        first_row = pl.multiple_of(16 * (2 * lax.rem(x, 2) + k), 16)
        dst = landing.at[s, pl.ds(first_row, 16)]
        for j in range(4):
            xd = plus(x, j)
            if i == 0 and j == 0:
                put_or_keep(kd == k, stage.at[i, xd], dst, dev(xd, zd, yd, kd), sem)
            else:
                put(stage.at[i, xd], dst, dev(xd, zd, yd, kd), sem)

    def spread_tokens(src, dst):
        rows = pl.ds(4 * k, 4)
        close, mirrored = new(), new()
        put(src.at[1 - s], dst.at[1, rows], dev(x, 3 - z, 3 - y, k), mirrored)
        put(src.at[s], dst.at[0, rows], sibling, close)
        dst[0, rows] = src[s]
        return close, mirrored

    def spread_rest(dst, sems_):
        close, mirrored = sems_
        far = dst.at[1, pl.ds(4 * k, 4)]
        arrived(far, mirrored)
        put(far, far, sibling, close)
        arrived(dst.at[0], close)

    lane = lax.broadcasted_iota(I32, (1, 512), 1)
    own_block = 4 * z + y
    query_pos = 128 * jnp.where(lane < 256, own_block, 15 - own_block) + lax.rem(lane, 128)
    ids = R.seg[s]

    def tokens_to(n):
        return jnp.sum(jnp.where(ids <= n, 1.0, 0.0), axis=1, keepdims=True).astype(I32)

    first, second = tokens_to(0), tokens_to(1)
    query_start = jnp.where(query_pos < first, 0, jnp.where(query_pos < second, first, second))
    head_lane = lax.broadcasted_iota(I32, (128, 128), 1) < 64

    def two_heads(v):
        zero = jnp.zeros_like(v)
        return jnp.concatenate([jnp.where(head_lane, v, zero), jnp.where(head_lane, zero, v)], axis=0)

    def own_heads(vt):
        return jnp.concatenate([vt[0:64, 0:128], vt[64:128, 128:256]], axis=0)

    def gain_row(i):
        return R.gains[i : i + 1, :]

    def full(ref):
        return ref[...].reshape(256, 1024)

    def keys_of(l, zz):
        return L[l].kv[zz, :, :, :, 0:128].reshape(512, 128)

    def values_of(l, zz):
        return L[l].kv[zz, :, :, :, 128:256].reshape(512, 128)

    def attention_forward(l, states, hook, late):
        kv = L[l].kv
        direct, relayed = [[new() for _ in range(4)] for _ in streams], [[new() for _ in range(4)] for _ in streams]
        from_mate = [new() for _ in streams]
        for i in streams:
            if i == 1:
                gather_forward(states[1])
            gather_finish(states[i])
            a = S[2 * l].a[i].reshape(128, 1024)
            w = L[l].wqk
            if i == 0:
                arrived(w.at[0:3], W[l].qk)
            qk = nn(a, w[...].reshape(1024, 256))
            w = L[l].wval
            if i == 0:
                arrived(w.at[0:3], W[l].v)
            u = nn(a, w[...].reshape(1024, 128))
            if l == 0:
                values = u.astype(BF)
            else:
                values = (0.5 * u + 0.5 * L[0].kv[z, yy, i, :, 128:256].astype(F32)).astype(BF)
            kv[z, yy, i, :, 0:128] = qk[:, 128:256].astype(BF)
            kv[z, yy, i, :, 128:256] = values
            own = kv.at[z, yy, i]
            for j in (1, 3):
                put(own, own, dev(x, plus(z, j), y, k), direct[i][j])
            put(own, own, partner, from_mate[i])
            put(own, own, dev(x, plus(z, 2), y, k), direct[i][2])
            L[l].q2[256 * i : 256 * i + 256, :] = two_heads((qk[:, 0:128].astype(BF) * 0.125).astype(BF))
        for i in streams:
            near = kv.at[z, mate, i]
            arrived(near, from_mate[i])
            for j in (1, 3):
                put(near, near, dev(x, plus(z, j), y, k), relayed[i][j])
        scores = R.scores
        top = jnp.full((1, 512), MASKED, F32)
        for j in (0, 3, 1, 2):
            zz = plus(z, j)
            for i in streams:
                if j % 2:
                    arrived(kv.at[zz, yy, i], direct[i][4 - j])
                    arrived(kv.at[zz, mate, i], relayed[i][4 - j])
                elif j:
                    arrived(kv.at[zz, mate, i], relayed[i][2])
            scores[4 * j : 4 * j + 4] = nt(keys_of(l, zz), L[l].q2[...]).reshape(4, 128, 512)

            def mask(i, top, j=j, zz=zz):
                block = 4 * zz + 2 * s + lax.div(i, 2)
                base = 128 * (block + lax.rem(i, 2) * (15 - 2 * block))
                row = lax.broadcasted_iota(I32, (128, 512), 0)
                seen = (row >= query_start - base) & (row <= query_pos - base)
                v = jnp.where(seen, scores[4 * j + i], MASKED)
                scores[4 * j + i] = v
                return jnp.maximum(top, jnp.max(v, axis=0, keepdims=True))

            top = lax.fori_loop(0, 4, mask, top)
            if j == 0:
                for i in streams:
                    opposite = kv.at[plus(z, 2), yy, i]
                    arrived(opposite, direct[i][2])
                    put(opposite, opposite, partner, relayed[i][2])
        hook()
        prob = L[l].prob
        for i in streams:
            lanes = slice(256 * i, 256 * i + 256)
            high = top[:, lanes]

            def expo(r, total):
                v = jnp.exp(scores[r, :, lanes] - high)
                prob[r, :, lanes] = v.astype(BF)
                return total + jnp.sum(v, axis=0, keepdims=True)

            share = 1.0 / lax.fori_loop(0, 16, expo, jnp.zeros((1, 256), F32))
            L[l].share[0:1, lanes] = share
            ot = jnp.zeros((128, 256), F32)
            for j in range(4):
                ot += tn(values_of(l, plus(z, j)), prob[4 * j : 4 * j + 4, :, lanes].reshape(512, 256))
            ot = ot * share
            ot = own_heads(ot)
            L[l].ot[:, 128 * i : 128 * i + 128] = ot
            o = jnp.transpose(ot).astype(BF)
            if i == 0:
                arrived(L[l].wout.at[0:3], W[l].o)
            part = jnp.concatenate([nn(o, L[l].wout[r].reshape(128, 256)) for r in range(4)], axis=1)
            rs_start(2 * l, i, part)
        for i in streams:
            rs_mid(2 * l, i)
        late()

    def feedforward_forward(l, states, early, hook):
        w = L[l].wgu

        def work(i):
            a = S[2 * l + 1].a[i].reshape(128, 1024)
            if i == 0:
                ring_end(W[l].gate)
            gate = nn(a, w[:, :, :, :, 0:384].reshape(1024, 384))
            if i == 0:
                ring_end(W[l].up)
            up = nn(a, w[:, :, :, :, 384:768].reshape(1024, 384))
            rows = slice(128 * i, 128 * i + 128)
            L[l].gu[rows, 0:384] = gate
            L[l].gu[rows, 384:768] = up
            hidden = (gate * jax.nn.sigmoid(gate) * up).astype(BF)
            L[l].hid[rows, :] = hidden
            if i == 0:
                ring_end(W[l].d)
            part = jnp.concatenate([nn(hidden, L[l].wdn[r].reshape(384, 256)) for r in range(4)], axis=1)
            rs_start(2 * l + 1, i, part)

        opened(states, 2 * l + 1, work, early)
        hook()

    def next_rows(n, between=nothing):
        def rows_of(i):
            rows = (S[n].h[i].astype(F32) + rs_end(n, i)).astype(BF)
            S[n + 1].h[i] = rows
            normed, _ = normalize(rows.astype(F32))
            return (normed * gain_row(n + 1)).astype(BF)

        return closed(rows_of, S[n + 1].a, between)

    def norm_backward(n, i):
        da = rs_end(4 + n, i)
        normed, inverse = normalize(S[n].h[i].astype(F32))
        gain_part = jnp.sum(da * normed, axis=0, keepdims=True)
        if i == 0:
            R.gg[n : n + 1, :] = gain_part
        else:
            R.gg[n : n + 1, :] += gain_part
        scaled = da * gain_row(n)
        mixed = scaled - normed * jnp.mean(scaled * normed, axis=-1, keepdims=True)
        return (S[n].gr[i].astype(F32) + inverse * mixed).astype(BF)

    def hand_back(n, between=nothing):
        def rows_of(i):
            rows = norm_backward(n, i)
            S[n - 1].gr[i] = rows
            return rows

        return closed(rows_of, S[n - 1].gb, between)

    def send_z(g, landing):
        sem = new()
        for j in (1, 3, 2):
            zd = plus(z, j)
            put(g.at[zd], landing.at[j - 1], dev(x, zd, y, k), sem)
        return sem

    def send_y(g, landing):
        sem = new()
        for j in (1, 3, 2):
            yd = plus(y, j)
            put(g.at[:, yd], landing.at[j - 1], dev(x, z, yd, k), sem)
        return sem

    def attention_backward(l, states, hook):
        n = 2 * l
        wo, dkv, prob = L[l].wout, L[l].dkv, L[l].prob
        ab, c_sem = [new() for _ in range(4)], new()
        dq = []
        for i in streams:
            if i == 1:
                gather_forward(states[1])
            gather_finish(states[i])
            gb = S[n].gb[i].reshape(128, 1024)
            dot_ = nt(wo[0].reshape(128, 256), gb[:, 0:256])
            for r in range(1, 4):
                dot_ += nt(wo[r].reshape(128, 256), gb[:, 256 * r : 256 * r + 256])
            dot_ = dot_.astype(BF).astype(F32)
            do2 = two_heads(jnp.transpose(dot_).astype(BF))
            share = L[l].share[0:1, 256 * i : 256 * i + 256]
            head_row = lax.broadcasted_iota(I32, (128, 128), 0) < 64
            scaled = dot_ * jnp.where(head_row, share[:, 0:128], share[:, 128:256])
            R.do2[256 * i : 256 * i + 256, :] = two_heads(jnp.transpose(scaled).astype(BF))
            prod = dot_ * L[l].ot[:, 128 * i : 128 * i + 128]
            delta = jnp.concatenate(
                [jnp.sum(prod[0:64], axis=0, keepdims=True), jnp.sum(prod[64:128], axis=0, keepdims=True)], axis=1
            )
            lanes = slice(256 * i, 256 * i + 256)
            dqt = jnp.zeros((128, 256), F32)
            for j in (2, 1, 3, 0):
                zz = plus(z, j)
                p = prob[4 * j : 4 * j + 4, :, lanes].reshape(512, 256)
                dp = nt(values_of(l, zz), do2)
                ds = (p.astype(F32) * ((dp - delta) * share)).astype(BF)
                R.ds[j, :, lanes] = ds
                if i == 1:
                    p = prob[4 * j : 4 * j + 4].reshape(512, 512)
                    dkv[zz, :, :, 0:128] = nn(R.ds[j], L[l].q2[...]).astype(BF).reshape(2, 256, 128)
                    dkv[zz, :, :, 128:256] = nn(p, R.do2[...]).astype(BF).reshape(2, 256, 128)
                    if j % 2:
                        put(dkv.at[zz], L[l].dkvab.at[j // 2], dev(x, zz, y, k), ab[j])
                    elif j:
                        put(dkv.at[zz, mate], L[l].dkvc, partner, c_sem)
                dqt += tn(keys_of(l, zz), ds)
            dq.append(jnp.transpose(own_heads(dqt) * 0.125).astype(BF))
        dq = jnp.concatenate(dq, axis=0)
        gb = full(S[n].gb)
        gw = L[l].gwout
        otb = L[l].ot[...].astype(BF)
        for i in range(4):
            gw[i] = nn(otb, gb[:, 256 * i : 256 * i + 256]).astype(BF).reshape(4, 32, 256)
        at = jnp.transpose(full(S[n].a))
        L[l].gwq[...] = nn(at, dq).astype(BF).reshape(4, 8, 32, 128)
        arrived(L[l].dkvc, c_sem)
        far = plus(z, 2)
        L[l].dkvds[...] = (dkv[far, yy].astype(F32) + L[l].dkvc[...].astype(F32)).astype(BF)
        d_sem, e_sem = new(), new()
        put(L[l].dkvds, L[l].dkvd, dev(x, far, y, k), d_sem)
        got = L[l].dkvab
        arrived(got.at[0], ab[1])
        arrived(got.at[1], ab[3])
        R.dkvf[...] = dkv[z].astype(F32) + got[0].astype(F32) + got[1].astype(F32)
        L[l].dkves[...] = R.dkvf[mate].astype(BF)
        put(L[l].dkves, L[l].dkve, partner, e_sem)
        arrived(L[l].dkvd, d_sem)
        arrived(L[l].dkve, e_sem)
        tot = R.dkvf[yy] + L[l].dkvd[...].astype(F32) + L[l].dkve[...].astype(F32)
        dk = tot[:, 0:128].astype(BF)
        dvals = tot[:, 128:256]
        if l == 1:
            half = 0.5 * dvals.astype(BF).astype(F32)
            du = half.astype(BF)
            R.dmh[...] = du
        else:
            du = (dvals + R.dmh[...].astype(F32)).astype(BF)
        for i in streams:
            rows = slice(128 * i, 128 * i + 128)
            da = nt(jnp.concatenate([dq[rows], dk[rows]], axis=1), L[l].wqk[...].reshape(1024, 256))
            da += nt(du[rows], L[l].wval[...].reshape(1024, 128))
            rs_start(4 + n, i, da)
        for i in streams:
            rs_mid(4 + n, i)
        grads = nn(at, jnp.concatenate([dk, du], axis=1)).astype(BF)
        L[l].gwk[...] = grads[:, 0:128].reshape(4, 8, 32, 128)
        L[l].gwv[...] = grads[:, 128:256].reshape(4, 4, 2, 32, 128)
        G[l].k = send_z(L[l].gwk, L[l].rzk)
        G[l].o = send_z(L[l].gwout, L[l].rzout)
        G[l].q = send_z(L[l].gwq, L[l].rzq)
        G[l].v = send_y(L[l].gwv, L[l].ryv)
        hook()

    def feedforward_backward(l, states, hook):
        n = 2 * l + 1

        def work(i):
            gb = S[n].gb[i].reshape(128, 1024)
            wd = L[l].wdn
            dhid = nt(gb[:, 0:256], wd[0].reshape(384, 256))
            for r in range(1, 4):
                dhid += nt(gb[:, 256 * r : 256 * r + 256], wd[r].reshape(384, 256))
            gu = L[l].gu[128 * i : 128 * i + 128, :]
            gate, up = gu[:, 0:384], gu[:, 384:768]
            sig = jax.nn.sigmoid(gate)
            dgate = dhid * up * sig * (1.0 + gate * (1.0 - sig))
            dup = dhid * (gate * sig)
            dgu = jnp.concatenate([dgate.astype(BF), dup.astype(BF)], axis=1)
            R.dgu[i] = dgu
            rs_start(4 + n, i, nt(dgu, L[l].wgu[...].reshape(1024, 768)))

        opened(states, 4 + n, work)
        at = jnp.transpose(full(S[n].a))
        gw = L[l].gwgu
        gw[...] = nn(at, R.dgu[...].reshape(256, 768)).astype(BF).reshape(4, 4, 2, 32, 768)
        far = plus(y, 2)
        G[l].g = [new() for _ in range(4)]
        put(gw.at[0:2, far], L[l].hygu.at[0], at_y(1), G[l].g[0])
        put(gw.at[2:4, far], L[l].hygu.at[1], at_y(3), G[l].g[1])
        gb = full(S[n].gb)
        ht = jnp.transpose(L[l].hid[...])
        gw = L[l].gwdn
        for i in range(4):
            gw[i] = nn(ht, gb[:, 256 * i : 256 * i + 256]).astype(BF).reshape(4, 96, 256)
        far = plus(z, 2)
        G[l].d = [new() for _ in range(4)]
        put(gw.at[far, 0:2], L[l].hzdn.at[0], at_z(1), G[l].d[0])
        put(gw.at[far, 2:4], L[l].hzdn.at[1], at_z(3), G[l].d[1])
        hook()

    def ff_push(l):
        gu, dn, hg, hd = L[l].gwgu, L[l].gwdn, L[l].hygu, L[l].hzdn
        for h, j in ((0, 1), (1, 3)):
            yd, zd, half = plus(y, j), plus(z, j), slice(2 * h, 2 * h + 2)
            arrived(hg.at[h], G[l].g[h])
            gu[half, yd] = (gu[half, yd].astype(F32) + hg[h].astype(F32)).astype(BF)
            put(gu.at[:, yd], L[l].bygu.at[h], at_y(j), G[l].g[2 + h])
            arrived(hd.at[h], G[l].d[h])
            dn[zd, half] = (dn[zd, half].astype(F32) + hd[h].astype(F32)).astype(BF)
            put(dn.at[zd], L[l].bzdn.at[h], at_z(j), G[l].d[2 + h])

    def summed(own, got):
        return own.astype(F32) + got[0].astype(F32) + got[1].astype(F32) + got[2].astype(F32)

    def rows_back(st, land):
        sem = new()
        for j in range(4):
            m = plus(slot_m, j)
            to = dev(x, z, 2 * k + lax.div(m, 2), lax.rem(m, 2))
            if j == 0:
                put_or_keep(s == k, st.at[m], land.at[y], to, sem)
            else:
                put(st.at[m], land.at[y], to, sem)
        return sem

    def four(land):
        return land[0].astype(F32) + land[1].astype(F32) + land[2].astype(F32) + land[3].astype(F32)

    def out_second(l):
        arrived(L[l].rzout, G[l].o)
        L[l].sout[...] = summed(L[l].gwout[z], L[l].rzout).astype(BF)
        G[l].o = rows_back(L[l].sout, L[l].yout)

    def out_third(l):
        arrived(L[l].yout, G[l].o)
        L[l].cout[...] = four(L[l].yout).astype(BF)
        G[l].o = cross_first(L[l].cout, L[l].fout)

    def out_end(l):
        arrived(L[l].fout, G[l].o)
        L[l].oo[...] = L[l].fout[...].astype(F32)

    def down_second(l):
        got = L[l].bzdn
        arrived(got.at[0], G[l].d[2])
        arrived(got.at[1], G[l].d[3])
        L[l].sdn[...] = (L[l].gwdn[z].astype(F32) + got[0].astype(F32) + got[1].astype(F32)).astype(BF)
        G[l].d = rows_back(L[l].sdn, L[l].ydn)

    def down_third(l):
        arrived(L[l].ydn, G[l].d)
        L[l].cdn[...] = four(L[l].ydn).astype(BF)
        G[l].d = cross_first(L[l].cdn, L[l].fdn)

    def down_end(l):
        arrived(L[l].fdn, G[l].d)
        L[l].od[...] = L[l].fdn[0:88, :].astype(F32)

    def rows_y(g, got, st, land, sem):
        arrived(got, sem)
        st[...] = summed(g[z], got).astype(BF)
        sem = new()
        land[0] = st[2 * y + k]
        for j in (2, 6, 4, 3, 7, 5, 1):
            yd, kd = plus(y, j // 2), flip(j)
            put(st.at[2 * yd + kd], land.at[j], dev(x, z, yd, kd), sem)
        return sem

    def rows_z(st, land):
        sem = new()
        land[0] = st[z, k]
        for j in (2, 6, 4, 3, 7, 5, 1):
            zd, kd = plus(z, j // 2), flip(j)
            put(st.at[zd, kd], land.at[j], dev(x, zd, y, kd), sem)
        return sem

    def halves(land, sem):
        arrived(land.at[1:8], sem)
        own = land[0].astype(F32) + land[2].astype(F32) + land[4].astype(F32) + land[6].astype(F32)
        far = land[1].astype(F32) + land[3].astype(F32) + land[5].astype(F32) + land[7].astype(F32)
        return jnp.where(k == 0, own, far), jnp.where(k == 0, far, own)

    def q_second(l):
        G[l].q = rows_y(L[l].gwq, L[l].rzq, L[l].sq, L[l].fq, G[l].q)

    def k_second(l):
        G[l].k = rows_y(L[l].gwk, L[l].rzk, L[l].sk, L[l].fk, G[l].k)

    def v_grad_second(l):
        g, got, st = L[l].gwv, L[l].ryv, L[l].sv
        arrived(got, G[l].v)
        for i in range(4):
            own = g[i, y].astype(F32) + got[0, i].astype(F32) + got[1, i].astype(F32) + got[2, i].astype(F32)
            st[i] = own.astype(BF)
        G[l].v = rows_z(st, L[l].fv)

    def gu_grad_second(l):
        g, got, st = L[l].gwgu, L[l].bygu, L[l].sgu
        arrived(got.at[0], G[l].g[2])
        arrived(got.at[1], G[l].g[3])
        for i in range(4):
            st[i] = (g[i, y].astype(F32) + got[0, i].astype(F32) + got[1, i].astype(F32)).astype(BF)
        G[l].g = rows_z(st, L[l].fgu)

    def att_end(l):
        for land, result, sem in ((L[l].fq, L[l].oq, G[l].q), (L[l].fk, L[l].ok, G[l].k), (L[l].fv, L[l].ov, G[l].v)):
            low, high = halves(land, sem)
            result[:, 0:128] = low
            result[:, 128:256] = high

    def gu_end(l):
        low, high = halves(L[l].fgu, G[l].g)
        both = jnp.concatenate(
            [
                jnp.concatenate([low[:, 0:384], high[:, 0:384]], axis=1),
                jnp.concatenate([low[:, 384:768], high[:, 384:768]], axis=1),
            ],
            axis=0,
        )
        main = both.astype(BF)
        rest = (both - main.astype(F32)).astype(BF)
        both = nt(main, R.pick[...]) + nt(rest, R.pick[...])
        L[l].og[...] = both[0:32]
        L[l].ou[...] = both[32:64]

    def nothing():
        pass

    def att_first(l):
        qk_first(l)
        W[l].v = z_first(L[l].vst, L[l].wval)
        W[l].o = cross_first(L[l].wo, L[l].cwo)

    def ff_first(l):
        W[l].gu = z_first(L[l].gus, L[l].wgu)
        W[l].d = cross_first(L[l].wds, L[l].cwd)

    qk_first(0)
    W[0].v = z_first(L[0].vst, L[0].wval)
    in_sems = spread_tokens(R.xin, R.hin)
    gx_sem = new()
    for j in (1, 3, 2):
        put(R.gst, R.gx.at[j - 1], dev(plus(x, j), z, y, k), gx_sem)
    W[0].o = cross_first(L[0].wo, L[0].cwo)
    pack_rest()
    ff_first(0)
    arrived(R.gx, gx_sem)
    R.g1[...] = R.gst[...] + R.gx[0] + R.gx[1] + R.gx[2]
    gy_sem = new()
    R.gyr[2 * y + k] = R.g1[...]
    for j in range(1, 8):
        put(R.g1, R.gyr.at[2 * y + k], dev(x, z, plus(y, j // 2), flip(j)), gy_sem)
    qk_second(0)
    v_second(0)
    W[0].o = cross_second(L[0].cwo, L[0].wout, W[0].o)
    arrived(R.gyr.at[0:7], gy_sem)
    for i in range(2):
        R.gz[z, i] = R.gyr[4 * i] + R.gyr[4 * i + 1] + R.gyr[4 * i + 2] + R.gyr[4 * i + 3]
    gz_sem = to_z(R.gz.at[z], R.gz.at[z])
    spread_rest(R.hin, in_sems)
    normed, _ = normalize(full(R.hin).astype(F32))
    for i in streams:
        S[0].h[i] = R.hin[i, t]
    gate_start(0)
    arrived(R.gz.at[0:3], gz_sem)
    R.gains[...] = jnp.concatenate([R.gz[i // 2, i % 2] for i in range(8)], axis=1)
    S[0].a[...] = (normed * gain_row(0)).astype(BF).reshape(2, 8, 16, 1024)
    W[0].o = cross_third(L[0].wout, W[0].o)
    W[0].d = cross_second(L[0].cwd, L[0].wdn, W[0].d)
    cot_sems = []

    def after_keys_0():
        ring_relay(W[0].gate)
        up_start(0)
        down_start(0)

    def after_att_0():
        att_first(1)
        ff_first(1)

    def in_gather_0():
        ring_relay(W[0].up)
        ring_relay(W[0].d)

    def in_ff_0():
        qk_second(1)
        v_second(1)

    def after_ff_0():
        W[1].o = cross_second(L[1].cwo, L[1].wout, W[1].o)
        gate_start(1)
        W[1].d = cross_second(L[1].cwd, L[1].wdn, W[1].d)

    def in_gather_1():
        W[1].o = cross_third(L[1].wout, W[1].o)

    def after_keys_1():
        ring_relay(W[1].gate)
        up_start(1)
        down_start(1)

    def after_att_1():
        cot_sems.append(spread_tokens(R.cot, S[3].gb))

    def in_gather_2():
        ring_relay(W[1].up)
        ring_relay(W[1].d)

    def take_cotangent():
        spread_rest(S[3].gb, cot_sems[0])
        for i in streams:
            S[3].gr[i] = S[3].gb[i, t]

    landed = SimpleNamespace(out=new(), ing=new())

    def finish_outputs():
        for i in streams:
            rows = (S[3].h[i].astype(F32) + rs_end(3, i)).astype(BF)
            to_owners(i, rows, R.outst, R.outrv, landed.out)

    none = (None, None)
    attention_forward(0, none, after_keys_0, after_att_0)
    feedforward_forward(0, next_rows(0, in_gather_0), in_ff_0, after_ff_0)
    attention_forward(1, next_rows(1, in_gather_1), after_keys_1, after_att_1)
    feedforward_forward(1, next_rows(2, in_gather_2), nothing, take_cotangent)

    def ff_grads(l):
        gu_grad_second(l)
        down_second(l)

    def att_grads():
        out_second(1)
        q_second(1)
        k_second(1)
        v_grad_second(1)

    def last_grads():
        out_second(0)
        q_second(0)
        ff_grads(0)

    def after_grads_1():
        att_grads()
        gu_end(1)

    def after_grads_0():
        last_grads()
        att_end(1)

    feedforward_backward(1, none, finish_outputs)
    states = hand_back(3, lambda: ff_push(1))
    attention_backward(1, states, lambda: ff_grads(1))
    states = hand_back(2, lambda: down_third(1))
    feedforward_backward(0, states, after_grads_1)
    states = hand_back(1, lambda: ff_push(0))
    out_third(1)
    attention_backward(0, states, after_grads_0)
    for i in streams:
        to_owners(i, norm_backward(0, i), R.ingst, R.ingrv, landed.ing)
    gg_sem = new()
    for j in (1, 3, 2):
        put(R.gg, R.ggx.at[j - 1], dev(plus(x, j), z, y, k), gg_sem)
    k_second(0)
    v_grad_second(0)
    out_third(0)
    down_third(0)
    arrived(R.ggx, gg_sem)
    gg = R.gg[...] + R.ggx[0] + R.ggx[1] + R.ggx[2]
    for i in range(4):
        R.ggz[i] = gg[:, 256 * i : 256 * i + 256]
    gg_sem = new()
    for j in (1, 3, 2):
        zd = plus(z, j)
        put(R.ggz.at[zd], R.ggzr.at[j - 1], dev(x, zd, y, k), gg_sem)
    out_end(1)
    down_end(1)
    gu_end(0)
    arrived(R.outrv, landed.out)
    R.out[...] = R.outrv[...].reshape(2, 1, 64, 256)
    arrived(R.ggzr, gg_sem)
    gg = R.ggz[z] + R.ggzr[0] + R.ggzr[1] + R.ggzr[2]
    R.ggy[0] = gg[:, 0:128]
    R.ggy[1] = gg[:, 128:256]
    gg_sem = new()
    R.ggyr[0] = R.ggy[s]
    for j in range(1, 8):
        yd = plus(y, j // 2)
        put(R.ggy.at[lax.div(yd, 2)], R.ggyr.at[j], dev(x, z, yd, flip(j)), gg_sem)
    arrived(R.ingrv, landed.ing)
    R.ing[...] = R.ingrv[...].reshape(2, 1, 64, 256)
    att_end(0)
    out_end(0)
    down_end(0)
    arrived(R.ggyr.at[1:8], gg_sem)
    gg = R.ggyr[0]
    for j in range(1, 8):
        gg = gg + R.ggyr[j]
    gg = jnp.sum(jnp.where(lax.broadcasted_iota(I32, (8, 128), 0) == x, gg, 0.0), axis=0, keepdims=True)
    part = lax.rem(c, 4)
    gain = jnp.zeros((1, 32), F32)
    for i in range(4):
        gain += jnp.where(part == i, gg[:, 32 * i : 32 * i + 32], 0.0)
    R.ogg[...] = gain
    for mine, copy in pending:
        if mine is None:
            copy.wait_send()
        else:

            @pl.when(jnp.logical_not(mine))
            def _(copy=copy):
                copy.wait_send()

    assert used[0] <= N_SEM, used


def call(*args):
    whole = pl.BlockSpec(memory_space=pltpu.VMEM)
    arguments, results, scratch = (specs_of(group) for group in groups())
    return pl.pallas_call(
        kernel,
        out_shape=[jax.ShapeDtypeStruct(shape, dtype) for shape, dtype in results],
        in_specs=[whole] * len(arguments),
        out_specs=[whole] * len(results),
        scratch_shapes=[pltpu.VMEM(shape, dtype) for shape, dtype in scratch]
        + [pltpu.SemaphoreType.DMA((N_SEM,))],
        compiler_params=pltpu.CompilerParams(
            collective_id=0, has_side_effects=True, vmem_limit_bytes=62 * 1024 * 1024
        ),
    )(*args)


def hand_out(*refs):
    n = len(refs) // 2
    copies = [pltpu.make_async_copy(refs[i], refs[n + i], refs[-1].at[i]) for i in range(n)]
    for copy in copies:
        copy.start()
    for copy in copies:
        copy.wait()


def body(inputs, cotangent, segment_ids, gains, *weights):
    first = (inputs.reshape(2, 4, 16, 1024), cotangent.reshape(2, 4, 16, 1024), segment_ids, gains)
    results = call(*first, *weights)
    anywhere = pl.BlockSpec(memory_space=pl.ANY)
    return tuple(
        pl.pallas_call(
            hand_out,
            out_shape=[jax.ShapeDtypeStruct(r.shape, r.dtype) for r in results],
            in_specs=[pl.BlockSpec(memory_space=pltpu.VMEM)] * len(results),
            out_specs=[anywhere] * len(results),
            scratch_shapes=[pltpu.SemaphoreType.DMA((len(results),))],
        )(*results)
    )


def solution(mesh):
    tokens = P(None, None, "ctx", None)
    weight = P("ctx", "section")
    return jax.shard_map(
        body,
        mesh=mesh,
        in_specs=(tokens, tokens, P(), P("section", "ctx")) + (weight,) * 14,
        out_specs=(P(None, None, "ctx", "section"),) * 2 + (P("section", "ctx"),) + (weight,) * 14,
        check_vma=False,
    )
```

```python
from types import SimpleNamespace

import jax
import jax.numpy as jnp
from jax import lax
from jax.experimental import pallas as pl
from jax.experimental.pallas import tpu as pltpu
from jax.sharding import PartitionSpec as P

MESH = pl.DeviceIdType.MESH
BF = jnp.bfloat16
F32 = jnp.float32
I32 = jnp.int32
EPS = 1e-06
MASKED = -1e30


def spec(dtype, *shape):
    return shape, dtype


FAR_IN = dict(xin=spec(BF, 2, 4, 16, 1024), cot=spec(BF, 2, 4, 16, 1024))
NEAR_IN = dict(seg=spec(I32, 2, 1, 2048), gains_in=spec(BF, 1, 32))
FAR_LAYER_IN = dict(
    wq=spec(BF, 32, 256),
    wk=spec(BF, 32, 256),
    wv=spec(BF, 32, 256),
    wo=spec(BF, 32, 256),
    wg=spec(BF, 32, 704),
    wu=spec(BF, 32, 704),
)
NEAR_LAYER_IN = dict(wd=spec(BF, 88, 256))
FAR_OUT = dict(out=spec(BF, 2, 1, 64, 256), ing=spec(BF, 2, 1, 64, 256))
NEAR_OUT = dict(ogg=spec(F32, 1, 32))
FAR_LAYER_OUT = dict(
    oq=spec(F32, 32, 256),
    ok=spec(F32, 32, 256),
    ov=spec(F32, 32, 256),
    oo=spec(F32, 32, 256),
    og=spec(F32, 32, 704),
    ou=spec(F32, 32, 704),
    od=spec(F32, 88, 256),
)
COMMON = dict(
    hin=spec(BF, 2, 8, 16, 1024),
    pick=spec(BF, 704, 768),
    gst=spec(F32, 8, 128),
    gx=spec(F32, 3, 8, 128),
    g1=spec(F32, 8, 128),
    gyr=spec(F32, 8, 8, 128),
    gz=spec(F32, 4, 2, 8, 128),
    gains=spec(F32, 8, 1024),
    gg=spec(F32, 8, 1024),
    ggx=spec(F32, 3, 8, 1024),
    ggz=spec(F32, 4, 8, 256),
    ggzr=spec(F32, 3, 8, 256),
    ggy=spec(F32, 2, 8, 128),
    ggyr=spec(F32, 8, 8, 128),
    scores=spec(F32, 16, 128, 512),
    outst=spec(BF, 2, 4, 16, 256),
    ingst=spec(BF, 2, 4, 16, 256),
    outrv=spec(BF, 2, 64, 256),
    ingrv=spec(BF, 2, 64, 256),
    dmh=spec(BF, 256, 128),
    ds=spec(BF, 4, 512, 512),
    do2=spec(BF, 512, 128),
    dgu=spec(BF, 2, 128, 768),
)
LAYER = dict(
    qkst=spec(BF, 2, 32, 256),
    vst=spec(BF, 2, 32, 128),
    gus=spec(BF, 2, 32, 768),
    wds=spec(BF, 96, 256),
    cwo=spec(BF, 32, 256),
    cwd=spec(BF, 96, 256),
    wqk=spec(BF, 4, 8, 32, 256),
    wval=spec(BF, 4, 4, 2, 32, 128),
    wout=spec(BF, 4, 4, 32, 256),
    wgu=spec(BF, 4, 4, 2, 32, 768),
    wdn=spec(BF, 4, 4, 96, 256),
    kv=spec(BF, 4, 2, 2, 128, 256),
    q2=spec(BF, 512, 128),
    prob=spec(BF, 16, 128, 512),
    ot=spec(F32, 128, 256),
    gu=spec(F32, 256, 768),
    hid=spec(BF, 256, 384),
    dkv=spec(BF, 4, 2, 256, 256),
    dkvab=spec(BF, 2, 2, 256, 256),
    dkvc=spec(BF, 256, 256),
    dkvds=spec(BF, 256, 256),
    dkvd=spec(BF, 256, 256),
    dkves=spec(BF, 256, 256),
    dkve=spec(BF, 256, 256),
    gwq=spec(BF, 4, 8, 32, 128),
    gwk=spec(BF, 4, 8, 32, 128),
    gwv=spec(BF, 4, 4, 2, 32, 128),
    gwout=spec(BF, 4, 4, 32, 256),
    gwgu=spec(BF, 4, 4, 2, 32, 768),
    gwdn=spec(BF, 4, 4, 96, 256),
    rzq=spec(BF, 3, 8, 32, 128),
    rzk=spec(BF, 3, 8, 32, 128),
    ryv=spec(BF, 3, 4, 2, 32, 128),
    rzout=spec(BF, 3, 4, 32, 256),
    hygu=spec(BF, 2, 2, 2, 32, 768),
    bygu=spec(BF, 2, 4, 2, 32, 768),
    hzdn=spec(BF, 2, 2, 96, 256),
    bzdn=spec(BF, 2, 4, 96, 256),
    share=spec(F32, 8, 512),
    sq=spec(BF, 8, 32, 128),
    sk=spec(BF, 8, 32, 128),
    sv=spec(BF, 4, 2, 32, 128),
    sout=spec(BF, 4, 32, 256),
    sgu=spec(BF, 4, 2, 32, 768),
    sdn=spec(BF, 4, 96, 256),
    fq=spec(BF, 8, 32, 128),
    fk=spec(BF, 8, 32, 128),
    fv=spec(BF, 8, 32, 128),
    fgu=spec(BF, 8, 32, 768),
    yout=spec(BF, 4, 32, 256),
    ydn=spec(BF, 4, 96, 256),
    cout=spec(BF, 32, 256),
    cdn=spec(BF, 96, 256),
    fout=spec(BF, 32, 256),
    fdn=spec(BF, 96, 256),
)
SUB = dict(
    a=spec(BF, 2, 8, 16, 1024),
    h=spec(BF, 2, 16, 1024),
    gr=spec(BF, 2, 16, 1024),
    gb=spec(BF, 2, 8, 16, 1024),
)
EXCHANGE = dict(
    pb=spec(BF, 2, 2, 4, 16, 1024),
    sib=spec(BF, 2, 4, 16, 1024),
    xs=spec(BF, 2, 3, 16, 1024),
    xr=spec(BF, 2, 3, 16, 1024),
)
N_SEM = 282
N_LAYERS, N_SUB, N_EXCHANGE = 2, 4, 8


def groups():
    arguments = [(4, 0, FAR_IN), (0, 0, NEAR_IN)]
    results = [(4, 0, FAR_OUT), (0, 0, NEAR_OUT)]
    scratch = [(0, 0, COMMON), (0, 0, FAR_IN), (0, 0, FAR_OUT)]
    for l in range(N_LAYERS):
        arguments += [(5, l, FAR_LAYER_IN), (1, l, NEAR_LAYER_IN)]
        results += [(5, l, FAR_LAYER_OUT)]
        scratch += [(1, l, LAYER), (1, l, FAR_LAYER_IN), (1, l, FAR_LAYER_OUT)]
    scratch += [(2, i, SUB) for i in range(N_SUB)] + [(3, n, EXCHANGE) for n in range(N_EXCHANGE)]
    return arguments, results, scratch


def named(refs):
    spaces = [[SimpleNamespace() for _ in range(n)] for n in (1, N_LAYERS, N_SUB, N_EXCHANGE, 1, N_LAYERS)]
    left = list(refs)
    for group in groups():
        for kind, index, specs in group:
            for name in specs:
                setattr(spaces[kind][index], name, left.pop(0))
    return spaces[0][0], spaces[1], spaces[2], spaces[3], spaces[4][0], spaces[5]


def specs_of(group):
    return [entry for _, _, specs in group for entry in specs.values()]


def blocks_of(group):
    spaces = [pl.ANY if kind >= 4 else pltpu.VMEM for kind, _, specs in group for _ in specs]
    return [pl.BlockSpec(memory_space=space) for space in spaces]


def nn(a, b):
    return lax.dot_general(a, b, (((1,), (0,)), ((), ())), preferred_element_type=F32)


def nt(a, b):
    return lax.dot_general(a, b, (((1,), (1,)), ((), ())), preferred_element_type=F32)


def tn(a, b):
    return lax.dot_general(a, b, (((0,), (0,)), ((), ())), preferred_element_type=F32)


def normalize(h):
    inverse = lax.rsqrt(jnp.mean(h * h, axis=-1, keepdims=True) + EPS)
    return h * inverse, inverse


def kernel(*refs):
    R, L, S, X, far_r, far_l = named(refs[:-1])
    sems = refs[-1]
    used = [0]
    pending, kept = [], []
    outgoing = []

    def new():
        used[0] += 1
        return sems.at[used[0] - 1]

    x = lax.axis_index("section")
    c = lax.axis_index("ctx")
    z, y, k = lax.div(c, 8), lax.rem(lax.div(c, 2), 4), lax.rem(c, 2)
    t = 2 * x + k
    s = lax.div(y, 2)
    yy = lax.rem(y, 2)
    other = 1 - k

    def plus(v, j):
        return lax.rem(v + j, 4)

    def dev(xd, zd, yd, kd):
        return {"section": xd, "ctx": zd * 8 + yd * 2 + kd}

    def flip(j):
        return k if j % 2 == 0 else other

    sibling = dev(x, z, y, other)

    def put(src, dst, to, rsem):
        if len(pending) % 32 == 0:
            outgoing.append(new())
        copy = pltpu.make_async_remote_copy(
            src_ref=src, dst_ref=dst, send_sem=outgoing[-1], recv_sem=rsem, device_id=to, device_id_type=MESH
        )
        copy.start()
        pending.append(copy)

    def put_or_keep(mine, src, dst, to, rsem):
        copy = pltpu.make_async_remote_copy(
            src_ref=src, dst_ref=dst, send_sem=new(), recv_sem=rsem, device_id=to, device_id_type=MESH
        )

        @pl.when(mine)
        def _():
            pltpu.make_async_copy(src, dst, rsem).start()

        @pl.when(jnp.logical_not(mine))
        def _():
            copy.start()

        kept.append((mine, copy))

    def arrived(ref, sem):
        pltpu.make_async_copy(ref, ref, sem).wait()

    barrier = pltpu.get_barrier_semaphore()

    def greet(d):
        pl.semaphore_signal(barrier, inc=1, device_id=d, device_id_type=MESH)

    count = 0
    for j in range(4):
        for i in range(2):
            if (j, i) != (0, 0):
                greet(dev(plus(x, j), z, y, flip(i)))
                count += 1
            if j:
                greet(dev(x, z, plus(y, j), flip(i)))
                greet(dev(x, plus(z, j), y, flip(i)))
                count += 2
            greet(dev(plus(x, j), 3 - z, 3 - y, flip(i)))
            count += 1
    crossing = jnp.where(x == z, 0, 1)

    @pl.when(x != z)
    def _():
        greet(dev(z, x, y, k))

    def fetch(src, dst):
        copy = pltpu.make_async_copy(src, dst, new())
        copy.start()
        return copy

    def fetch_att(l):
        ends = ((far_l[l].wq, L[l].wq), (far_l[l].wk, L[l].wk), (far_l[l].wv, L[l].wv), (far_l[l].wo, L[l].wo))
        return [fetch(src, dst) for src, dst in ends]

    def wait_for(copies):
        for copy in copies:
            copy.wait()

    coming = fetch_att(0)
    xin_coming = fetch(far_r.xin, R.xin)
    later = fetch_att(1) + [fetch(far_r.cot, R.cot)]
    for l in range(2):
        later += [fetch(far_l[l].wg, L[l].wg), fetch(far_l[l].wu, L[l].wu)]
    leaving = []

    def leave(src, dst):
        leaving.append(fetch(src, dst))

    def pack_att(l):
        for i in range(2):
            L[l].qkst[i, :, 0:128] = L[l].wq[:, 128 * i : 128 * i + 128]
            L[l].qkst[i, :, 128:256] = L[l].wk[:, 128 * i : 128 * i + 128]
            L[l].vst[i] = L[l].wv[:, 128 * i : 128 * i + 128]

    def pack_rest():
        lane = lax.broadcasted_iota(I32, (1, 768), 1)
        half = (lane >= 384).astype(I32)
        place = lane - 384 * half
        group = (place >= 96).astype(I32) + (place >= 192).astype(I32) + (place >= 288).astype(I32)
        place = place - 96 * group
        unit = jnp.where(place < 88, 352 * half + 88 * group + place, -1)
        R.pick[...] = (lax.broadcasted_iota(I32, (704, 768), 0) == unit).astype(F32).astype(BF)
        stacked = jnp.concatenate([w[...] for l in range(2) for w in (L[l].wg, L[l].wu)], axis=0)
        stacked = nn(stacked, R.pick[...]).astype(BF)
        for l in range(2):
            for i in range(2):
                for n in range(2):
                    rows = stacked[64 * l + 32 * n : 64 * l + 32 * n + 32, 384 * i : 384 * i + 384]
                    L[l].gus[i, :, 384 * n : 384 * n + 384] = rows
            L[l].wds[0:88, :] = L[l].wd[...]
            L[l].wds[88:96, :] = jnp.zeros((8, 256), BF)
        pack_att(1)
        R.gg[...] = jnp.zeros((8, 1024), F32)

    wait_for(coming)
    pack_att(0)
    column = lax.broadcasted_iota(I32, (32, 128), 1) - 32 * lax.rem(c, 4)
    spot = (lax.broadcasted_iota(I32, (32, 128), 0) == column).astype(F32).astype(BF)
    piece = nn(jnp.broadcast_to(R.gains_in[...].astype(F32), (8, 32)).astype(BF), spot)
    R.gst[...] = jnp.where(lax.broadcasted_iota(I32, (8, 128), 0) == x, piece, 0.0)
    pl.semaphore_wait(barrier, count + crossing)

    W = [SimpleNamespace(), SimpleNamespace()]
    G = [SimpleNamespace(), SimpleNamespace()]
    partner = dev(x, z, y + 1 - 2 * yy, k)
    mate = 1 - yy
    slot_m = 2 * yy + k

    def keep(src, dst, sem):
        pltpu.make_async_copy(src, dst, sem).start()

    def to_z(src, dst, js=(1, 3, 2)):
        sem = new()
        for j in js:
            put(src, dst, dev(x, plus(z, j), y, k), sem)
        return sem

    def to_y(src, dst, js=(1, 3, 2)):
        sem = new()
        for j in js:
            put(src, dst, dev(x, z, plus(y, j), k), sem)
        return sem

    def qk_first(l):
        src, dst = L[l].qkst, L[l].wqk.at[z, 2 * y + k]
        sem = W[l].qk = new()
        keep(src.at[k], dst, sem)
        for j in (2, 6, 4, 3, 7, 5, 1):
            put(src.at[flip(j)], dst, dev(x, z, plus(y, j // 2), flip(j)), sem)

    def qk_second(l):
        w = L[l].wqk
        arrived(w.at[z], W[l].qk)
        W[l].qk = to_z(w.at[z], w.at[z])

    def z_first(src, w):
        sem, dst = new(), w.at[z, y, k]
        keep(src.at[k], dst, sem)
        for j in (2, 6, 4, 3, 7, 5, 1):
            put(src.at[flip(j)], dst, dev(x, plus(z, j // 2), y, flip(j)), sem)
        return sem

    def v_second(l):
        w = L[l].wval
        arrived(w.at[:, y], W[l].v)
        W[l].v = to_y(w.at[:, y], w.at[:, y])

    def at_y(j):
        return dev(x, z, plus(y, j), k)

    def at_z(j):
        return dev(x, plus(z, j), y, k)

    def ring_start(block, v, at):
        sems_ = [new() for _ in range(4)]
        put(block(v), block(v), at(1), sems_[0])
        put(block(v), block(v), at(3), sems_[1])
        return block, v, at, sems_

    def ring_relay(state):
        block, v, at, sems_ = state
        before, after = plus(v, 3), plus(v, 1)
        arrived(block(before), sems_[0])
        put(block(before, 0), block(before, 0), at(1), sems_[2])
        arrived(block(after), sems_[1])
        put(block(after, 1), block(after, 1), at(3), sems_[3])

    def ring_end(state):
        block, v, at, sems_ = state
        far = plus(v, 2)
        arrived(block(far, 0), sems_[2])
        arrived(block(far, 1), sems_[3])

    def halved(h):
        return slice(None) if h is None else slice(2 * h, 2 * h + 2)

    def gate_start(l):
        arrived(L[l].wgu.at[:, y], W[l].gu)
        W[l].gate = ring_start(lambda v, h=None: L[l].wgu.at[halved(h), v, :, :, 0:384], y, at_y)

    def up_start(l):
        W[l].up = ring_start(lambda v, h=None: L[l].wgu.at[halved(h), v, :, :, 384:768], y, at_y)

    def down_start(l):
        arrived(L[l].wdn.at[z], W[l].d)
        W[l].d = ring_start(lambda v, h=None: L[l].wdn.at[v, halved(h)], z, at_z)

    def cross_first(src, dst):
        sem = new()
        put_or_keep(x == z, src, dst, dev(z, x, y, k), sem)
        return sem

    def cross_second(src, w, sem):
        arrived(src, sem)
        sem, dst = new(), w.at[z, slot_m]
        put_or_keep(s == k, src, dst, dev(x, z, y, s), sem)
        for j in (1, 3, 2):
            put(src, dst, dev(x, z, plus(y, j), s), sem)
        return sem

    def cross_third(w, sem):
        arrived(w.at[z], sem)
        return to_z(w.at[z], w.at[z])

    streams = (0, 1)
    sums = {}

    def rs_start(n, i, part):
        pb, sib = X[n].pb, X[n].sib
        for r in range(8):
            pb[i, r % 2, r // 2] = part[16 * r : 16 * r + 16].astype(BF)
        sem = sums[n, i] = new()
        for j in (1, 3, 2, 0):
            xd = plus(x, j)
            put(pb.at[i, other, xd], sib.at[i, xd], sibling, sem)

    def rs_mid(n, i):
        pb, sib, xs, xr = X[n].pb, X[n].sib, X[n].xs, X[n].xr
        arrived(sib.at[i], sums[n, i])
        sem = sums[n, i] = new()
        for j in (1, 3, 2):
            xd = plus(x, j)
            xs[i, j - 1] = (pb[i, k, xd].astype(F32) + sib[i, xd].astype(F32)).astype(BF)
            put(xs.at[i, j - 1], xr.at[i, j - 1], dev(xd, z, y, k), sem)

    def rs_end(n, i):
        pb, sib, xr = X[n].pb, X[n].sib, X[n].xr
        total = pb[i, k, x].astype(F32) + sib[i, x].astype(F32)
        arrived(xr.at[i], sums[n, i])
        for j in (1, 3, 2):
            total += xr[i, j - 1].astype(F32)
        return total

    def gather_start(buf, i, block):
        buf[i, t] = block
        mine = buf.at[i, t]
        rx = {j: new() for j in (1, 3, 2)}
        rk = new()
        for j in (1, 3, 2):
            put(mine, mine, dev(plus(x, j), z, y, k), rx[j])
        put(mine, mine, sibling, rk)
        return buf, i, rx, rk

    def gather_forward(state):
        if state is not None:
            buf, i, rx, rk = state
            for j in (1, 3, 2):
                slot = buf.at[i, 2 * plus(x, 4 - j) + k]
                arrived(slot, rx[j])
                put(slot, slot, sibling, rk)

    def gather_finish(state):
        if state is not None:
            buf, i, rx, rk = state
            arrived(buf.at[i, 0:4], rk)

    def nothing():
        pass

    def opened(states, n, work, early=nothing):
        gather_finish(states[0])
        work(0)
        gather_forward(states[1])
        rs_mid(n, 0)
        early()
        gather_finish(states[1])
        work(1)
        rs_mid(n, 1)

    def closed(rows_of, buf, between):
        first = gather_start(buf, 0, rows_of(0))
        second = gather_start(buf, 1, rows_of(1))
        between()
        gather_forward(first)
        return first, second

    def to_owners(i, rows, stage, landing, sem):
        for r in range(4):
            stage[i, r] = rows[:, 256 * r : 256 * r + 256]
        zd, yd = (z, y) if i == 0 else (3 - z, 3 - y)
        kd = lax.div(x, 2)
        first_row = pl.multiple_of(16 * (2 * lax.rem(x, 2) + k), 16)
        dst = landing.at[s, pl.ds(first_row, 16)]
        for j in range(4):
            xd = plus(x, j)
            if i == 0 and j == 0:
                put_or_keep(kd == k, stage.at[i, xd], dst, dev(xd, zd, yd, kd), sem)
            else:
                put(stage.at[i, xd], dst, dev(xd, zd, yd, kd), sem)

    def spread_tokens(src, dst):
        rows = pl.ds(4 * k, 4)
        close, mirrored = new(), new()
        put(src.at[1 - s], dst.at[1, rows], dev(x, 3 - z, 3 - y, k), mirrored)
        put(src.at[s], dst.at[0, rows], sibling, close)
        dst[0, rows] = src[s]
        return close, mirrored

    def spread_rest(dst, sems_):
        close, mirrored = sems_
        far = dst.at[1, pl.ds(4 * k, 4)]
        arrived(far, mirrored)
        put(far, far, sibling, close)
        arrived(dst.at[0], close)

    lane = lax.broadcasted_iota(I32, (1, 512), 1)
    own_block = 4 * z + y
    query_pos = 128 * jnp.where(lane < 256, own_block, 15 - own_block) + lax.rem(lane, 128)
    ids = R.seg[s]

    def tokens_to(n):
        return jnp.sum(jnp.where(ids <= n, 1.0, 0.0), axis=1, keepdims=True).astype(I32)

    first, second = tokens_to(0), tokens_to(1)
    query_start = jnp.where(query_pos < first, 0, jnp.where(query_pos < second, first, second))
    head_lane = lax.broadcasted_iota(I32, (128, 128), 1) < 64

    def two_heads(v):
        zero = jnp.zeros_like(v)
        return jnp.concatenate([jnp.where(head_lane, v, zero), jnp.where(head_lane, zero, v)], axis=0)

    def own_heads(vt):
        return jnp.concatenate([vt[0:64, 0:128], vt[64:128, 128:256]], axis=0)

    def gain_row(i):
        return R.gains[i : i + 1, :]

    def full(ref):
        return ref[...].reshape(256, 1024)

    def keys_of(l, zz):
        return L[l].kv[zz, :, :, :, 0:128].reshape(512, 128)

    def values_of(l, zz):
        return L[l].kv[zz, :, :, :, 128:256].reshape(512, 128)

    def attention_forward(l, states, hook, late):
        kv = L[l].kv
        direct, relayed = ([{j: new() for j in (1, 2, 3)} for _ in streams] for _ in range(2))
        from_mate = [new() for _ in streams]
        for i in streams:
            if i == 1:
                gather_forward(states[1])
            gather_finish(states[i])
            a = S[2 * l].a[i].reshape(128, 1024)
            w = L[l].wqk
            if i == 0:
                arrived(w.at[0:3], W[l].qk)
            qk = nn(a, w[...].reshape(1024, 256))
            w = L[l].wval
            if i == 0:
                arrived(w.at[0:3], W[l].v)
            u = nn(a, w[...].reshape(1024, 128))
            if l == 0:
                values = u.astype(BF)
            else:
                values = (0.5 * u + 0.5 * L[0].kv[z, yy, i, :, 128:256].astype(F32)).astype(BF)
            kv[z, yy, i, :, 0:128] = qk[:, 128:256].astype(BF)
            kv[z, yy, i, :, 128:256] = values
            own = kv.at[z, yy, i]
            for j in (1, 3):
                put(own, own, dev(x, plus(z, j), y, k), direct[i][j])
            put(own, own, partner, from_mate[i])
            put(own, own, dev(x, plus(z, 2), y, k), direct[i][2])
            L[l].q2[256 * i : 256 * i + 256, :] = two_heads((qk[:, 0:128].astype(BF) * 0.125).astype(BF))
        for i in streams:
            near = kv.at[z, mate, i]
            arrived(near, from_mate[i])
            for j in (1, 3):
                put(near, near, dev(x, plus(z, j), y, k), relayed[i][j])
        scores = R.scores
        top = jnp.full((1, 512), MASKED, F32)
        for j in (0, 3, 1, 2):
            zz = plus(z, j)
            for i in streams:
                if j % 2:
                    arrived(kv.at[zz, yy, i], direct[i][4 - j])
                    arrived(kv.at[zz, mate, i], relayed[i][4 - j])
                elif j:
                    arrived(kv.at[zz, mate, i], relayed[i][2])
            if j == 1:
                hook()
            scores[4 * j : 4 * j + 4] = nt(keys_of(l, zz), L[l].q2[...]).reshape(4, 128, 512)

            def mask(i, top, j=j, zz=zz):
                block = 4 * zz + 2 * s + lax.div(i, 2)
                base = 128 * (block + lax.rem(i, 2) * (15 - 2 * block))
                row = lax.broadcasted_iota(I32, (128, 512), 0)
                seen = (row >= query_start - base) & (row <= query_pos - base)
                v = jnp.where(seen, scores[4 * j + i], MASKED)
                scores[4 * j + i] = v
                return jnp.maximum(top, jnp.max(v, axis=0, keepdims=True))

            top = lax.fori_loop(0, 4, mask, top)
            if j == 0:
                for i in streams:
                    opposite = kv.at[plus(z, 2), yy, i]
                    arrived(opposite, direct[i][2])
                    put(opposite, opposite, partner, relayed[i][2])
        prob = L[l].prob
        for i in streams:
            lanes = slice(256 * i, 256 * i + 256)
            high = top[:, lanes]

            def expo(r, total):
                v = jnp.exp(scores[r, :, lanes] - high)
                prob[r, :, lanes] = v.astype(BF)
                return total + jnp.sum(v, axis=0, keepdims=True)

            share = 1.0 / lax.fori_loop(0, 16, expo, jnp.zeros((1, 256), F32))
            L[l].share[0:1, lanes] = share
            ot = jnp.zeros((128, 256), F32)
            for j in range(4):
                ot += tn(values_of(l, plus(z, j)), prob[4 * j : 4 * j + 4, :, lanes].reshape(512, 256))
            ot = ot * share
            ot = own_heads(ot)
            L[l].ot[:, 128 * i : 128 * i + 128] = ot
            o = jnp.transpose(ot).astype(BF)
            if i == 0:
                arrived(L[l].wout.at[0:3], W[l].o)
            part = jnp.concatenate([nn(o, L[l].wout[r].reshape(128, 256)) for r in range(4)], axis=1)
            rs_start(2 * l, i, part)
        for i in streams:
            rs_mid(2 * l, i)
        late()

    def feedforward_forward(l, states, early, hook):
        w = L[l].wgu

        def work(i):
            a = S[2 * l + 1].a[i].reshape(128, 1024)
            if i == 0:
                ring_end(W[l].gate)
            gate = nn(a, w[:, :, :, :, 0:384].reshape(1024, 384))
            if i == 0:
                ring_end(W[l].up)
            up = nn(a, w[:, :, :, :, 384:768].reshape(1024, 384))
            rows = slice(128 * i, 128 * i + 128)
            L[l].gu[rows, 0:384] = gate
            L[l].gu[rows, 384:768] = up
            hidden = (gate * jax.nn.sigmoid(gate) * up).astype(BF)
            L[l].hid[rows, :] = hidden
            if i == 0:
                ring_end(W[l].d)
            part = jnp.concatenate([nn(hidden, L[l].wdn[r].reshape(384, 256)) for r in range(4)], axis=1)
            rs_start(2 * l + 1, i, part)

        opened(states, 2 * l + 1, work, early)
        hook()

    def next_rows(n, between=nothing):
        def rows_of(i):
            rows = (S[n].h[i].astype(F32) + rs_end(n, i)).astype(BF)
            S[n + 1].h[i] = rows
            normed, _ = normalize(rows.astype(F32))
            return (normed * gain_row(n + 1)).astype(BF)

        return closed(rows_of, S[n + 1].a, between)

    def norm_backward(n, i):
        da = rs_end(4 + n, i)
        normed, inverse = normalize(S[n].h[i].astype(F32))
        gain_part = jnp.sum(da * normed, axis=0, keepdims=True)
        if i == 0:
            R.gg[n : n + 1, :] = gain_part
        else:
            R.gg[n : n + 1, :] += gain_part
        scaled = da * gain_row(n)
        mixed = scaled - normed * jnp.mean(scaled * normed, axis=-1, keepdims=True)
        return (S[n].gr[i].astype(F32) + inverse * mixed).astype(BF)

    def hand_back(n, between=nothing):
        def rows_of(i):
            rows = norm_backward(n, i)
            S[n - 1].gr[i] = rows
            return rows

        return closed(rows_of, S[n - 1].gb, between)

    def send_z(g, landing):
        sem = new()
        for j in (1, 3, 2):
            zd = plus(z, j)
            put(g.at[zd], landing.at[j - 1], dev(x, zd, y, k), sem)
        return sem

    def send_y(g, landing):
        sem = new()
        for j in (1, 3, 2):
            yd = plus(y, j)
            put(g.at[:, yd], landing.at[j - 1], dev(x, z, yd, k), sem)
        return sem

    def attention_backward(l, states, hook):
        n = 2 * l
        wo, dkv, prob = L[l].wout, L[l].dkv, L[l].prob
        ab, own_ab, c_sem = {j: new() for j in (1, 3)}, {j: new() for j in (1, 3)}, new()
        dq = []
        for i in streams:
            if i == 1:
                gather_forward(states[1])
            gather_finish(states[i])
            gb = S[n].gb[i].reshape(128, 1024)
            dot_ = nt(wo[0].reshape(128, 256), gb[:, 0:256])
            for r in range(1, 4):
                dot_ += nt(wo[r].reshape(128, 256), gb[:, 256 * r : 256 * r + 256])
            dot_ = dot_.astype(BF).astype(F32)
            do2 = two_heads(jnp.transpose(dot_).astype(BF))
            share = L[l].share[0:1, 256 * i : 256 * i + 256]
            head_row = lax.broadcasted_iota(I32, (128, 128), 0) < 64
            scaled = dot_ * jnp.where(head_row, share[:, 0:128], share[:, 128:256])
            R.do2[256 * i : 256 * i + 256, :] = two_heads(jnp.transpose(scaled).astype(BF))
            prod = dot_ * L[l].ot[:, 128 * i : 128 * i + 128]
            delta = jnp.concatenate(
                [jnp.sum(prod[0:64], axis=0, keepdims=True), jnp.sum(prod[64:128], axis=0, keepdims=True)], axis=1
            )
            lanes = slice(256 * i, 256 * i + 256)
            dqt = jnp.zeros((128, 256), F32)
            for j in (2, 1, 3, 0):
                zz = plus(z, j)
                p = prob[4 * j : 4 * j + 4, :, lanes].reshape(512, 256)
                dp = nt(values_of(l, zz), do2)
                ds = (p.astype(F32) * ((dp - delta) * share)).astype(BF)
                R.ds[j, :, lanes] = ds
                if i == 1:
                    p = prob[4 * j : 4 * j + 4].reshape(512, 512)
                    dkv[zz, :, :, 0:128] = nn(R.ds[j], L[l].q2[...]).astype(BF).reshape(2, 256, 128)
                    dkv[zz, :, :, 128:256] = nn(p, R.do2[...]).astype(BF).reshape(2, 256, 128)
                    if j % 2:
                        put(dkv.at[zz, mate], L[l].dkvab.at[j // 2, mate], dev(x, zz, y, k), ab[j])
                    elif j:
                        put(dkv.at[zz, mate], L[l].dkvc, partner, c_sem)
                dqt += tn(keys_of(l, zz), ds)
                if i == 1 and j == 3:
                    for r in (1, 3):
                        put(dkv.at[plus(z, r), yy], L[l].dkvab.at[r // 2, yy], dev(x, plus(z, r), y, k), own_ab[r])
            dq.append(jnp.transpose(own_heads(dqt) * 0.125).astype(BF))
        dq = jnp.concatenate(dq, axis=0)
        gb = full(S[n].gb)
        arrived(L[l].dkvc, c_sem)
        far = plus(z, 2)
        L[l].dkvds[...] = (dkv[far, yy].astype(F32) + L[l].dkvc[...].astype(F32)).astype(BF)
        d_sem, e_sem = new(), new()
        put(L[l].dkvds, L[l].dkvd, dev(x, far, y, k), d_sem)
        got = L[l].dkvab
        arrived(got.at[0, mate], ab[1])
        arrived(got.at[1, mate], ab[3])
        L[l].dkves[...] = (dkv[z, mate].astype(F32) + got[0, mate].astype(F32) + got[1, mate].astype(F32)).astype(BF)
        put(L[l].dkves, L[l].dkve, partner, e_sem)
        gw = L[l].gwout
        otb = L[l].ot[...].astype(BF)
        for i in range(4):
            gw[i] = nn(otb, gb[:, 256 * i : 256 * i + 256]).astype(BF).reshape(4, 32, 256)
        at = jnp.transpose(full(S[n].a))
        L[l].gwq[...] = nn(at, dq).astype(BF).reshape(4, 8, 32, 128)
        arrived(got.at[0, yy], own_ab[1])
        arrived(got.at[1, yy], own_ab[3])
        tot = dkv[z, yy].astype(F32) + got[0, yy].astype(F32) + got[1, yy].astype(F32)
        arrived(L[l].dkvd, d_sem)
        arrived(L[l].dkve, e_sem)
        tot = tot + L[l].dkvd[...].astype(F32) + L[l].dkve[...].astype(F32)
        dk = tot[:, 0:128].astype(BF)
        dvals = tot[:, 128:256]
        if l == 1:
            half = 0.5 * dvals.astype(BF).astype(F32)
            du = half.astype(BF)
            R.dmh[...] = du
        else:
            du = (dvals + R.dmh[...].astype(F32)).astype(BF)
        def send_grads():
            grads = nn(at, jnp.concatenate([dk, du], axis=1)).astype(BF)
            L[l].gwk[...] = grads[:, 0:128].reshape(4, 8, 32, 128)
            L[l].gwv[...] = grads[:, 128:256].reshape(4, 4, 2, 32, 128)
            G[l].k = send_z(L[l].gwk, L[l].rzk)
            G[l].v = send_y(L[l].gwv, L[l].ryv)

        if l == 0:
            send_grads()
        for i in streams:
            rows = slice(128 * i, 128 * i + 128)
            da = nt(jnp.concatenate([dq[rows], dk[rows]], axis=1), L[l].wqk[...].reshape(1024, 256))
            da += nt(du[rows], L[l].wval[...].reshape(1024, 128))
            rs_start(4 + n, i, da)
        for i in streams:
            rs_mid(4 + n, i)
        if l == 1:
            send_grads()
        G[l].o = send_z(L[l].gwout, L[l].rzout)
        G[l].q = send_z(L[l].gwq, L[l].rzq)
        hook()

    def feedforward_backward(l, states, hook):
        n = 2 * l + 1

        def work(i):
            gb = S[n].gb[i].reshape(128, 1024)
            wd = L[l].wdn
            dhid = nt(gb[:, 0:256], wd[0].reshape(384, 256))
            for r in range(1, 4):
                dhid += nt(gb[:, 256 * r : 256 * r + 256], wd[r].reshape(384, 256))
            gu = L[l].gu[128 * i : 128 * i + 128, :]
            gate, up = gu[:, 0:384], gu[:, 384:768]
            sig = jax.nn.sigmoid(gate)
            dgate = dhid * up * sig * (1.0 + gate * (1.0 - sig))
            dup = dhid * (gate * sig)
            dgu = jnp.concatenate([dgate.astype(BF), dup.astype(BF)], axis=1)
            R.dgu[i] = dgu
            rs_start(4 + n, i, nt(dgu, L[l].wgu[...].reshape(1024, 768)))

        opened(states, 4 + n, work)
        at = jnp.transpose(full(S[n].a))
        gw = L[l].gwgu
        gw[...] = nn(at, R.dgu[...].reshape(256, 768)).astype(BF).reshape(4, 4, 2, 32, 768)
        far = plus(y, 2)
        G[l].g = [new() for _ in range(4)]
        put(gw.at[0:2, far], L[l].hygu.at[0], at_y(1), G[l].g[0])
        put(gw.at[2:4, far], L[l].hygu.at[1], at_y(3), G[l].g[1])
        gb = full(S[n].gb)
        ht = jnp.transpose(L[l].hid[...])
        gw = L[l].gwdn
        for i in range(4):
            gw[i] = nn(ht, gb[:, 256 * i : 256 * i + 256]).astype(BF).reshape(4, 96, 256)
        far = plus(z, 2)
        G[l].d = [new() for _ in range(4)]
        put(gw.at[far, 0:2], L[l].hzdn.at[0], at_z(1), G[l].d[0])
        put(gw.at[far, 2:4], L[l].hzdn.at[1], at_z(3), G[l].d[1])
        hook()

    def ff_push(l):
        gu, dn, hg, hd = L[l].gwgu, L[l].gwdn, L[l].hygu, L[l].hzdn
        for h, j in ((0, 1), (1, 3)):
            yd, zd, half = plus(y, j), plus(z, j), slice(2 * h, 2 * h + 2)
            arrived(hg.at[h], G[l].g[h])
            gu[half, yd] = (gu[half, yd].astype(F32) + hg[h].astype(F32)).astype(BF)
            put(gu.at[:, yd], L[l].bygu.at[h], at_y(j), G[l].g[2 + h])
            arrived(hd.at[h], G[l].d[h])
            dn[zd, half] = (dn[zd, half].astype(F32) + hd[h].astype(F32)).astype(BF)
            put(dn.at[zd], L[l].bzdn.at[h], at_z(j), G[l].d[2 + h])

    def summed(own, got):
        return own.astype(F32) + got[0].astype(F32) + got[1].astype(F32) + got[2].astype(F32)

    def rows_back(st, land):
        sem = new()
        for j in range(4):
            m = plus(slot_m, j)
            to = dev(x, z, 2 * k + lax.div(m, 2), lax.rem(m, 2))
            if j == 0:
                put_or_keep(s == k, st.at[m], land.at[y], to, sem)
            else:
                put(st.at[m], land.at[y], to, sem)
        return sem

    def four(land):
        return land[0].astype(F32) + land[1].astype(F32) + land[2].astype(F32) + land[3].astype(F32)

    def out_second(l):
        arrived(L[l].rzout, G[l].o)
        L[l].sout[...] = summed(L[l].gwout[z], L[l].rzout).astype(BF)
        G[l].o = rows_back(L[l].sout, L[l].yout)

    def out_third(l):
        arrived(L[l].yout, G[l].o)
        L[l].cout[...] = four(L[l].yout).astype(BF)
        G[l].o = cross_first(L[l].cout, L[l].fout)

    def out_end(l):
        arrived(L[l].fout, G[l].o)
        L[l].oo[...] = L[l].fout[...].astype(F32)
        leave(L[l].oo, far_l[l].oo)

    def down_second(l):
        got = L[l].bzdn
        arrived(got.at[0], G[l].d[2])
        arrived(got.at[1], G[l].d[3])
        L[l].sdn[...] = (L[l].gwdn[z].astype(F32) + got[0].astype(F32) + got[1].astype(F32)).astype(BF)
        G[l].d = rows_back(L[l].sdn, L[l].ydn)

    def down_third(l):
        arrived(L[l].ydn, G[l].d)
        L[l].cdn[...] = four(L[l].ydn).astype(BF)
        G[l].d = cross_first(L[l].cdn, L[l].fdn)

    def down_end(l):
        arrived(L[l].fdn, G[l].d)
        L[l].od[...] = L[l].fdn[0:88, :].astype(F32)
        leave(L[l].od, far_l[l].od)

    def rows_y(g, got, st, land, sem):
        arrived(got, sem)
        st[...] = summed(g[z], got).astype(BF)
        sem = new()
        land[0] = st[2 * y + k]
        for j in (2, 6, 4, 3, 7, 5, 1):
            yd, kd = plus(y, j // 2), flip(j)
            put(st.at[2 * yd + kd], land.at[j], dev(x, z, yd, kd), sem)
        return sem

    def rows_z(st, land):
        sem = new()
        land[0] = st[z, k]
        for j in (2, 6, 4, 3, 7, 5, 1):
            zd, kd = plus(z, j // 2), flip(j)
            put(st.at[zd, kd], land.at[j], dev(x, zd, y, kd), sem)
        return sem

    def halves(land, sem):
        arrived(land.at[1:8], sem)
        own = land[0].astype(F32) + land[2].astype(F32) + land[4].astype(F32) + land[6].astype(F32)
        far = land[1].astype(F32) + land[3].astype(F32) + land[5].astype(F32) + land[7].astype(F32)
        return jnp.where(k == 0, own, far), jnp.where(k == 0, far, own)

    def q_second(l):
        G[l].q = rows_y(L[l].gwq, L[l].rzq, L[l].sq, L[l].fq, G[l].q)

    def k_second(l):
        G[l].k = rows_y(L[l].gwk, L[l].rzk, L[l].sk, L[l].fk, G[l].k)

    def v_grad_second(l):
        g, got, st = L[l].gwv, L[l].ryv, L[l].sv
        arrived(got, G[l].v)
        for i in range(4):
            own = g[i, y].astype(F32) + got[0, i].astype(F32) + got[1, i].astype(F32) + got[2, i].astype(F32)
            st[i] = own.astype(BF)
        G[l].v = rows_z(st, L[l].fv)

    def gu_grad_second(l):
        g, got, st = L[l].gwgu, L[l].bygu, L[l].sgu
        arrived(got.at[0], G[l].g[2])
        arrived(got.at[1], G[l].g[3])
        for i in range(4):
            st[i] = (g[i, y].astype(F32) + got[0, i].astype(F32) + got[1, i].astype(F32)).astype(BF)
        G[l].g = rows_z(st, L[l].fgu)

    def att_end(l):
        f = far_l[l]
        for land, result, sem, to in (
            (L[l].fq, L[l].oq, G[l].q, f.oq),
            (L[l].fk, L[l].ok, G[l].k, f.ok),
            (L[l].fv, L[l].ov, G[l].v, f.ov),
        ):
            low, high = halves(land, sem)
            result[:, 0:128] = low
            result[:, 128:256] = high
            leave(result, to)

    def gu_end(l):
        low, high = halves(L[l].fgu, G[l].g)
        both = jnp.concatenate(
            [
                jnp.concatenate([low[:, 0:384], high[:, 0:384]], axis=1),
                jnp.concatenate([low[:, 384:768], high[:, 384:768]], axis=1),
            ],
            axis=0,
        )
        main = both.astype(BF)
        rest = (both - main.astype(F32)).astype(BF)
        both = nt(main, R.pick[...]) + nt(rest, R.pick[...])
        L[l].og[...] = both[0:32]
        L[l].ou[...] = both[32:64]
        leave(L[l].og, far_l[l].og)
        leave(L[l].ou, far_l[l].ou)

    def nothing():
        pass

    def att_first(l):
        qk_first(l)
        W[l].v = z_first(L[l].vst, L[l].wval)
        W[l].o = cross_first(L[l].wo, L[l].cwo)

    def ff_first(l):
        W[l].gu = z_first(L[l].gus, L[l].wgu)
        W[l].d = cross_first(L[l].wds, L[l].cwd)

    qk_first(0)
    W[0].v = z_first(L[0].vst, L[0].wval)
    xin_coming.wait()
    in_sems = spread_tokens(R.xin, R.hin)
    gx_sem = new()
    for j in (1, 3, 2):
        put(R.gst, R.gx.at[j - 1], dev(plus(x, j), z, y, k), gx_sem)
    W[0].o = cross_first(L[0].wo, L[0].cwo)
    wait_for(later)
    pack_rest()
    ff_first(0)
    arrived(R.gx, gx_sem)
    R.g1[...] = R.gst[...] + R.gx[0] + R.gx[1] + R.gx[2]
    gy_sem = new()
    R.gyr[2 * y + k] = R.g1[...]
    for j in range(1, 8):
        put(R.g1, R.gyr.at[2 * y + k], dev(x, z, plus(y, j // 2), flip(j)), gy_sem)
    qk_second(0)
    v_second(0)
    W[0].o = cross_second(L[0].cwo, L[0].wout, W[0].o)
    arrived(R.gyr.at[0:7], gy_sem)
    for i in range(2):
        R.gz[z, i] = R.gyr[4 * i] + R.gyr[4 * i + 1] + R.gyr[4 * i + 2] + R.gyr[4 * i + 3]
    gz_sem = to_z(R.gz.at[z], R.gz.at[z])
    spread_rest(R.hin, in_sems)
    normed, _ = normalize(full(R.hin).astype(F32))
    for i in streams:
        S[0].h[i] = R.hin[i, t]
    gate_start(0)
    arrived(R.gz.at[0:3], gz_sem)
    R.gains[...] = jnp.concatenate([R.gz[i // 2, i % 2] for i in range(8)], axis=1)
    S[0].a[...] = (normed * gain_row(0)).astype(BF).reshape(2, 8, 16, 1024)
    W[0].o = cross_third(L[0].wout, W[0].o)
    W[0].d = cross_second(L[0].cwd, L[0].wdn, W[0].d)
    cot_sems = []

    def after_keys_0():
        ring_relay(W[0].gate)
        up_start(0)
        down_start(0)

    def after_att_0():
        att_first(1)
        ff_first(1)

    def in_gather_0():
        ring_relay(W[0].up)
        ring_relay(W[0].d)

    def in_ff_0():
        qk_second(1)
        v_second(1)

    def after_ff_0():
        W[1].o = cross_second(L[1].cwo, L[1].wout, W[1].o)
        gate_start(1)
        W[1].d = cross_second(L[1].cwd, L[1].wdn, W[1].d)

    def in_gather_1():
        W[1].o = cross_third(L[1].wout, W[1].o)

    def after_keys_1():
        ring_relay(W[1].gate)
        up_start(1)
        down_start(1)

    def after_att_1():
        cot_sems.append(spread_tokens(R.cot, S[3].gb))

    def in_gather_2():
        ring_relay(W[1].up)
        ring_relay(W[1].d)

    def take_cotangent():
        spread_rest(S[3].gb, cot_sems[0])
        for i in streams:
            S[3].gr[i] = S[3].gb[i, t]

    landed = SimpleNamespace(out=new(), ing=new())

    def finish_outputs():
        for i in streams:
            rows = (S[3].h[i].astype(F32) + rs_end(3, i)).astype(BF)
            to_owners(i, rows, R.outst, R.outrv, landed.out)

    none = (None, None)
    attention_forward(0, none, after_keys_0, after_att_0)
    feedforward_forward(0, next_rows(0, in_gather_0), in_ff_0, after_ff_0)
    attention_forward(1, next_rows(1, in_gather_1), after_keys_1, after_att_1)
    feedforward_forward(1, next_rows(2, in_gather_2), nothing, take_cotangent)

    def ff_grads(l):
        gu_grad_second(l)
        down_second(l)

    def att_grads():
        out_second(1)
        q_second(1)
        k_second(1)
        v_grad_second(1)

    def last_grads():
        out_second(0)
        q_second(0)
        ff_grads(0)

    def after_grads_1():
        att_grads()
        gu_end(1)

    def after_grads_0():
        last_grads()
        att_end(1)

    feedforward_backward(1, none, finish_outputs)
    states = hand_back(3, lambda: ff_push(1))
    attention_backward(1, states, lambda: ff_grads(1))
    states = hand_back(2, lambda: down_third(1))
    feedforward_backward(0, states, after_grads_1)
    states = hand_back(1, lambda: ff_push(0))
    out_third(1)
    attention_backward(0, states, after_grads_0)
    for i in streams:
        to_owners(i, norm_backward(0, i), R.ingst, R.ingrv, landed.ing)
    gg_sem = new()
    for j in (1, 3, 2):
        put(R.gg, R.ggx.at[j - 1], dev(plus(x, j), z, y, k), gg_sem)
    k_second(0)
    v_grad_second(0)
    out_third(0)
    down_third(0)
    arrived(R.ggx, gg_sem)
    gg = R.gg[...] + R.ggx[0] + R.ggx[1] + R.ggx[2]
    for i in range(4):
        R.ggz[i] = gg[:, 256 * i : 256 * i + 256]
    gg_sem = new()
    for j in (1, 3, 2):
        zd = plus(z, j)
        put(R.ggz.at[zd], R.ggzr.at[j - 1], dev(x, zd, y, k), gg_sem)
    out_end(1)
    down_end(1)
    gu_end(0)
    arrived(R.outrv, landed.out)
    R.out[...] = R.outrv[...].reshape(2, 1, 64, 256)
    leave(R.out, far_r.out)
    arrived(R.ggzr, gg_sem)
    gg = R.ggz[z] + R.ggzr[0] + R.ggzr[1] + R.ggzr[2]
    R.ggy[0] = gg[:, 0:128]
    R.ggy[1] = gg[:, 128:256]
    gg_sem = new()
    R.ggyr[0] = R.ggy[s]
    for j in range(1, 8):
        yd = plus(y, j // 2)
        put(R.ggy.at[lax.div(yd, 2)], R.ggyr.at[j], dev(x, z, yd, flip(j)), gg_sem)
    arrived(R.ingrv, landed.ing)
    R.ing[...] = R.ingrv[...].reshape(2, 1, 64, 256)
    leave(R.ing, far_r.ing)
    att_end(0)
    out_end(0)
    down_end(0)
    arrived(R.ggyr.at[1:8], gg_sem)
    gg = R.ggyr[0]
    for j in range(1, 8):
        gg = gg + R.ggyr[j]
    gg = jnp.sum(jnp.where(lax.broadcasted_iota(I32, (8, 128), 0) == x, gg, 0.0), axis=0, keepdims=True)
    part = lax.rem(c, 4)
    gain = jnp.zeros((1, 32), F32)
    for i in range(4):
        gain += jnp.where(part == i, gg[:, 32 * i : 32 * i + 32], 0.0)
    R.ogg[...] = gain
    wait_for(leaving)
    for copy in pending:
        copy.wait_send()
    for mine, copy in kept:

        @pl.when(jnp.logical_not(mine))
        def _(copy=copy):
            copy.wait_send()

    assert used[0] <= N_SEM, used


def call(*args):
    arguments, results, scratch = groups()
    return pl.pallas_call(
        kernel,
        out_shape=[jax.ShapeDtypeStruct(shape, dtype) for shape, dtype in specs_of(results)],
        in_specs=blocks_of(arguments),
        out_specs=blocks_of(results),
        scratch_shapes=[pltpu.VMEM(shape, dtype) for shape, dtype in specs_of(scratch)]
        + [pltpu.SemaphoreType.DMA((N_SEM,))],
        compiler_params=pltpu.CompilerParams(
            collective_id=0, has_side_effects=True, vmem_limit_bytes=62 * 1024 * 1024
        ),
    )(*args)


def hand_out(*refs):
    n = len(refs) // 2
    copies = [pltpu.make_async_copy(refs[i], refs[n + i], refs[-1].at[i]) for i in range(n)]
    for copy in copies:
        copy.start()
    for copy in copies:
        copy.wait()


def body(inputs, cotangent, segment_ids, gains, *weights):
    first = (inputs.reshape(2, 4, 16, 1024), cotangent.reshape(2, 4, 16, 1024), segment_ids, gains)
    results = call(*first, *weights)
    anywhere = pl.BlockSpec(memory_space=pl.ANY)
    return tuple(
        pl.pallas_call(
            hand_out,
            out_shape=[jax.ShapeDtypeStruct(r.shape, r.dtype) for r in results],
            in_specs=[pl.BlockSpec(memory_space=pltpu.VMEM)] * len(results),
            out_specs=[anywhere] * len(results),
            scratch_shapes=[pltpu.SemaphoreType.DMA((len(results),))],
        )(*results)
    )


def solution(mesh):
    tokens = P(None, None, "ctx", None)
    weight = P("ctx", "section")
    return jax.shard_map(
        body,
        mesh=mesh,
        in_specs=(tokens, tokens, P(), P("section", "ctx")) + (weight,) * 14,
        out_specs=(P(None, None, "ctx", "section"),) * 2 + (P("section", "ctx"),) + (weight,) * 14,
        check_vma=False,
    )
```

```python
from types import SimpleNamespace

import jax
import jax.numpy as jnp
from jax import lax
from jax.experimental import pallas as pl
from jax.experimental.pallas import tpu as pltpu
from jax.sharding import PartitionSpec as P

MESH = pl.DeviceIdType.MESH
BF = jnp.bfloat16
F32 = jnp.float32
I32 = jnp.int32
EPS = 1e-06
MASKED = -1e30


def spec(dtype, *shape):
    return shape, dtype


FAR_IN = dict(xin=spec(BF, 2, 4, 16, 1024), cot=spec(BF, 2, 4, 16, 1024))
NEAR_IN = dict(seg=spec(I32, 2, 1, 2048), gains_in=spec(BF, 1, 32))
FAR_LAYER_IN = dict(
    wq=spec(BF, 32, 256),
    wk=spec(BF, 32, 256),
    wv=spec(BF, 32, 256),
    wo=spec(BF, 32, 256),
    wg=spec(BF, 32, 704),
    wu=spec(BF, 32, 704),
)
NEAR_LAYER_IN = dict(wd=spec(BF, 88, 256))
FAR_OUT = dict(out=spec(BF, 2, 1, 64, 256), ing=spec(BF, 2, 1, 64, 256))
NEAR_OUT = dict(ogg=spec(F32, 1, 32))
FAR_LAYER_OUT = dict(
    oq=spec(F32, 32, 256),
    ok=spec(F32, 32, 256),
    ov=spec(F32, 32, 256),
    oo=spec(F32, 32, 256),
    og=spec(F32, 32, 704),
    ou=spec(F32, 32, 704),
    od=spec(F32, 88, 256),
)
COMMON = dict(
    hin=spec(BF, 2, 8, 16, 1024),
    pick=spec(BF, 704, 768),
    gst=spec(F32, 8, 128),
    gx=spec(F32, 3, 8, 128),
    g1=spec(F32, 8, 128),
    gyr=spec(F32, 8, 8, 128),
    gz=spec(F32, 4, 2, 8, 128),
    gains=spec(F32, 8, 1024),
    normed=spec(F32, 256, 1024),
    gg=spec(F32, 8, 1024),
    ggx=spec(F32, 3, 8, 1024),
    ggz=spec(F32, 4, 8, 256),
    ggzr=spec(F32, 3, 8, 256),
    ggy=spec(F32, 2, 8, 128),
    ggyr=spec(F32, 8, 8, 128),
    scores=spec(F32, 16, 128, 512),
    outst=spec(BF, 2, 4, 16, 256),
    ingst=spec(BF, 2, 4, 16, 256),
    outrv=spec(BF, 2, 64, 256),
    ingrv=spec(BF, 2, 64, 256),
    dmh=spec(BF, 256, 128),
    ds=spec(BF, 4, 512, 512),
    do2=spec(BF, 512, 128),
    dgu=spec(BF, 2, 128, 768),
)
LAYER = dict(
    qkst=spec(BF, 2, 32, 256),
    vst=spec(BF, 2, 32, 128),
    gus=spec(BF, 2, 32, 768),
    wds=spec(BF, 96, 256),
    cwo=spec(BF, 32, 256),
    cwd=spec(BF, 96, 256),
    wqk=spec(BF, 4, 8, 32, 256),
    wval=spec(BF, 4, 4, 2, 32, 128),
    wout=spec(BF, 4, 4, 32, 256),
    wgu=spec(BF, 4, 4, 2, 32, 768),
    wdn=spec(BF, 4, 4, 96, 256),
    kv=spec(BF, 4, 2, 2, 128, 256),
    q2=spec(BF, 512, 128),
    prob=spec(BF, 16, 128, 512),
    ot=spec(F32, 128, 256),
    gu=spec(F32, 256, 768),
    hid=spec(BF, 256, 384),
    dkv=spec(BF, 4, 2, 256, 256),
    dkvab=spec(BF, 2, 2, 256, 256),
    dkvc=spec(BF, 256, 256),
    dkvds=spec(BF, 256, 256),
    dkvd=spec(BF, 256, 256),
    dkves=spec(BF, 256, 256),
    dkve=spec(BF, 256, 256),
    gwk=spec(BF, 4, 8, 32, 128),
    gwv=spec(BF, 4, 4, 2, 32, 256),
    gwout=spec(BF, 4, 4, 32, 256),
    gwgu=spec(BF, 4, 4, 2, 32, 768),
    gwdn=spec(BF, 4, 4, 96, 256),
    rzk=spec(BF, 3, 8, 32, 128),
    ryv=spec(BF, 3, 4, 2, 32, 256),
    rzout=spec(BF, 3, 4, 32, 256),
    hygu=spec(BF, 2, 2, 2, 32, 768),
    bygu=spec(BF, 2, 4, 2, 32, 768),
    hzdn=spec(BF, 2, 2, 96, 256),
    bzdn=spec(BF, 2, 4, 96, 256),
    share=spec(F32, 8, 512),
    sk=spec(BF, 8, 32, 128),
    sv=spec(BF, 4, 2, 32, 256),
    sout=spec(BF, 4, 32, 256),
    sgu=spec(BF, 4, 2, 32, 768),
    sdn=spec(BF, 4, 96, 256),
    fk=spec(BF, 8, 32, 128),
    fv=spec(BF, 8, 32, 256),
    fgu=spec(BF, 8, 32, 768),
    yout=spec(BF, 4, 32, 256),
    ydn=spec(BF, 4, 96, 256),
    cout=spec(BF, 32, 256),
    cdn=spec(BF, 96, 256),
    fout=spec(BF, 32, 256),
    fdn=spec(BF, 96, 256),
)
SUB = dict(
    a=spec(BF, 2, 8, 16, 1024),
    h=spec(BF, 2, 16, 1024),
    gr=spec(BF, 2, 16, 1024),
    gb=spec(BF, 2, 8, 16, 1024),
)
EXCHANGE = dict(
    pb=spec(BF, 2, 2, 4, 16, 1024),
    sib=spec(BF, 2, 4, 16, 1024),
    xs=spec(BF, 2, 3, 16, 1024),
    xr=spec(BF, 2, 3, 16, 1024),
)
N_SEM = 282
N_LAYERS, N_SUB, N_EXCHANGE = 2, 4, 8


def groups():
    arguments = [(4, 0, FAR_IN), (0, 0, NEAR_IN)]
    results = [(4, 0, FAR_OUT), (0, 0, NEAR_OUT)]
    scratch = [(0, 0, COMMON), (0, 0, FAR_IN), (0, 0, FAR_OUT)]
    for l in range(N_LAYERS):
        arguments += [(5, l, FAR_LAYER_IN), (1, l, NEAR_LAYER_IN)]
        results += [(5, l, FAR_LAYER_OUT)]
        scratch += [(1, l, LAYER), (1, l, FAR_LAYER_IN), (1, l, FAR_LAYER_OUT)]
    scratch += [(2, i, SUB) for i in range(N_SUB)] + [(3, n, EXCHANGE) for n in range(N_EXCHANGE)]
    return arguments, results, scratch


def named(refs):
    spaces = [[SimpleNamespace() for _ in range(n)] for n in (1, N_LAYERS, N_SUB, N_EXCHANGE, 1, N_LAYERS)]
    left = list(refs)
    for group in groups():
        for kind, index, specs in group:
            for name in specs:
                setattr(spaces[kind][index], name, left.pop(0))
    return spaces[0][0], spaces[1], spaces[2], spaces[3], spaces[4][0], spaces[5]


def specs_of(group):
    return [entry for _, _, specs in group for entry in specs.values()]


def blocks_of(group):
    spaces = [pl.ANY if kind >= 4 else pltpu.VMEM for kind, _, specs in group for _ in specs]
    return [pl.BlockSpec(memory_space=space) for space in spaces]


def nn(a, b):
    return lax.dot_general(a, b, (((1,), (0,)), ((), ())), preferred_element_type=F32)


def nt(a, b):
    return lax.dot_general(a, b, (((1,), (1,)), ((), ())), preferred_element_type=F32)


def tn(a, b):
    return lax.dot_general(a, b, (((0,), (0,)), ((), ())), preferred_element_type=F32)


def normalize(h):
    inverse = lax.rsqrt(jnp.mean(h * h, axis=-1, keepdims=True) + EPS)
    return h * inverse, inverse


def kernel(*refs):
    R, L, S, X, far_r, far_l = named(refs[:-1])
    sems = refs[-1]
    used = [0]
    pending, kept = [], []
    outgoing = []

    def new():
        used[0] += 1
        return sems.at[used[0] - 1]

    x = lax.axis_index("section")
    c = lax.axis_index("ctx")
    z, y, k = lax.div(c, 8), lax.rem(lax.div(c, 2), 4), lax.rem(c, 2)
    t = 2 * x + k
    s = lax.div(y, 2)
    yy = lax.rem(y, 2)
    other = 1 - k

    def plus(v, j):
        return lax.rem(v + j, 4)

    def dev(xd, zd, yd, kd):
        return {"section": xd, "ctx": zd * 8 + yd * 2 + kd}

    def flip(j):
        return k if j % 2 == 0 else other

    sibling = dev(x, z, y, other)

    def put(src, dst, to, rsem):
        if len(pending) % 32 == 0:
            outgoing.append(new())
        copy = pltpu.make_async_remote_copy(
            src_ref=src, dst_ref=dst, send_sem=outgoing[-1], recv_sem=rsem, device_id=to, device_id_type=MESH
        )
        copy.start()
        pending.append(copy)

    def put_or_keep(mine, src, dst, to, rsem):
        copy = pltpu.make_async_remote_copy(
            src_ref=src, dst_ref=dst, send_sem=new(), recv_sem=rsem, device_id=to, device_id_type=MESH
        )

        @pl.when(mine)
        def _():
            pltpu.make_async_copy(src, dst, rsem).start()

        @pl.when(jnp.logical_not(mine))
        def _():
            copy.start()

        kept.append((mine, copy))

    def arrived(ref, sem):
        pltpu.make_async_copy(ref, ref, sem).wait()

    barrier = pltpu.get_barrier_semaphore()

    def greet(d):
        pl.semaphore_signal(barrier, inc=1, device_id=d, device_id_type=MESH)

    count = 0
    for j in range(4):
        for i in range(2):
            if (j, i) != (0, 0):
                greet(dev(plus(x, j), z, y, flip(i)))
                count += 1
            if j:
                greet(dev(x, z, plus(y, j), flip(i)))
                greet(dev(x, plus(z, j), y, flip(i)))
                count += 2
            greet(dev(plus(x, j), 3 - z, 3 - y, flip(i)))
            count += 1
    crossing = jnp.where(x == z, 0, 1)

    @pl.when(x != z)
    def _():
        greet(dev(z, x, y, k))

    def fetch(src, dst):
        copy = pltpu.make_async_copy(src, dst, new())
        copy.start()
        return copy

    def fetch_att(l):
        ends = ((far_l[l].wq, L[l].wq), (far_l[l].wk, L[l].wk), (far_l[l].wv, L[l].wv), (far_l[l].wo, L[l].wo))
        return [fetch(src, dst) for src, dst in ends]

    def wait_for(copies):
        for copy in copies:
            copy.wait()

    coming = fetch_att(0)
    xin_coming = fetch(far_r.xin, R.xin)
    later = fetch_att(1) + [fetch(far_r.cot, R.cot)]
    for l in range(2):
        later += [fetch(far_l[l].wg, L[l].wg), fetch(far_l[l].wu, L[l].wu)]
    leaving = []

    def leave(src, dst):
        leaving.append(fetch(src, dst))

    def pack_att(l):
        for i in range(2):
            L[l].qkst[i, :, 0:128] = L[l].wq[:, 128 * i : 128 * i + 128]
            L[l].qkst[i, :, 128:256] = L[l].wk[:, 128 * i : 128 * i + 128]
            L[l].vst[i] = L[l].wv[:, 128 * i : 128 * i + 128]

    def pack_rest():
        lane = lax.broadcasted_iota(I32, (1, 768), 1)
        half = (lane >= 384).astype(I32)
        place = lane - 384 * half
        group = (place >= 96).astype(I32) + (place >= 192).astype(I32) + (place >= 288).astype(I32)
        place = place - 96 * group
        unit = jnp.where(place < 88, 352 * half + 88 * group + place, -1)
        R.pick[...] = (lax.broadcasted_iota(I32, (704, 768), 0) == unit).astype(F32).astype(BF)
        stacked = jnp.concatenate([w[...] for l in range(2) for w in (L[l].wg, L[l].wu)], axis=0)
        stacked = nn(stacked, R.pick[...]).astype(BF)
        for l in range(2):
            for i in range(2):
                for n in range(2):
                    rows = stacked[64 * l + 32 * n : 64 * l + 32 * n + 32, 384 * i : 384 * i + 384]
                    L[l].gus[i, :, 384 * n : 384 * n + 384] = rows
            L[l].wds[0:88, :] = L[l].wd[...]
            L[l].wds[88:96, :] = jnp.zeros((8, 256), BF)
        pack_att(1)
        R.gg[...] = jnp.zeros((8, 1024), F32)

    wait_for(coming)
    pack_att(0)
    column = lax.broadcasted_iota(I32, (32, 128), 1) - 32 * lax.rem(c, 4)
    spot = (lax.broadcasted_iota(I32, (32, 128), 0) == column).astype(F32).astype(BF)
    piece = nn(jnp.broadcast_to(R.gains_in[...].astype(F32), (8, 32)).astype(BF), spot)
    R.gst[...] = jnp.where(lax.broadcasted_iota(I32, (8, 128), 0) == x, piece, 0.0)
    pl.semaphore_wait(barrier, count + crossing)

    W = [SimpleNamespace(), SimpleNamespace()]
    G = [SimpleNamespace(), SimpleNamespace()]
    partner = dev(x, z, y + 1 - 2 * yy, k)
    mate = 1 - yy
    slot_m = 2 * yy + k

    def keep(src, dst, sem):
        pltpu.make_async_copy(src, dst, sem).start()

    def to_z(src, dst, js=(1, 3, 2)):
        sem = new()
        for j in js:
            put(src, dst, dev(x, plus(z, j), y, k), sem)
        return sem

    def to_y(src, dst, js=(1, 3, 2)):
        sem = new()
        for j in js:
            put(src, dst, dev(x, z, plus(y, j), k), sem)
        return sem

    def qk_first(l):
        src, dst = L[l].qkst, L[l].wqk.at[z, 2 * y + k]
        sem = W[l].qk = new()
        keep(src.at[k], dst, sem)
        for j in (2, 6, 4, 3, 7, 5, 1):
            put(src.at[flip(j)], dst, dev(x, z, plus(y, j // 2), flip(j)), sem)

    def qk_second(l):
        w = L[l].wqk
        arrived(w.at[z], W[l].qk)
        W[l].qk = to_z(w.at[z], w.at[z])

    def z_first(src, w):
        sem, dst = new(), w.at[z, y, k]
        keep(src.at[k], dst, sem)
        for j in (2, 6, 4, 3, 7, 5, 1):
            put(src.at[flip(j)], dst, dev(x, plus(z, j // 2), y, flip(j)), sem)
        return sem

    def v_second(l):
        w = L[l].wval
        arrived(w.at[:, y], W[l].v)
        W[l].v = to_y(w.at[:, y], w.at[:, y])

    def at_y(j):
        return dev(x, z, plus(y, j), k)

    def at_z(j):
        return dev(x, plus(z, j), y, k)

    def ring_start(block, v, at, direct=False):
        sems_ = [new() for _ in range(4)]
        put(block(v), block(v), at(1), sems_[0])
        put(block(v), block(v), at(3), sems_[1])
        if direct:
            put(block(v), block(v), at(2), sems_[2])
        return block, v, at, sems_, direct

    def ring_relay(state):
        block, v, at, sems_, direct = state
        if direct:
            return
        before, after = plus(v, 3), plus(v, 1)
        arrived(block(before), sems_[0])
        put(block(before, 0), block(before, 0), at(1), sems_[2])
        arrived(block(after), sems_[1])
        put(block(after, 1), block(after, 1), at(3), sems_[3])

    def ring_end(state):
        block, v, at, sems_, direct = state
        far = plus(v, 2)
        if direct:
            arrived(block(plus(v, 3)), sems_[0])
            arrived(block(plus(v, 1)), sems_[1])
            arrived(block(far), sems_[2])
            return
        arrived(block(far, 0), sems_[2])
        arrived(block(far, 1), sems_[3])

    def halved(h):
        return slice(None) if h is None else slice(2 * h, 2 * h + 2)

    def gate_start(l):
        arrived(L[l].wgu.at[:, y], W[l].gu)
        W[l].gate = ring_start(lambda v, h=None: L[l].wgu.at[halved(h), v, :, :, 0:384], y, at_y)

    def up_start(l):
        W[l].up = ring_start(lambda v, h=None: L[l].wgu.at[halved(h), v, :, :, 384:768], y, at_y)

    def down_start(l):
        arrived(L[l].wdn.at[z], W[l].d)
        W[l].d = ring_start(lambda v, h=None: L[l].wdn.at[v, halved(h)], z, at_z, True)

    def cross_first(src, dst):
        sem = new()
        put_or_keep(x == z, src, dst, dev(z, x, y, k), sem)
        return sem

    def cross_second(src, w, sem):
        arrived(src, sem)
        sem, dst = new(), w.at[z, slot_m]
        put_or_keep(s == k, src, dst, dev(x, z, y, s), sem)
        for j in (1, 3, 2):
            put(src, dst, dev(x, z, plus(y, j), s), sem)
        return sem

    def cross_third(w, sem):
        arrived(w.at[z], sem)
        return to_z(w.at[z], w.at[z])

    streams = (0, 1)
    sums = {}

    def rs_start(n, i, part):
        pb, sib = X[n].pb, X[n].sib
        for r in range(8):
            pb[i, r % 2, r // 2] = part[16 * r : 16 * r + 16].astype(BF)
        sem = sums[n, i] = new()
        for j in (1, 3, 2, 0):
            xd = plus(x, j)
            put(pb.at[i, other, xd], sib.at[i, xd], sibling, sem)

    def rs_mid(n, i):
        pb, sib, xs, xr = X[n].pb, X[n].sib, X[n].xs, X[n].xr
        arrived(sib.at[i], sums[n, i])
        sem = sums[n, i] = new()
        for j in (1, 3, 2):
            xd = plus(x, j)
            xs[i, j - 1] = (pb[i, k, xd].astype(F32) + sib[i, xd].astype(F32)).astype(BF)
            put(xs.at[i, j - 1], xr.at[i, j - 1], dev(xd, z, y, k), sem)

    def rs_end(n, i):
        pb, sib, xr = X[n].pb, X[n].sib, X[n].xr
        total = pb[i, k, x].astype(F32) + sib[i, x].astype(F32)
        arrived(xr.at[i], sums[n, i])
        for j in (1, 3, 2):
            total += xr[i, j - 1].astype(F32)
        return total

    def gather_start(buf, i, block):
        buf[i, t] = block
        mine = buf.at[i, t]
        rx = {j: new() for j in (1, 3, 2)}
        rk = new()
        for j in (1, 3, 2):
            put(mine, mine, dev(plus(x, j), z, y, k), rx[j])
        put(mine, mine, sibling, rk)
        return buf, i, rx, rk

    def gather_forward(state):
        if state is not None:
            buf, i, rx, rk = state
            for j in (1, 3, 2):
                slot = buf.at[i, 2 * plus(x, 4 - j) + k]
                arrived(slot, rx[j])
                put(slot, slot, sibling, rk)

    def gather_finish(state):
        if state is not None:
            buf, i, rx, rk = state
            arrived(buf.at[i, 0:4], rk)

    def nothing():
        pass

    def opened(states, n, work, early=nothing):
        gather_finish(states[0])
        work(0)
        gather_forward(states[1])
        rs_mid(n, 0)
        early()
        gather_finish(states[1])
        work(1)
        rs_mid(n, 1)

    def closed(rows_of, buf, between):
        first = gather_start(buf, 0, rows_of(0))
        second = gather_start(buf, 1, rows_of(1))
        between()
        gather_forward(first)
        return first, second

    def to_owners(i, rows, stage, landing, sem):
        for r in range(4):
            stage[i, r] = rows[:, 256 * r : 256 * r + 256]
        zd, yd = (z, y) if i == 0 else (3 - z, 3 - y)
        kd = lax.div(x, 2)
        first_row = pl.multiple_of(16 * (2 * lax.rem(x, 2) + k), 16)
        dst = landing.at[s, pl.ds(first_row, 16)]
        for j in range(4):
            xd = plus(x, j)
            if i == 0 and j == 0:
                put_or_keep(kd == k, stage.at[i, xd], dst, dev(xd, zd, yd, kd), sem)
            else:
                put(stage.at[i, xd], dst, dev(xd, zd, yd, kd), sem)

    def spread_tokens(src, dst):
        rows = pl.ds(4 * k, 4)
        close, mirrored = new(), new()
        put(src.at[1 - s], dst.at[1, rows], dev(x, 3 - z, 3 - y, k), mirrored)
        put(src.at[s], dst.at[0, rows], sibling, close)
        dst[0, rows] = src[s]
        return close, mirrored

    def spread_rest(dst, sems_):
        close, mirrored = sems_
        far = dst.at[1, pl.ds(4 * k, 4)]
        arrived(far, mirrored)
        put(far, far, sibling, close)
        arrived(dst.at[0], close)

    lane = lax.broadcasted_iota(I32, (1, 512), 1)
    own_block = 4 * z + y
    query_pos = 128 * jnp.where(lane < 256, own_block, 15 - own_block) + lax.rem(lane, 128)
    ids = R.seg[s]

    def tokens_to(n):
        return jnp.sum(jnp.where(ids <= n, 1.0, 0.0), axis=1, keepdims=True).astype(I32)

    first, second = tokens_to(0), tokens_to(1)
    query_start = jnp.where(query_pos < first, 0, jnp.where(query_pos < second, first, second))
    head_lane = lax.broadcasted_iota(I32, (128, 128), 1) < 64

    def two_heads(v):
        zero = jnp.zeros_like(v)
        return jnp.concatenate([jnp.where(head_lane, v, zero), jnp.where(head_lane, zero, v)], axis=0)

    def own_heads(vt):
        return jnp.concatenate([vt[0:64, 0:128], vt[64:128, 128:256]], axis=0)

    def gain_row(i):
        return R.gains[i : i + 1, :]

    def full(ref):
        return ref[...].reshape(256, 1024)

    def keys_of(l, zz):
        return L[l].kv[zz, :, :, :, 0:128].reshape(512, 128)

    def values_of(l, zz):
        return L[l].kv[zz, :, :, :, 128:256].reshape(512, 128)

    def attention_forward(l, states, hook, late):
        kv = L[l].kv
        direct, relayed = ([{j: new() for j in (1, 2, 3)} for _ in streams] for _ in range(2))
        from_mate = [new() for _ in streams]
        for i in streams:
            if i == 1:
                gather_forward(states[1])
            gather_finish(states[i])
            a = S[2 * l].a[i].reshape(128, 1024)
            w = L[l].wqk
            if i == 0:
                arrived(w.at[0:3], W[l].qk)
            qk = nn(a, w[...].reshape(1024, 256))
            w = L[l].wval
            if i == 0:
                arrived(w.at[0:3], W[l].v)
            u = nn(a, w[...].reshape(1024, 128))
            if l == 0:
                values = u.astype(BF)
            else:
                values = (0.5 * u + 0.5 * L[0].kv[z, yy, i, :, 128:256].astype(F32)).astype(BF)
            kv[z, yy, i, :, 0:128] = qk[:, 128:256].astype(BF)
            kv[z, yy, i, :, 128:256] = values
            own = kv.at[z, yy, i]
            for j in (1, 3):
                put(own, own, dev(x, plus(z, j), y, k), direct[i][j])
            put(own, own, partner, from_mate[i])
            put(own, own, dev(x, plus(z, 2), y, k), direct[i][2])
            L[l].q2[256 * i : 256 * i + 256, :] = two_heads((qk[:, 0:128].astype(BF) * 0.125).astype(BF))
        for i in streams:
            near = kv.at[z, mate, i]
            arrived(near, from_mate[i])
            for j in (1, 3):
                put(near, near, dev(x, plus(z, j), y, k), relayed[i][j])
        scores = R.scores
        top = jnp.full((1, 512), MASKED, F32)
        for j in (0, 3, 1, 2):
            zz = plus(z, j)
            for i in streams:
                if j % 2:
                    arrived(kv.at[zz, yy, i], direct[i][4 - j])
                    arrived(kv.at[zz, mate, i], relayed[i][4 - j])
                elif j:
                    arrived(kv.at[zz, mate, i], relayed[i][2])
            if j == 1:
                hook()
            scores[4 * j : 4 * j + 4] = nt(keys_of(l, zz), L[l].q2[...]).reshape(4, 128, 512)

            def mask(i, top, j=j, zz=zz):
                block = 4 * zz + 2 * s + lax.div(i, 2)
                base = 128 * (block + lax.rem(i, 2) * (15 - 2 * block))
                row = lax.broadcasted_iota(I32, (128, 512), 0)
                seen = (row >= query_start - base) & (row <= query_pos - base)
                v = jnp.where(seen, scores[4 * j + i], MASKED)
                scores[4 * j + i] = v
                return jnp.maximum(top, jnp.max(v, axis=0, keepdims=True))

            top = lax.fori_loop(0, 4, mask, top)
            if j == 0:
                for i in streams:
                    opposite = kv.at[plus(z, 2), yy, i]
                    arrived(opposite, direct[i][2])
                    put(opposite, opposite, partner, relayed[i][2])
        prob = L[l].prob
        for i in streams:
            lanes = slice(256 * i, 256 * i + 256)
            high = top[:, lanes]

            def expo(r, total):
                v = jnp.exp(scores[r, :, lanes] - high)
                prob[r, :, lanes] = v.astype(BF)
                return total + jnp.sum(v, axis=0, keepdims=True)

            share = 1.0 / lax.fori_loop(0, 16, expo, jnp.zeros((1, 256), F32))
            L[l].share[0:1, lanes] = share
            ot = jnp.zeros((128, 256), F32)
            for j in range(4):
                ot += tn(values_of(l, plus(z, j)), prob[4 * j : 4 * j + 4, :, lanes].reshape(512, 256))
            ot = ot * share
            ot = own_heads(ot)
            L[l].ot[:, 128 * i : 128 * i + 128] = ot
            o = jnp.transpose(ot).astype(BF)
            if i == 0:
                arrived(L[l].wout.at[0:3], W[l].o)
            part = jnp.concatenate([nn(o, L[l].wout[r].reshape(128, 256)) for r in range(4)], axis=1)
            rs_start(2 * l, i, part)
        for i in streams:
            rs_mid(2 * l, i)
        late()

    def feedforward_forward(l, states, early, hook):
        w = L[l].wgu

        def work(i):
            a = S[2 * l + 1].a[i].reshape(128, 1024)
            if i == 0:
                ring_end(W[l].gate)
            gate = nn(a, w[:, :, :, :, 0:384].reshape(1024, 384))
            if i == 0:
                ring_end(W[l].up)
            up = nn(a, w[:, :, :, :, 384:768].reshape(1024, 384))
            rows = slice(128 * i, 128 * i + 128)
            L[l].gu[rows, 0:384] = gate
            L[l].gu[rows, 384:768] = up
            hidden = (gate * jax.nn.sigmoid(gate) * up).astype(BF)
            L[l].hid[rows, :] = hidden
            if i == 0:
                ring_end(W[l].d)
            part = jnp.concatenate([nn(hidden, L[l].wdn[r].reshape(384, 256)) for r in range(4)], axis=1)
            rs_start(2 * l + 1, i, part)

        opened(states, 2 * l + 1, work, early)
        hook()

    def next_rows(n, between=nothing):
        def rows_of(i):
            rows = (S[n].h[i].astype(F32) + rs_end(n, i)).astype(BF)
            S[n + 1].h[i] = rows
            normed, _ = normalize(rows.astype(F32))
            return (normed * gain_row(n + 1)).astype(BF)

        return closed(rows_of, S[n + 1].a, between)

    def norm_backward(n, i):
        da = rs_end(4 + n, i)
        normed, inverse = normalize(S[n].h[i].astype(F32))
        gain_part = jnp.sum(da * normed, axis=0, keepdims=True)
        if n == 0:
            pass
        elif i == 0:
            R.gg[n : n + 1, :] = gain_part
        else:
            R.gg[n : n + 1, :] += gain_part
        scaled = da * gain_row(n)
        mixed = scaled - normed * jnp.mean(scaled * normed, axis=-1, keepdims=True)
        return (S[n].gr[i].astype(F32) + inverse * mixed).astype(BF)

    def hand_back(n, between=nothing):
        def rows_of(i):
            rows = norm_backward(n, i)
            S[n - 1].gr[i] = rows
            return rows

        return closed(rows_of, S[n - 1].gb, between)

    def send_z(g, landing):
        sem = new()
        for j in (1, 3, 2):
            zd = plus(z, j)
            put(g.at[zd], landing.at[j - 1], dev(x, zd, y, k), sem)
        return sem

    def send_y(g, landing):
        sem = new()
        for j in (1, 3, 2):
            yd = plus(y, j)
            put(g.at[:, yd], landing.at[j - 1], dev(x, z, yd, k), sem)
        return sem

    def attention_backward(l, states, hook):
        n = 2 * l
        wo, dkv, prob = L[l].wout, L[l].dkv, L[l].prob
        ab, own_ab, c_sem = {j: new() for j in (1, 3)}, {j: new() for j in (1, 3)}, new()
        dq = []
        for i in streams:
            if i == 1:
                gather_forward(states[1])
            gather_finish(states[i])
            gb = S[n].gb[i].reshape(128, 1024)
            dot_ = nt(wo[0].reshape(128, 256), gb[:, 0:256])
            for r in range(1, 4):
                dot_ += nt(wo[r].reshape(128, 256), gb[:, 256 * r : 256 * r + 256])
            dot_ = dot_.astype(BF).astype(F32)
            do2 = two_heads(jnp.transpose(dot_).astype(BF))
            share = L[l].share[0:1, 256 * i : 256 * i + 256]
            head_row = lax.broadcasted_iota(I32, (128, 128), 0) < 64
            scaled = dot_ * jnp.where(head_row, share[:, 0:128], share[:, 128:256])
            R.do2[256 * i : 256 * i + 256, :] = two_heads(jnp.transpose(scaled).astype(BF))
            prod = dot_ * L[l].ot[:, 128 * i : 128 * i + 128]
            delta = jnp.concatenate(
                [jnp.sum(prod[0:64], axis=0, keepdims=True), jnp.sum(prod[64:128], axis=0, keepdims=True)], axis=1
            )
            lanes = slice(256 * i, 256 * i + 256)
            dqt = jnp.zeros((128, 256), F32)
            for j in (2, 1, 3, 0):
                zz = plus(z, j)
                p = prob[4 * j : 4 * j + 4, :, lanes].reshape(512, 256)
                dp = nt(values_of(l, zz), do2)
                ds = (p.astype(F32) * ((dp - delta) * share)).astype(BF)
                R.ds[j, :, lanes] = ds
                if i == 1:
                    p = prob[4 * j : 4 * j + 4].reshape(512, 512)
                    dkv[zz, :, :, 0:128] = nn(R.ds[j], L[l].q2[...]).astype(BF).reshape(2, 256, 128)
                    dkv[zz, :, :, 128:256] = nn(p, R.do2[...]).astype(BF).reshape(2, 256, 128)
                    if j % 2:
                        put(dkv.at[zz, mate], L[l].dkvab.at[j // 2, mate], dev(x, zz, y, k), ab[j])
                    elif j:
                        put(dkv.at[zz, mate], L[l].dkvc, partner, c_sem)
                dqt += tn(keys_of(l, zz), ds)
                if i == 1 and j == 3:
                    for r in (1, 3):
                        put(dkv.at[plus(z, r), yy], L[l].dkvab.at[r // 2, yy], dev(x, plus(z, r), y, k), own_ab[r])
            dq.append(jnp.transpose(own_heads(dqt) * 0.125).astype(BF))
        dq = jnp.concatenate(dq, axis=0)
        gb = full(S[n].gb)
        arrived(L[l].dkvc, c_sem)
        far = plus(z, 2)
        L[l].dkvds[...] = (dkv[far, yy].astype(F32) + L[l].dkvc[...].astype(F32)).astype(BF)
        d_sem, e_sem = new(), new()
        put(L[l].dkvds, L[l].dkvd, dev(x, far, y, k), d_sem)
        got = L[l].dkvab
        arrived(got.at[0, mate], ab[1])
        arrived(got.at[1, mate], ab[3])
        L[l].dkves[...] = (dkv[z, mate].astype(F32) + got[0, mate].astype(F32) + got[1, mate].astype(F32)).astype(BF)
        put(L[l].dkves, L[l].dkve, partner, e_sem)
        gw = L[l].gwout
        otb = L[l].ot[...].astype(BF)
        for i in range(4):
            gw[i] = nn(otb, gb[:, 256 * i : 256 * i + 256]).astype(BF).reshape(4, 32, 256)
        at = jnp.transpose(full(S[n].a))
        arrived(got.at[0, yy], own_ab[1])
        arrived(got.at[1, yy], own_ab[3])
        tot = dkv[z, yy].astype(F32) + got[0, yy].astype(F32) + got[1, yy].astype(F32)
        arrived(L[l].dkvd, d_sem)
        arrived(L[l].dkve, e_sem)
        tot = tot + L[l].dkvd[...].astype(F32) + L[l].dkve[...].astype(F32)
        dk = tot[:, 0:128].astype(BF)
        dvals = tot[:, 128:256]
        if l == 1:
            half = 0.5 * dvals.astype(BF).astype(F32)
            du = half.astype(BF)
            R.dmh[...] = du
        else:
            du = (dvals + R.dmh[...].astype(F32)).astype(BF)
        def send_grads():
            grads = nn(at, jnp.concatenate([dq, du, dk], axis=1)).astype(BF)
            L[l].gwv[...] = grads[:, 0:256].reshape(4, 4, 2, 32, 256)
            L[l].gwk[...] = grads[:, 256:384].reshape(4, 8, 32, 128)
            G[l].k = send_z(L[l].gwk, L[l].rzk)
            G[l].v = send_y(L[l].gwv, L[l].ryv)

        if l == 0:
            send_grads()
        for i in streams:
            rows = slice(128 * i, 128 * i + 128)
            da = nt(jnp.concatenate([dq[rows], dk[rows]], axis=1), L[l].wqk[...].reshape(1024, 256))
            da += nt(du[rows], L[l].wval[...].reshape(1024, 128))
            rs_start(4 + n, i, da)
            if l == 0:
                gain_part = jnp.sum(da * R.normed[rows, :], axis=0, keepdims=True)
                if i == 0:
                    R.gg[0:1, :] = gain_part
                else:
                    R.gg[0:1, :] += gain_part
        if l == 0:
            for j in (1, 3, 2):
                put(R.gg, R.ggx.at[j - 1], dev(plus(x, j), z, y, k), landed.gx)
        for i in streams:
            rs_mid(4 + n, i)
        if l == 1:
            send_grads()
        G[l].o = send_z(L[l].gwout, L[l].rzout)
        hook()

    def feedforward_backward(l, states, hook):
        n = 2 * l + 1

        def work(i):
            gb = S[n].gb[i].reshape(128, 1024)
            wd = L[l].wdn
            dhid = nt(gb[:, 0:256], wd[0].reshape(384, 256))
            for r in range(1, 4):
                dhid += nt(gb[:, 256 * r : 256 * r + 256], wd[r].reshape(384, 256))
            gu = L[l].gu[128 * i : 128 * i + 128, :]
            gate, up = gu[:, 0:384], gu[:, 384:768]
            sig = jax.nn.sigmoid(gate)
            dgate = dhid * up * sig * (1.0 + gate * (1.0 - sig))
            dup = dhid * (gate * sig)
            dgu = jnp.concatenate([dgate.astype(BF), dup.astype(BF)], axis=1)
            R.dgu[i] = dgu
            rs_start(4 + n, i, nt(dgu, L[l].wgu[...].reshape(1024, 768)))

        opened(states, 4 + n, work)
        at = jnp.transpose(full(S[n].a))
        gw = L[l].gwgu
        gw[...] = nn(at, R.dgu[...].reshape(256, 768)).astype(BF).reshape(4, 4, 2, 32, 768)
        far = plus(y, 2)
        G[l].g = [new() for _ in range(4)]
        put(gw.at[0:2, far], L[l].hygu.at[0], at_y(1), G[l].g[0])
        put(gw.at[2:4, far], L[l].hygu.at[1], at_y(3), G[l].g[1])
        gb = full(S[n].gb)
        ht = jnp.transpose(L[l].hid[...])
        gw = L[l].gwdn
        for i in range(4):
            gw[i] = nn(ht, gb[:, 256 * i : 256 * i + 256]).astype(BF).reshape(4, 96, 256)
        far = plus(z, 2)
        G[l].d = [new() for _ in range(4)]
        put(gw.at[far, 0:2], L[l].hzdn.at[0], at_z(1), G[l].d[0])
        put(gw.at[far, 2:4], L[l].hzdn.at[1], at_z(3), G[l].d[1])
        hook()

    def ff_push(l):
        gu, dn, hg, hd = L[l].gwgu, L[l].gwdn, L[l].hygu, L[l].hzdn
        for h, j in ((0, 1), (1, 3)):
            yd, zd, half = plus(y, j), plus(z, j), slice(2 * h, 2 * h + 2)
            arrived(hg.at[h], G[l].g[h])
            gu[half, yd] = (gu[half, yd].astype(F32) + hg[h].astype(F32)).astype(BF)
            put(gu.at[:, yd], L[l].bygu.at[h], at_y(j), G[l].g[2 + h])
            arrived(hd.at[h], G[l].d[h])
            dn[zd, half] = (dn[zd, half].astype(F32) + hd[h].astype(F32)).astype(BF)
            put(dn.at[zd], L[l].bzdn.at[h], at_z(j), G[l].d[2 + h])

    def summed(own, got):
        return own.astype(F32) + got[0].astype(F32) + got[1].astype(F32) + got[2].astype(F32)

    def rows_back(st, land):
        sem = new()
        for j in range(4):
            m = plus(slot_m, j)
            to = dev(x, z, 2 * k + lax.div(m, 2), lax.rem(m, 2))
            if j == 0:
                put_or_keep(s == k, st.at[m], land.at[y], to, sem)
            else:
                put(st.at[m], land.at[y], to, sem)
        return sem

    def four(land):
        return land[0].astype(F32) + land[1].astype(F32) + land[2].astype(F32) + land[3].astype(F32)

    def out_second(l):
        arrived(L[l].rzout, G[l].o)
        L[l].sout[...] = summed(L[l].gwout[z], L[l].rzout).astype(BF)
        G[l].o = rows_back(L[l].sout, L[l].yout)

    def out_third(l):
        arrived(L[l].yout, G[l].o)
        L[l].cout[...] = four(L[l].yout).astype(BF)
        G[l].o = cross_first(L[l].cout, L[l].fout)

    def out_end(l):
        arrived(L[l].fout, G[l].o)
        L[l].oo[...] = L[l].fout[...].astype(F32)
        leave(L[l].oo, far_l[l].oo)

    def down_second(l):
        got = L[l].bzdn
        arrived(got.at[0], G[l].d[2])
        arrived(got.at[1], G[l].d[3])
        L[l].sdn[...] = (L[l].gwdn[z].astype(F32) + got[0].astype(F32) + got[1].astype(F32)).astype(BF)
        G[l].d = rows_back(L[l].sdn, L[l].ydn)

    def down_third(l):
        arrived(L[l].ydn, G[l].d)
        L[l].cdn[...] = four(L[l].ydn).astype(BF)
        G[l].d = cross_first(L[l].cdn, L[l].fdn)

    def down_end(l):
        arrived(L[l].fdn, G[l].d)
        L[l].od[...] = L[l].fdn[0:88, :].astype(F32)
        leave(L[l].od, far_l[l].od)

    def rows_y(g, got, st, land, sem):
        arrived(got, sem)
        st[...] = summed(g[z], got).astype(BF)
        sem = new()
        land[0] = st[2 * y + k]
        for j in (2, 6, 4, 3, 7, 5, 1):
            yd, kd = plus(y, j // 2), flip(j)
            put(st.at[2 * yd + kd], land.at[j], dev(x, z, yd, kd), sem)
        return sem

    def rows_z(st, land):
        sem = new()
        land[0] = st[z, k]
        for j in (2, 6, 4, 3, 7, 5, 1):
            zd, kd = plus(z, j // 2), flip(j)
            put(st.at[zd, kd], land.at[j], dev(x, zd, y, kd), sem)
        return sem

    def halves(land, sem):
        if sem is not None:
            arrived(land.at[1:8], sem)
        own = land[0].astype(F32) + land[2].astype(F32) + land[4].astype(F32) + land[6].astype(F32)
        far = land[1].astype(F32) + land[3].astype(F32) + land[5].astype(F32) + land[7].astype(F32)
        return jnp.where(k == 0, own, far), jnp.where(k == 0, far, own)

    def k_second(l):
        G[l].k = rows_y(L[l].gwk, L[l].rzk, L[l].sk, L[l].fk, G[l].k)

    def v_grad_second(l):
        g, got, st = L[l].gwv, L[l].ryv, L[l].sv
        arrived(got, G[l].v)
        for i in range(4):
            own = g[i, y].astype(F32) + got[0, i].astype(F32) + got[1, i].astype(F32) + got[2, i].astype(F32)
            st[i] = own.astype(BF)
        G[l].v = rows_z(st, L[l].fv)

    def gu_grad_second(l):
        g, got, st = L[l].gwgu, L[l].bygu, L[l].sgu
        arrived(got.at[0], G[l].g[2])
        arrived(got.at[1], G[l].g[3])
        for i in range(4):
            st[i] = (g[i, y].astype(F32) + got[0, i].astype(F32) + got[1, i].astype(F32)).astype(BF)
        G[l].g = rows_z(st, L[l].fgu)

    def att_end(l):
        f = far_l[l]
        arrived(L[l].fv.at[1:8], G[l].v)
        for land, result, sem, to in (
            (L[l].fk, L[l].ok, G[l].k, f.ok),
            (L[l].fv.at[:, :, 0:128], L[l].oq, None, f.oq),
            (L[l].fv.at[:, :, 128:256], L[l].ov, None, f.ov),
        ):
            low, high = halves(land, sem)
            result[:, 0:128] = low
            result[:, 128:256] = high
            leave(result, to)

    def gu_end(l):
        low, high = halves(L[l].fgu, G[l].g)
        both = jnp.concatenate(
            [
                jnp.concatenate([low[:, 0:384], high[:, 0:384]], axis=1),
                jnp.concatenate([low[:, 384:768], high[:, 384:768]], axis=1),
            ],
            axis=0,
        )
        main = both.astype(BF)
        rest = (both - main.astype(F32)).astype(BF)
        both = nt(main, R.pick[...]) + nt(rest, R.pick[...])
        L[l].og[...] = both[0:32]
        L[l].ou[...] = both[32:64]
        leave(L[l].og, far_l[l].og)
        leave(L[l].ou, far_l[l].ou)

    def nothing():
        pass

    def att_first(l):
        qk_first(l)
        W[l].v = z_first(L[l].vst, L[l].wval)
        W[l].o = cross_first(L[l].wo, L[l].cwo)

    def ff_first(l):
        W[l].gu = z_first(L[l].gus, L[l].wgu)
        W[l].d = cross_first(L[l].wds, L[l].cwd)

    qk_first(0)
    W[0].v = z_first(L[0].vst, L[0].wval)
    xin_coming.wait()
    in_sems = spread_tokens(R.xin, R.hin)
    gx_sem = new()
    for j in (1, 3, 2):
        put(R.gst, R.gx.at[j - 1], dev(plus(x, j), z, y, k), gx_sem)
    W[0].o = cross_first(L[0].wo, L[0].cwo)
    wait_for(later)
    pack_rest()
    ff_first(0)
    arrived(R.gx, gx_sem)
    R.g1[...] = R.gst[...] + R.gx[0] + R.gx[1] + R.gx[2]
    gy_sem = new()
    R.gyr[2 * y + k] = R.g1[...]
    for j in range(1, 8):
        put(R.g1, R.gyr.at[2 * y + k], dev(x, z, plus(y, j // 2), flip(j)), gy_sem)
    qk_second(0)
    v_second(0)
    W[0].o = cross_second(L[0].cwo, L[0].wout, W[0].o)
    arrived(R.gyr.at[0:7], gy_sem)
    for i in range(2):
        R.gz[z, i] = R.gyr[4 * i] + R.gyr[4 * i + 1] + R.gyr[4 * i + 2] + R.gyr[4 * i + 3]
    gz_sem = to_z(R.gz.at[z], R.gz.at[z])
    spread_rest(R.hin, in_sems)
    normed, _ = normalize(full(R.hin).astype(F32))
    R.normed[...] = normed
    for i in streams:
        S[0].h[i] = R.hin[i, t]
    gate_start(0)
    arrived(R.gz.at[0:3], gz_sem)
    R.gains[...] = jnp.concatenate([R.gz[i // 2, i % 2] for i in range(8)], axis=1)
    S[0].a[...] = (normed * gain_row(0)).astype(BF).reshape(2, 8, 16, 1024)
    W[0].o = cross_third(L[0].wout, W[0].o)
    W[0].d = cross_second(L[0].cwd, L[0].wdn, W[0].d)
    cot_sems = []

    def after_keys_0():
        ring_relay(W[0].gate)
        up_start(0)
        down_start(0)
        att_first(1)
        ff_first(1)

    def in_gather_0():
        ring_relay(W[0].up)
        ring_relay(W[0].d)

    def in_ff_0():
        qk_second(1)
        v_second(1)

    def after_ff_0():
        W[1].o = cross_second(L[1].cwo, L[1].wout, W[1].o)
        gate_start(1)
        W[1].d = cross_second(L[1].cwd, L[1].wdn, W[1].d)

    def in_gather_1():
        W[1].o = cross_third(L[1].wout, W[1].o)

    def after_keys_1():
        ring_relay(W[1].gate)
        up_start(1)
        down_start(1)

    def after_att_1():
        cot_sems.append(spread_tokens(R.cot, S[3].gb))

    def in_gather_2():
        ring_relay(W[1].up)
        ring_relay(W[1].d)

    def take_cotangent():
        spread_rest(S[3].gb, cot_sems[0])
        for i in streams:
            S[3].gr[i] = S[3].gb[i, t]

    landed = SimpleNamespace(out=new(), ing=new(), gx=new())

    def finish_outputs():
        for i in streams:
            rows = (S[3].h[i].astype(F32) + rs_end(3, i)).astype(BF)
            to_owners(i, rows, R.outst, R.outrv, landed.out)

    none = (None, None)
    attention_forward(0, none, after_keys_0, nothing)
    feedforward_forward(0, next_rows(0, in_gather_0), in_ff_0, after_ff_0)
    attention_forward(1, next_rows(1, in_gather_1), after_keys_1, after_att_1)
    feedforward_forward(1, next_rows(2, in_gather_2), nothing, take_cotangent)

    def ff_grads(l):
        gu_grad_second(l)
        down_second(l)

    def att_grads():
        out_second(1)
        k_second(1)
        v_grad_second(1)

    def last_grads():
        ff_grads(0)

    def after_grads_1():
        att_grads()
        gu_end(1)

    def after_grads_0():
        last_grads()
        att_end(1)

    feedforward_backward(1, none, finish_outputs)
    states = hand_back(3, lambda: ff_push(1))
    attention_backward(1, states, lambda: ff_grads(1))
    states = hand_back(2, lambda: down_third(1))
    feedforward_backward(0, states, after_grads_1)
    states = hand_back(1, lambda: ff_push(0))
    out_third(1)
    attention_backward(0, states, after_grads_0)
    arrived(R.ggx, landed.gx)
    gg = R.gg[...] + R.ggx[0] + R.ggx[1] + R.ggx[2]
    for i in range(4):
        R.ggz[i] = gg[:, 256 * i : 256 * i + 256]
    gg_sem = new()
    for j in (1, 3, 2):
        zd = plus(z, j)
        put(R.ggz.at[zd], R.ggzr.at[j - 1], dev(x, zd, y, k), gg_sem)
    for i in streams:
        to_owners(i, norm_backward(0, i), R.ingst, R.ingrv, landed.ing)
    arrived(R.ggzr, gg_sem)
    gg = R.ggz[z] + R.ggzr[0] + R.ggzr[1] + R.ggzr[2]
    R.ggy[0] = gg[:, 0:128]
    R.ggy[1] = gg[:, 128:256]
    gg_sem = new()
    R.ggyr[0] = R.ggy[s]
    for j in range(1, 8):
        yd = plus(y, j // 2)
        put(R.ggy.at[lax.div(yd, 2)], R.ggyr.at[j], dev(x, z, yd, flip(j)), gg_sem)
    k_second(0)
    v_grad_second(0)
    out_second(0)
    down_third(0)
    out_third(0)
    out_end(1)
    down_end(1)
    gu_end(0)
    arrived(R.outrv, landed.out)
    R.out[...] = R.outrv[...].reshape(2, 1, 64, 256)
    leave(R.out, far_r.out)
    arrived(R.ingrv, landed.ing)
    R.ing[...] = R.ingrv[...].reshape(2, 1, 64, 256)
    leave(R.ing, far_r.ing)
    att_end(0)
    out_end(0)
    down_end(0)
    arrived(R.ggyr.at[1:8], gg_sem)
    gg = R.ggyr[0]
    for j in range(1, 8):
        gg = gg + R.ggyr[j]
    gg = jnp.sum(jnp.where(lax.broadcasted_iota(I32, (8, 128), 0) == x, gg, 0.0), axis=0, keepdims=True)
    part = lax.rem(c, 4)
    gain = jnp.zeros((1, 32), F32)
    for i in range(4):
        gain += jnp.where(part == i, gg[:, 32 * i : 32 * i + 32], 0.0)
    R.ogg[...] = gain
    wait_for(leaving)
    for copy in pending:
        copy.wait_send()
    for mine, copy in kept:

        @pl.when(jnp.logical_not(mine))
        def _(copy=copy):
            copy.wait_send()

    assert used[0] <= N_SEM, used


def call(*args):
    arguments, results, scratch = groups()
    return pl.pallas_call(
        kernel,
        out_shape=[jax.ShapeDtypeStruct(shape, dtype) for shape, dtype in specs_of(results)],
        in_specs=blocks_of(arguments),
        out_specs=blocks_of(results),
        scratch_shapes=[pltpu.VMEM(shape, dtype) for shape, dtype in specs_of(scratch)]
        + [pltpu.SemaphoreType.DMA((N_SEM,))],
        compiler_params=pltpu.CompilerParams(
            collective_id=0, has_side_effects=True, vmem_limit_bytes=62 * 1024 * 1024
        ),
    )(*args)


def hand_out(*refs):
    n = len(refs) // 2
    copies = [pltpu.make_async_copy(refs[i], refs[n + i], refs[-1].at[i]) for i in range(n)]
    for copy in copies:
        copy.start()
    for copy in copies:
        copy.wait()


def body(inputs, cotangent, segment_ids, gains, *weights):
    first = (inputs.reshape(2, 4, 16, 1024), cotangent.reshape(2, 4, 16, 1024), segment_ids, gains)
    results = call(*first, *weights)
    anywhere = pl.BlockSpec(memory_space=pl.ANY)
    return tuple(
        pl.pallas_call(
            hand_out,
            out_shape=[jax.ShapeDtypeStruct(r.shape, r.dtype) for r in results],
            in_specs=[pl.BlockSpec(memory_space=pltpu.VMEM)] * len(results),
            out_specs=[anywhere] * len(results),
            scratch_shapes=[pltpu.SemaphoreType.DMA((len(results),))],
        )(*results)
    )


def solution(mesh):
    tokens = P(None, None, "ctx", None)
    weight = P("ctx", "section")
    return jax.shard_map(
        body,
        mesh=mesh,
        in_specs=(tokens, tokens, P(), P("section", "ctx")) + (weight,) * 14,
        out_specs=(P(None, None, "ctx", "section"),) * 2 + (P("section", "ctx"),) + (weight,) * 14,
        check_vma=False,
    )
```

```python
from types import SimpleNamespace

import jax
import jax.numpy as jnp
from jax import lax
from jax.experimental import pallas as pl
from jax.experimental.pallas import tpu as pltpu
from jax.sharding import PartitionSpec as P

MESH = pl.DeviceIdType.MESH
BF = jnp.bfloat16
F32 = jnp.float32
I32 = jnp.int32
EPS = 1e-06
MASKED = -1e30


def spec(dtype, *shape):
    return shape, dtype


FAR_IN = dict(xin=spec(BF, 2, 4, 16, 1024), cot=spec(BF, 2, 4, 16, 1024))
NEAR_IN = dict(seg=spec(I32, 2, 1, 2048), gains_in=spec(BF, 1, 32))
FAR_LAYER_IN = dict(
    wq=spec(BF, 32, 256),
    wk=spec(BF, 32, 256),
    wv=spec(BF, 32, 256),
    wo=spec(BF, 32, 256),
    wg=spec(BF, 32, 704),
    wu=spec(BF, 32, 704),
)
NEAR_LAYER_IN = dict(wd=spec(BF, 88, 256))
FAR_OUT = dict(out=spec(BF, 2, 1, 64, 256), ing=spec(BF, 2, 1, 64, 256))
NEAR_OUT = dict(ogg=spec(F32, 1, 32))
FAR_LAYER_OUT = dict(
    oq=spec(F32, 32, 256),
    ok=spec(F32, 32, 256),
    ov=spec(F32, 32, 256),
    oo=spec(F32, 32, 256),
    og=spec(F32, 32, 704),
    ou=spec(F32, 32, 704),
    od=spec(F32, 88, 256),
)
COMMON = dict(
    hin=spec(BF, 2, 8, 16, 1024),
    pick=spec(BF, 704, 768),
    gst=spec(F32, 8, 128),
    gx=spec(F32, 3, 8, 128),
    g1=spec(F32, 8, 128),
    gyr=spec(F32, 8, 8, 128),
    gz=spec(F32, 4, 2, 8, 128),
    gains=spec(F32, 8, 1024),
    normed=spec(F32, 256, 1024),
    gg=spec(F32, 8, 1024),
    ggx=spec(F32, 3, 8, 1024),
    ggz=spec(F32, 4, 8, 256),
    ggzr=spec(F32, 3, 8, 256),
    ggy=spec(F32, 2, 8, 128),
    ggyr=spec(F32, 8, 8, 128),
    scores=spec(F32, 16, 128, 512),
    outst=spec(BF, 2, 4, 16, 256),
    ingst=spec(BF, 2, 4, 16, 256),
    outrv=spec(BF, 2, 64, 256),
    ingrv=spec(BF, 2, 64, 256),
    dmh=spec(BF, 256, 128),
    ds=spec(BF, 4, 512, 512),
    do2=spec(BF, 512, 128),
    dgu=spec(BF, 2, 128, 768),
)
LAYER = dict(
    qkst=spec(BF, 2, 32, 256),
    vst=spec(BF, 2, 32, 128),
    gus=spec(BF, 2, 32, 768),
    wds=spec(BF, 96, 256),
    cwo=spec(BF, 32, 256),
    cwd=spec(BF, 96, 256),
    wqk=spec(BF, 4, 8, 32, 256),
    wval=spec(BF, 4, 4, 2, 32, 128),
    wout=spec(BF, 4, 4, 32, 256),
    wgu=spec(BF, 4, 4, 2, 32, 768),
    wdn=spec(BF, 4, 4, 96, 256),
    kv=spec(BF, 4, 2, 2, 128, 256),
    q2=spec(BF, 512, 128),
    prob=spec(BF, 16, 128, 512),
    ot=spec(F32, 128, 256),
    gu=spec(F32, 256, 768),
    hid=spec(BF, 256, 384),
    dkv=spec(BF, 4, 2, 256, 256),
    dkvab=spec(BF, 2, 2, 256, 256),
    dkvc=spec(BF, 256, 256),
    dkvds=spec(BF, 256, 256),
    dkvd=spec(BF, 256, 256),
    dkves=spec(BF, 256, 256),
    dkve=spec(BF, 256, 256),
    gwk=spec(BF, 4, 8, 32, 128),
    gwv=spec(BF, 4, 4, 2, 32, 256),
    gwout=spec(BF, 4, 4, 32, 256),
    gwgu=spec(BF, 4, 4, 2, 32, 768),
    gwdn=spec(BF, 4, 4, 96, 256),
    rzk=spec(BF, 3, 8, 32, 128),
    ryv=spec(BF, 3, 4, 2, 32, 256),
    rzout=spec(BF, 3, 4, 32, 256),
    hygu=spec(BF, 2, 2, 2, 32, 768),
    bygu=spec(BF, 2, 4, 2, 32, 768),
    hzdn=spec(BF, 2, 2, 96, 256),
    bzdn=spec(BF, 2, 4, 96, 256),
    share=spec(F32, 8, 512),
    sk=spec(BF, 8, 32, 128),
    sv=spec(BF, 4, 2, 32, 256),
    sout=spec(BF, 4, 32, 256),
    sgu=spec(BF, 4, 2, 32, 768),
    sdn=spec(BF, 4, 96, 256),
    fk=spec(BF, 8, 32, 128),
    fv=spec(BF, 8, 32, 256),
    fgu=spec(BF, 8, 32, 768),
    yout=spec(BF, 4, 32, 256),
    ydn=spec(BF, 4, 96, 256),
    cout=spec(BF, 32, 256),
    cdn=spec(BF, 96, 256),
    fout=spec(BF, 32, 256),
    fdn=spec(BF, 96, 256),
)
SUB = dict(
    a=spec(BF, 2, 8, 16, 1024),
    h=spec(BF, 2, 16, 1024),
    gr=spec(BF, 2, 16, 1024),
    gb=spec(BF, 2, 8, 16, 1024),
)
EXCHANGE = dict(
    pb=spec(BF, 2, 2, 4, 16, 1024),
    sib=spec(BF, 2, 4, 16, 1024),
    xs=spec(BF, 2, 3, 16, 1024),
    xr=spec(BF, 2, 3, 16, 1024),
)
N_SEM = 282
N_LAYERS, N_SUB, N_EXCHANGE = 2, 4, 8


def groups():
    arguments = [(4, 0, FAR_IN), (0, 0, NEAR_IN)]
    results = [(4, 0, FAR_OUT), (0, 0, NEAR_OUT)]
    scratch = [(0, 0, COMMON), (0, 0, FAR_IN), (0, 0, FAR_OUT)]
    for l in range(N_LAYERS):
        arguments += [(5, l, FAR_LAYER_IN), (1, l, NEAR_LAYER_IN)]
        results += [(5, l, FAR_LAYER_OUT)]
        scratch += [(1, l, LAYER), (1, l, FAR_LAYER_IN), (1, l, FAR_LAYER_OUT)]
    scratch += [(2, i, SUB) for i in range(N_SUB)] + [(3, n, EXCHANGE) for n in range(N_EXCHANGE)]
    return arguments, results, scratch


def named(refs):
    spaces = [[SimpleNamespace() for _ in range(n)] for n in (1, N_LAYERS, N_SUB, N_EXCHANGE, 1, N_LAYERS)]
    left = list(refs)
    for group in groups():
        for kind, index, specs in group:
            for name in specs:
                setattr(spaces[kind][index], name, left.pop(0))
    return spaces[0][0], spaces[1], spaces[2], spaces[3], spaces[4][0], spaces[5]


def specs_of(group):
    return [entry for _, _, specs in group for entry in specs.values()]


def blocks_of(group):
    spaces = [pl.ANY if kind >= 4 else pltpu.VMEM for kind, _, specs in group for _ in specs]
    return [pl.BlockSpec(memory_space=space) for space in spaces]


def nn(a, b):
    return lax.dot_general(a, b, (((1,), (0,)), ((), ())), preferred_element_type=F32)


def nt(a, b):
    return lax.dot_general(a, b, (((1,), (1,)), ((), ())), preferred_element_type=F32)


def tn(a, b):
    return lax.dot_general(a, b, (((0,), (0,)), ((), ())), preferred_element_type=F32)


def normalize(h):
    inverse = lax.rsqrt(jnp.mean(h * h, axis=-1, keepdims=True) + EPS)
    return h * inverse, inverse


def kernel(*refs):
    R, L, S, X, far_r, far_l = named(refs[:-1])
    sems = refs[-1]
    used = [0]
    pending, kept = [], []
    outgoing = []

    def new():
        used[0] += 1
        return sems.at[used[0] - 1]

    x = lax.axis_index("section")
    c = lax.axis_index("ctx")
    z, y, k = lax.div(c, 8), lax.rem(lax.div(c, 2), 4), lax.rem(c, 2)
    t = 2 * x + k
    s = lax.div(y, 2)
    yy = lax.rem(y, 2)
    other = 1 - k

    def plus(v, j):
        return lax.rem(v + j, 4)

    def dev(xd, zd, yd, kd):
        return {"section": xd, "ctx": zd * 8 + yd * 2 + kd}

    def flip(j):
        return k if j % 2 == 0 else other

    sibling = dev(x, z, y, other)

    def put(src, dst, to, rsem):
        if len(pending) % 32 == 0:
            outgoing.append(new())
        copy = pltpu.make_async_remote_copy(
            src_ref=src, dst_ref=dst, send_sem=outgoing[-1], recv_sem=rsem, device_id=to, device_id_type=MESH
        )
        copy.start()
        pending.append(copy)

    def put_or_keep(mine, src, dst, to, rsem):
        copy = pltpu.make_async_remote_copy(
            src_ref=src, dst_ref=dst, send_sem=new(), recv_sem=rsem, device_id=to, device_id_type=MESH
        )

        @pl.when(mine)
        def _():
            pltpu.make_async_copy(src, dst, rsem).start()

        @pl.when(jnp.logical_not(mine))
        def _():
            copy.start()

        kept.append((mine, copy))

    def arrived(ref, sem):
        pltpu.make_async_copy(ref, ref, sem).wait()

    barrier = pltpu.get_barrier_semaphore()

    def greet(d):
        pl.semaphore_signal(barrier, inc=1, device_id=d, device_id_type=MESH)

    count = 0
    for j in range(4):
        for i in range(2):
            if (j, i) != (0, 0):
                greet(dev(plus(x, j), z, y, flip(i)))
                count += 1
            if j:
                greet(dev(x, z, plus(y, j), flip(i)))
                greet(dev(x, plus(z, j), y, flip(i)))
                count += 2
            greet(dev(plus(x, j), 3 - z, 3 - y, flip(i)))
            count += 1
    crossing = jnp.where(x == z, 0, 1)

    @pl.when(x != z)
    def _():
        greet(dev(z, x, y, k))

    def fetch(src, dst):
        copy = pltpu.make_async_copy(src, dst, new())
        copy.start()
        return copy

    def fetch_att(l):
        ends = ((far_l[l].wq, L[l].wq), (far_l[l].wk, L[l].wk), (far_l[l].wv, L[l].wv), (far_l[l].wo, L[l].wo))
        return [fetch(src, dst) for src, dst in ends]

    def wait_for(copies):
        for copy in copies:
            copy.wait()

    coming = fetch_att(0)
    xin_coming = fetch(far_r.xin, R.xin)
    later = fetch_att(1) + [fetch(far_r.cot, R.cot)]
    for l in range(2):
        later += [fetch(far_l[l].wg, L[l].wg), fetch(far_l[l].wu, L[l].wu)]
    leaving = []

    def leave(src, dst):
        leaving.append(fetch(src, dst))

    def pack_att(l):
        for i in range(2):
            L[l].qkst[i, :, 0:128] = L[l].wq[:, 128 * i : 128 * i + 128]
            L[l].qkst[i, :, 128:256] = L[l].wk[:, 128 * i : 128 * i + 128]
            L[l].vst[i] = L[l].wv[:, 128 * i : 128 * i + 128]

    def pack_rest():
        lane = lax.broadcasted_iota(I32, (1, 768), 1)
        half = (lane >= 384).astype(I32)
        place = lane - 384 * half
        group = (place >= 96).astype(I32) + (place >= 192).astype(I32) + (place >= 288).astype(I32)
        place = place - 96 * group
        unit = jnp.where(place < 88, 352 * half + 88 * group + place, -1)
        R.pick[...] = (lax.broadcasted_iota(I32, (704, 768), 0) == unit).astype(F32).astype(BF)
        stacked = jnp.concatenate([w[...] for l in range(2) for w in (L[l].wg, L[l].wu)], axis=0)
        stacked = nn(stacked, R.pick[...]).astype(BF)
        for l in range(2):
            for i in range(2):
                for n in range(2):
                    rows = stacked[64 * l + 32 * n : 64 * l + 32 * n + 32, 384 * i : 384 * i + 384]
                    L[l].gus[i, :, 384 * n : 384 * n + 384] = rows
            L[l].wds[0:88, :] = L[l].wd[...]
            L[l].wds[88:96, :] = jnp.zeros((8, 256), BF)
        pack_att(1)
        R.gg[...] = jnp.zeros((8, 1024), F32)

    wait_for(coming)
    pack_att(0)
    column = lax.broadcasted_iota(I32, (32, 128), 1) - 32 * lax.rem(c, 4)
    spot = (lax.broadcasted_iota(I32, (32, 128), 0) == column).astype(F32).astype(BF)
    piece = nn(jnp.broadcast_to(R.gains_in[...].astype(F32), (8, 32)).astype(BF), spot)
    R.gst[...] = jnp.where(lax.broadcasted_iota(I32, (8, 128), 0) == x, piece, 0.0)
    pl.semaphore_wait(barrier, count + crossing)

    W = [SimpleNamespace(), SimpleNamespace()]
    G = [SimpleNamespace(), SimpleNamespace()]
    partner = dev(x, z, y + 1 - 2 * yy, k)
    mate = 1 - yy
    slot_m = 2 * yy + k

    def keep(src, dst, sem):
        pltpu.make_async_copy(src, dst, sem).start()

    def to_z(src, dst, js=(1, 3, 2)):
        sem = new()
        for j in js:
            put(src, dst, dev(x, plus(z, j), y, k), sem)
        return sem

    def to_y(src, dst, js=(1, 3, 2)):
        sem = new()
        for j in js:
            put(src, dst, dev(x, z, plus(y, j), k), sem)
        return sem

    def qk_first(l):
        src, dst = L[l].qkst, L[l].wqk.at[z, 2 * y + k]
        sem = W[l].qk = new()
        keep(src.at[k], dst, sem)
        for j in (2, 6, 4, 3, 7, 5, 1):
            put(src.at[flip(j)], dst, dev(x, z, plus(y, j // 2), flip(j)), sem)

    def qk_second(l):
        w = L[l].wqk
        arrived(w.at[z], W[l].qk)
        W[l].qk = to_z(w.at[z], w.at[z])

    def z_first(src, w):
        sem, dst = new(), w.at[z, y, k]
        keep(src.at[k], dst, sem)
        for j in (2, 6, 4, 3, 7, 5, 1):
            put(src.at[flip(j)], dst, dev(x, plus(z, j // 2), y, flip(j)), sem)
        return sem

    def v_second(l):
        w = L[l].wval
        arrived(w.at[:, y], W[l].v)
        W[l].v = to_y(w.at[:, y], w.at[:, y])

    def at_y(j):
        return dev(x, z, plus(y, j), k)

    def at_z(j):
        return dev(x, plus(z, j), y, k)

    def ring_start(block, v, at, direct=False):
        sems_ = [new() for _ in range(4)]
        put(block(v), block(v), at(1), sems_[0])
        put(block(v), block(v), at(3), sems_[1])
        if direct:
            put(block(v), block(v), at(2), sems_[2])
        return block, v, at, sems_, direct

    def ring_relay(state):
        block, v, at, sems_, direct = state
        if direct:
            return
        before, after = plus(v, 3), plus(v, 1)
        arrived(block(before), sems_[0])
        put(block(before, 0), block(before, 0), at(1), sems_[2])
        arrived(block(after), sems_[1])
        put(block(after, 1), block(after, 1), at(3), sems_[3])

    def ring_end(state):
        block, v, at, sems_, direct = state
        far = plus(v, 2)
        if direct:
            arrived(block(plus(v, 3)), sems_[0])
            arrived(block(plus(v, 1)), sems_[1])
            arrived(block(far), sems_[2])
            return
        arrived(block(far, 0), sems_[2])
        arrived(block(far, 1), sems_[3])

    def halved(h):
        return slice(None) if h is None else slice(2 * h, 2 * h + 2)

    def gate_start(l):
        arrived(L[l].wgu.at[:, y], W[l].gu)
        W[l].gate = ring_start(lambda v, h=None: L[l].wgu.at[halved(h), v, :, :, 0:384], y, at_y)

    def up_start(l):
        W[l].up = ring_start(lambda v, h=None: L[l].wgu.at[halved(h), v, :, :, 384:768], y, at_y)

    def down_start(l):
        arrived(L[l].wdn.at[z], W[l].d)
        W[l].d = ring_start(lambda v, h=None: L[l].wdn.at[v, halved(h)], z, at_z, True)

    def cross_first(src, dst):
        sem = new()
        put_or_keep(x == z, src, dst, dev(z, x, y, k), sem)
        return sem

    def cross_second(src, w, sem):
        arrived(src, sem)
        sem, dst = new(), w.at[z, slot_m]
        put_or_keep(s == k, src, dst, dev(x, z, y, s), sem)
        for j in (1, 3, 2):
            put(src, dst, dev(x, z, plus(y, j), s), sem)
        return sem

    def cross_third(w, sem):
        arrived(w.at[z], sem)
        return to_z(w.at[z], w.at[z])

    streams = (0, 1)
    sums = {}

    def rs_start(n, i, part):
        pb, sib = X[n].pb, X[n].sib
        for r in range(8):
            pb[i, r % 2, r // 2] = part[16 * r : 16 * r + 16].astype(BF)
        sem = sums[n, i] = new()
        for j in (1, 3, 2, 0):
            xd = plus(x, j)
            put(pb.at[i, other, xd], sib.at[i, xd], sibling, sem)

    def rs_mid(n, i):
        pb, sib, xs, xr = X[n].pb, X[n].sib, X[n].xs, X[n].xr
        arrived(sib.at[i], sums[n, i])
        sem = sums[n, i] = new()
        for j in (1, 3, 2):
            xd = plus(x, j)
            xs[i, j - 1] = (pb[i, k, xd].astype(F32) + sib[i, xd].astype(F32)).astype(BF)
            put(xs.at[i, j - 1], xr.at[i, j - 1], dev(xd, z, y, k), sem)

    def rs_end(n, i):
        pb, sib, xr = X[n].pb, X[n].sib, X[n].xr
        total = pb[i, k, x].astype(F32) + sib[i, x].astype(F32)
        arrived(xr.at[i], sums[n, i])
        for j in (1, 3, 2):
            total += xr[i, j - 1].astype(F32)
        return total

    def gather_start(buf, i, block):
        buf[i, t] = block
        mine = buf.at[i, t]
        rx = {j: new() for j in (1, 3, 2)}
        rk = new()
        for j in (1, 3, 2):
            put(mine, mine, dev(plus(x, j), z, y, k), rx[j])
        put(mine, mine, sibling, rk)
        return buf, i, rx, rk

    def gather_forward(state):
        if state is not None:
            buf, i, rx, rk = state
            for j in (1, 3, 2):
                slot = buf.at[i, 2 * plus(x, 4 - j) + k]
                arrived(slot, rx[j])
                put(slot, slot, sibling, rk)

    def gather_finish(state):
        if state is not None:
            buf, i, rx, rk = state
            arrived(buf.at[i, 0:4], rk)

    def nothing():
        pass

    def opened(states, n, work, early=nothing):
        gather_finish(states[0])
        work(0)
        gather_forward(states[1])
        rs_mid(n, 0)
        early()
        gather_finish(states[1])
        work(1)
        rs_mid(n, 1)

    def closed(rows_of, buf, between):
        first = gather_start(buf, 0, rows_of(0))
        second = gather_start(buf, 1, rows_of(1))
        between()
        gather_forward(first)
        return first, second

    def to_owners(i, rows, stage, landing, sem):
        for r in range(4):
            stage[i, r] = rows[:, 256 * r : 256 * r + 256]
        zd, yd = (z, y) if i == 0 else (3 - z, 3 - y)
        kd = lax.div(x, 2)
        first_row = pl.multiple_of(16 * (2 * lax.rem(x, 2) + k), 16)
        dst = landing.at[s, pl.ds(first_row, 16)]
        for j in range(4):
            xd = plus(x, j)
            if i == 0 and j == 0:
                put_or_keep(kd == k, stage.at[i, xd], dst, dev(xd, zd, yd, kd), sem)
            else:
                put(stage.at[i, xd], dst, dev(xd, zd, yd, kd), sem)

    def spread_tokens(src, dst):
        rows = pl.ds(4 * k, 4)
        close, mirrored = new(), new()
        put(src.at[1 - s], dst.at[1, rows], dev(x, 3 - z, 3 - y, k), mirrored)
        put(src.at[s], dst.at[0, rows], sibling, close)
        dst[0, rows] = src[s]
        return close, mirrored

    def spread_rest(dst, sems_):
        close, mirrored = sems_
        far = dst.at[1, pl.ds(4 * k, 4)]
        arrived(far, mirrored)
        put(far, far, sibling, close)
        arrived(dst.at[0], close)

    lane = lax.broadcasted_iota(I32, (1, 512), 1)
    own_block = 4 * z + y
    query_pos = 128 * jnp.where(lane < 256, own_block, 15 - own_block) + lax.rem(lane, 128)
    ids = R.seg[s]

    def tokens_to(n):
        return jnp.sum(jnp.where(ids <= n, 1.0, 0.0), axis=1, keepdims=True).astype(I32)

    first, second = tokens_to(0), tokens_to(1)
    query_start = jnp.where(query_pos < first, 0, jnp.where(query_pos < second, first, second))
    head_lane = lax.broadcasted_iota(I32, (128, 128), 1) < 64

    def two_heads(v):
        zero = jnp.zeros_like(v)
        return jnp.concatenate([jnp.where(head_lane, v, zero), jnp.where(head_lane, zero, v)], axis=0)

    def own_heads(vt):
        return jnp.concatenate([vt[0:64, 0:128], vt[64:128, 128:256]], axis=0)

    def gain_row(i):
        return R.gains[i : i + 1, :]

    def full(ref):
        return ref[...].reshape(256, 1024)

    def keys_of(l, zz):
        return L[l].kv[zz, :, :, :, 0:128].reshape(512, 128)

    def values_of(l, zz):
        return L[l].kv[zz, :, :, :, 128:256].reshape(512, 128)

    def attention_forward(l, states, hook, late):
        kv = L[l].kv
        direct, relayed = ([{j: new() for j in (1, 2, 3)} for _ in streams] for _ in range(2))
        from_mate = [new() for _ in streams]
        for i in streams:
            if i == 1:
                gather_forward(states[1])
            gather_finish(states[i])
            a = S[2 * l].a[i].reshape(128, 1024)
            w = L[l].wqk
            if i == 0:
                arrived(w.at[0:3], W[l].qk)
            qk = nn(a, w[...].reshape(1024, 256))
            w = L[l].wval
            if i == 0:
                arrived(w.at[0:3], W[l].v)
            u = nn(a, w[...].reshape(1024, 128))
            if l == 0:
                values = u.astype(BF)
            else:
                values = (0.5 * u + 0.5 * L[0].kv[z, yy, i, :, 128:256].astype(F32)).astype(BF)
            kv[z, yy, i, :, 0:128] = qk[:, 128:256].astype(BF)
            kv[z, yy, i, :, 128:256] = values
            own = kv.at[z, yy, i]
            for j in (1, 3):
                put(own, own, dev(x, plus(z, j), y, k), direct[i][j])
            put(own, own, partner, from_mate[i])
            put(own, own, dev(x, plus(z, 2), y, k), direct[i][2])
            L[l].q2[256 * i : 256 * i + 256, :] = two_heads((qk[:, 0:128].astype(BF) * 0.125).astype(BF))
        for i in streams:
            near = kv.at[z, mate, i]
            arrived(near, from_mate[i])
            for j in (1, 3):
                put(near, near, dev(x, plus(z, j), y, k), relayed[i][j])
        scores = R.scores
        top = jnp.full((1, 512), MASKED, F32)
        for j in (0, 3, 1, 2):
            zz = plus(z, j)
            for i in streams:
                if j % 2:
                    arrived(kv.at[zz, yy, i], direct[i][4 - j])
                    arrived(kv.at[zz, mate, i], relayed[i][4 - j])
                elif j:
                    arrived(kv.at[zz, mate, i], relayed[i][2])
            if j == 1:
                hook()
            scores[4 * j : 4 * j + 4] = nt(keys_of(l, zz), L[l].q2[...]).reshape(4, 128, 512)

            def mask(i, top, j=j, zz=zz):
                block = 4 * zz + 2 * s + lax.div(i, 2)
                base = 128 * (block + lax.rem(i, 2) * (15 - 2 * block))
                row = lax.broadcasted_iota(I32, (128, 512), 0)
                seen = (row >= query_start - base) & (row <= query_pos - base)
                v = jnp.where(seen, scores[4 * j + i], MASKED)
                scores[4 * j + i] = v
                return jnp.maximum(top, jnp.max(v, axis=0, keepdims=True))

            top = lax.fori_loop(0, 4, mask, top)
            if j == 0:
                for i in streams:
                    opposite = kv.at[plus(z, 2), yy, i]
                    arrived(opposite, direct[i][2])
                    put(opposite, opposite, partner, relayed[i][2])
        prob = L[l].prob
        for i in streams:
            lanes = slice(256 * i, 256 * i + 256)
            high = top[:, lanes]

            def expo(r, total):
                v = jnp.exp(scores[r, :, lanes] - high)
                prob[r, :, lanes] = v.astype(BF)
                return total + jnp.sum(v, axis=0, keepdims=True)

            share = 1.0 / lax.fori_loop(0, 16, expo, jnp.zeros((1, 256), F32))
            L[l].share[0:1, lanes] = share
            ot = jnp.zeros((128, 256), F32)
            for j in range(4):
                ot += tn(values_of(l, plus(z, j)), prob[4 * j : 4 * j + 4, :, lanes].reshape(512, 256))
            ot = ot * share
            ot = own_heads(ot)
            L[l].ot[:, 128 * i : 128 * i + 128] = ot
            o = jnp.transpose(ot).astype(BF)
            if i == 0:
                arrived(L[l].wout.at[0:3], W[l].o)
            part = jnp.concatenate([nn(o, L[l].wout[r].reshape(128, 256)) for r in range(4)], axis=1)
            rs_start(2 * l, i, part)
        for i in streams:
            rs_mid(2 * l, i)
        late()

    def feedforward_forward(l, states, early, hook):
        w = L[l].wgu

        def work(i):
            a = S[2 * l + 1].a[i].reshape(128, 1024)
            if i == 0:
                ring_end(W[l].gate)
            gate = nn(a, w[:, :, :, :, 0:384].reshape(1024, 384))
            if i == 0:
                ring_end(W[l].up)
            up = nn(a, w[:, :, :, :, 384:768].reshape(1024, 384))
            rows = slice(128 * i, 128 * i + 128)
            L[l].gu[rows, 0:384] = gate
            L[l].gu[rows, 384:768] = up
            hidden = (gate * jax.nn.sigmoid(gate) * up).astype(BF)
            L[l].hid[rows, :] = hidden
            if i == 0:
                ring_end(W[l].d)
            part = jnp.concatenate([nn(hidden, L[l].wdn[r].reshape(384, 256)) for r in range(4)], axis=1)
            rs_start(2 * l + 1, i, part)

        opened(states, 2 * l + 1, work, early)
        hook()

    def next_rows(n, between=nothing):
        def rows_of(i):
            rows = (S[n].h[i].astype(F32) + rs_end(n, i)).astype(BF)
            S[n + 1].h[i] = rows
            normed, _ = normalize(rows.astype(F32))
            return (normed * gain_row(n + 1)).astype(BF)

        return closed(rows_of, S[n + 1].a, between)

    def norm_backward(n, i):
        da = rs_end(4 + n, i)
        normed, inverse = normalize(S[n].h[i].astype(F32))
        gain_part = jnp.sum(da * normed, axis=0, keepdims=True)
        if n == 0:
            pass
        elif i == 0:
            R.gg[n : n + 1, :] = gain_part
        else:
            R.gg[n : n + 1, :] += gain_part
        scaled = da * gain_row(n)
        mixed = scaled - normed * jnp.mean(scaled * normed, axis=-1, keepdims=True)
        return (S[n].gr[i].astype(F32) + inverse * mixed).astype(BF)

    def hand_back(n, between=nothing):
        def rows_of(i):
            rows = norm_backward(n, i)
            S[n - 1].gr[i] = rows
            return rows

        return closed(rows_of, S[n - 1].gb, between)

    def send_z(g, landing):
        sem = new()
        for j in (1, 3, 2):
            zd = plus(z, j)
            put(g.at[zd], landing.at[j - 1], dev(x, zd, y, k), sem)
        return sem

    def send_y(g, landing):
        sem = new()
        for j in (1, 3, 2):
            yd = plus(y, j)
            put(g.at[:, yd], landing.at[j - 1], dev(x, z, yd, k), sem)
        return sem

    def attention_backward(l, states, hook):
        n = 2 * l
        wo, dkv, prob = L[l].wout, L[l].dkv, L[l].prob
        ab, own_ab, c_sem = {j: new() for j in (1, 3)}, {j: new() for j in (1, 3)}, new()
        dq = []
        for i in streams:
            if i == 1:
                gather_forward(states[1])
            gather_finish(states[i])
            gb = S[n].gb[i].reshape(128, 1024)
            dot_ = nt(wo[0].reshape(128, 256), gb[:, 0:256])
            for r in range(1, 4):
                dot_ += nt(wo[r].reshape(128, 256), gb[:, 256 * r : 256 * r + 256])
            dot_ = dot_.astype(BF).astype(F32)
            do2 = two_heads(jnp.transpose(dot_).astype(BF))
            share = L[l].share[0:1, 256 * i : 256 * i + 256]
            head_row = lax.broadcasted_iota(I32, (128, 128), 0) < 64
            scaled = dot_ * jnp.where(head_row, share[:, 0:128], share[:, 128:256])
            R.do2[256 * i : 256 * i + 256, :] = two_heads(jnp.transpose(scaled).astype(BF))
            prod = dot_ * L[l].ot[:, 128 * i : 128 * i + 128]
            delta = jnp.concatenate(
                [jnp.sum(prod[0:64], axis=0, keepdims=True), jnp.sum(prod[64:128], axis=0, keepdims=True)], axis=1
            )
            lanes = slice(256 * i, 256 * i + 256)
            dqt = jnp.zeros((128, 256), F32)
            for j in (2, 1, 3, 0):
                zz = plus(z, j)
                p = prob[4 * j : 4 * j + 4, :, lanes].reshape(512, 256)
                dp = nt(values_of(l, zz), do2)
                ds = (p.astype(F32) * ((dp - delta) * share)).astype(BF)
                R.ds[j, :, lanes] = ds
                if i == 1:
                    p = prob[4 * j : 4 * j + 4].reshape(512, 512)
                    dkv[zz, :, :, 0:128] = nn(R.ds[j], L[l].q2[...]).astype(BF).reshape(2, 256, 128)
                    dkv[zz, :, :, 128:256] = nn(p, R.do2[...]).astype(BF).reshape(2, 256, 128)
                    if j % 2:
                        put(dkv.at[zz, mate], L[l].dkvab.at[j // 2, mate], dev(x, zz, y, k), ab[j])
                    elif j:
                        put(dkv.at[zz, mate], L[l].dkvc, partner, c_sem)
                dqt += tn(keys_of(l, zz), ds)
                if i == 1 and j == 3:
                    for r in (1, 3):
                        put(dkv.at[plus(z, r), yy], L[l].dkvab.at[r // 2, yy], dev(x, plus(z, r), y, k), own_ab[r])
            dq.append(jnp.transpose(own_heads(dqt) * 0.125).astype(BF))
        dq = jnp.concatenate(dq, axis=0)
        gb = full(S[n].gb)
        arrived(L[l].dkvc, c_sem)
        far = plus(z, 2)
        L[l].dkvds[...] = (dkv[far, yy].astype(F32) + L[l].dkvc[...].astype(F32)).astype(BF)
        d_sem, e_sem = new(), new()
        put(L[l].dkvds, L[l].dkvd, dev(x, far, y, k), d_sem)
        got = L[l].dkvab
        arrived(got.at[0, mate], ab[1])
        arrived(got.at[1, mate], ab[3])
        L[l].dkves[...] = (dkv[z, mate].astype(F32) + got[0, mate].astype(F32) + got[1, mate].astype(F32)).astype(BF)
        put(L[l].dkves, L[l].dkve, partner, e_sem)
        gw = L[l].gwout
        otb = L[l].ot[...].astype(BF)
        for i in range(4):
            gw[i] = nn(otb, gb[:, 256 * i : 256 * i + 256]).astype(BF).reshape(4, 32, 256)
        at = jnp.transpose(full(S[n].a))
        if l == 0:
            G[l].o = send_z(L[l].gwout, L[l].rzout)
        arrived(got.at[0, yy], own_ab[1])
        arrived(got.at[1, yy], own_ab[3])
        tot = dkv[z, yy].astype(F32) + got[0, yy].astype(F32) + got[1, yy].astype(F32)
        arrived(L[l].dkvd, d_sem)
        arrived(L[l].dkve, e_sem)
        tot = tot + L[l].dkvd[...].astype(F32) + L[l].dkve[...].astype(F32)
        dk = tot[:, 0:128].astype(BF)
        dvals = tot[:, 128:256]
        if l == 1:
            half = 0.5 * dvals.astype(BF).astype(F32)
            du = half.astype(BF)
            R.dmh[...] = du
        else:
            du = (dvals + R.dmh[...].astype(F32)).astype(BF)
        def send_grads():
            grads = nn(at, jnp.concatenate([dq, du, dk], axis=1)).astype(BF)
            L[l].gwv[...] = grads[:, 0:256].reshape(4, 4, 2, 32, 256)
            L[l].gwk[...] = grads[:, 256:384].reshape(4, 8, 32, 128)
            G[l].k = send_z(L[l].gwk, L[l].rzk)
            G[l].v = send_y(L[l].gwv, L[l].ryv)

        if l == 0:
            send_grads()
        for i in streams:
            rows = slice(128 * i, 128 * i + 128)
            da = nt(jnp.concatenate([dq[rows], dk[rows]], axis=1), L[l].wqk[...].reshape(1024, 256))
            da += nt(du[rows], L[l].wval[...].reshape(1024, 128))
            rs_start(4 + n, i, da)
            if l == 0:
                gain_part = jnp.sum(da * R.normed[rows, :], axis=0, keepdims=True)
                if i == 0:
                    R.gg[0:1, :] = gain_part
                else:
                    R.gg[0:1, :] += gain_part
        if l == 0:
            for j in (1, 3, 2):
                put(R.gg, R.ggx.at[j - 1], dev(plus(x, j), z, y, k), landed.gx)
        for i in streams:
            rs_mid(4 + n, i)
        if l == 1:
            send_grads()
        if l == 1:
            G[l].o = send_z(L[l].gwout, L[l].rzout)
        hook()

    def feedforward_backward(l, states, hook):
        n = 2 * l + 1

        def work(i):
            gb = S[n].gb[i].reshape(128, 1024)
            wd = L[l].wdn
            dhid = nt(gb[:, 0:256], wd[0].reshape(384, 256))
            for r in range(1, 4):
                dhid += nt(gb[:, 256 * r : 256 * r + 256], wd[r].reshape(384, 256))
            gu = L[l].gu[128 * i : 128 * i + 128, :]
            gate, up = gu[:, 0:384], gu[:, 384:768]
            sig = jax.nn.sigmoid(gate)
            dgate = dhid * up * sig * (1.0 + gate * (1.0 - sig))
            dup = dhid * (gate * sig)
            dgu = jnp.concatenate([dgate.astype(BF), dup.astype(BF)], axis=1)
            R.dgu[i] = dgu
            rs_start(4 + n, i, nt(dgu, L[l].wgu[...].reshape(1024, 768)))

        opened(states, 4 + n, work)
        at = jnp.transpose(full(S[n].a))
        gw = L[l].gwgu
        gw[...] = nn(at, R.dgu[...].reshape(256, 768)).astype(BF).reshape(4, 4, 2, 32, 768)
        far = plus(y, 2)
        G[l].g = [new() for _ in range(4)]
        put(gw.at[0:2, far], L[l].hygu.at[0], at_y(1), G[l].g[0])
        put(gw.at[2:4, far], L[l].hygu.at[1], at_y(3), G[l].g[1])
        gb = full(S[n].gb)
        ht = jnp.transpose(L[l].hid[...])
        gw = L[l].gwdn
        for i in range(4):
            gw[i] = nn(ht, gb[:, 256 * i : 256 * i + 256]).astype(BF).reshape(4, 96, 256)
        far = plus(z, 2)
        G[l].d = [new() for _ in range(4)]
        put(gw.at[far, 0:2], L[l].hzdn.at[0], at_z(1), G[l].d[0])
        put(gw.at[far, 2:4], L[l].hzdn.at[1], at_z(3), G[l].d[1])
        hook()

    def ff_push(l):
        gu, dn, hg, hd = L[l].gwgu, L[l].gwdn, L[l].hygu, L[l].hzdn
        for h, j in ((0, 1), (1, 3)):
            yd, zd, half = plus(y, j), plus(z, j), slice(2 * h, 2 * h + 2)
            arrived(hg.at[h], G[l].g[h])
            gu[half, yd] = (gu[half, yd].astype(F32) + hg[h].astype(F32)).astype(BF)
            put(gu.at[:, yd], L[l].bygu.at[h], at_y(j), G[l].g[2 + h])
            arrived(hd.at[h], G[l].d[h])
            dn[zd, half] = (dn[zd, half].astype(F32) + hd[h].astype(F32)).astype(BF)
            put(dn.at[zd], L[l].bzdn.at[h], at_z(j), G[l].d[2 + h])

    def summed(own, got):
        return own.astype(F32) + got[0].astype(F32) + got[1].astype(F32) + got[2].astype(F32)

    def rows_back(st, land):
        sem = new()
        for j in range(4):
            m = plus(slot_m, j)
            to = dev(x, z, 2 * k + lax.div(m, 2), lax.rem(m, 2))
            if j == 0:
                put_or_keep(s == k, st.at[m], land.at[y], to, sem)
            else:
                put(st.at[m], land.at[y], to, sem)
        return sem

    def four(land):
        return land[0].astype(F32) + land[1].astype(F32) + land[2].astype(F32) + land[3].astype(F32)

    def out_second(l):
        arrived(L[l].rzout, G[l].o)
        L[l].sout[...] = summed(L[l].gwout[z], L[l].rzout).astype(BF)
        G[l].o = rows_back(L[l].sout, L[l].yout)

    def out_third(l):
        arrived(L[l].yout, G[l].o)
        L[l].cout[...] = four(L[l].yout).astype(BF)
        G[l].o = cross_first(L[l].cout, L[l].fout)

    def out_end(l):
        arrived(L[l].fout, G[l].o)
        L[l].oo[...] = L[l].fout[...].astype(F32)
        leave(L[l].oo, far_l[l].oo)

    def down_second(l):
        got = L[l].bzdn
        arrived(got.at[0], G[l].d[2])
        arrived(got.at[1], G[l].d[3])
        L[l].sdn[...] = (L[l].gwdn[z].astype(F32) + got[0].astype(F32) + got[1].astype(F32)).astype(BF)
        G[l].d = rows_back(L[l].sdn, L[l].ydn)

    def down_third(l):
        arrived(L[l].ydn, G[l].d)
        L[l].cdn[...] = four(L[l].ydn).astype(BF)
        G[l].d = cross_first(L[l].cdn, L[l].fdn)

    def down_end(l):
        arrived(L[l].fdn, G[l].d)
        L[l].od[...] = L[l].fdn[0:88, :].astype(F32)
        leave(L[l].od, far_l[l].od)

    def rows_y(g, got, st, land, sem):
        arrived(got, sem)
        st[...] = summed(g[z], got).astype(BF)
        sem = new()
        land[0] = st[2 * y + k]
        for j in (2, 6, 4, 3, 7, 5, 1):
            yd, kd = plus(y, j // 2), flip(j)
            put(st.at[2 * yd + kd], land.at[j], dev(x, z, yd, kd), sem)
        return sem

    def rows_z(st, land):
        sem = new()
        land[0] = st[z, k]
        for j in (2, 6, 4, 3, 7, 5, 1):
            zd, kd = plus(z, j // 2), flip(j)
            put(st.at[zd, kd], land.at[j], dev(x, zd, y, kd), sem)
        return sem

    def halves(land, sem):
        if sem is not None:
            arrived(land.at[1:8], sem)
        own = land[0].astype(F32) + land[2].astype(F32) + land[4].astype(F32) + land[6].astype(F32)
        far = land[1].astype(F32) + land[3].astype(F32) + land[5].astype(F32) + land[7].astype(F32)
        return jnp.where(k == 0, own, far), jnp.where(k == 0, far, own)

    def k_second(l):
        G[l].k = rows_y(L[l].gwk, L[l].rzk, L[l].sk, L[l].fk, G[l].k)

    def v_grad_second(l):
        g, got, st = L[l].gwv, L[l].ryv, L[l].sv
        arrived(got, G[l].v)
        for i in range(4):
            own = g[i, y].astype(F32) + got[0, i].astype(F32) + got[1, i].astype(F32) + got[2, i].astype(F32)
            st[i] = own.astype(BF)
        G[l].v = rows_z(st, L[l].fv)

    def gu_grad_second(l):
        g, got, st = L[l].gwgu, L[l].bygu, L[l].sgu
        arrived(got.at[0], G[l].g[2])
        arrived(got.at[1], G[l].g[3])
        for i in range(4):
            st[i] = (g[i, y].astype(F32) + got[0, i].astype(F32) + got[1, i].astype(F32)).astype(BF)
        G[l].g = rows_z(st, L[l].fgu)

    def att_end(l):
        f = far_l[l]
        arrived(L[l].fv.at[1:8], G[l].v)
        for land, result, sem, to in (
            (L[l].fk, L[l].ok, G[l].k, f.ok),
            (L[l].fv.at[:, :, 0:128], L[l].oq, None, f.oq),
            (L[l].fv.at[:, :, 128:256], L[l].ov, None, f.ov),
        ):
            low, high = halves(land, sem)
            result[:, 0:128] = low
            result[:, 128:256] = high
            leave(result, to)

    def gu_end(l):
        low, high = halves(L[l].fgu, G[l].g)
        both = jnp.concatenate(
            [
                jnp.concatenate([low[:, 0:384], high[:, 0:384]], axis=1),
                jnp.concatenate([low[:, 384:768], high[:, 384:768]], axis=1),
            ],
            axis=0,
        )
        main = both.astype(BF)
        rest = (both - main.astype(F32)).astype(BF)
        both = nt(main, R.pick[...]) + nt(rest, R.pick[...])
        L[l].og[...] = both[0:32]
        L[l].ou[...] = both[32:64]
        leave(L[l].og, far_l[l].og)
        leave(L[l].ou, far_l[l].ou)

    def nothing():
        pass

    def att_first(l):
        qk_first(l)
        W[l].v = z_first(L[l].vst, L[l].wval)
        W[l].o = cross_first(L[l].wo, L[l].cwo)

    def ff_first(l):
        W[l].gu = z_first(L[l].gus, L[l].wgu)
        W[l].d = cross_first(L[l].wds, L[l].cwd)

    qk_first(0)
    W[0].v = z_first(L[0].vst, L[0].wval)
    xin_coming.wait()
    in_sems = spread_tokens(R.xin, R.hin)
    gx_sem = new()
    for j in (1, 3, 2):
        put(R.gst, R.gx.at[j - 1], dev(plus(x, j), z, y, k), gx_sem)
    W[0].o = cross_first(L[0].wo, L[0].cwo)
    wait_for(later)
    pack_rest()
    ff_first(0)
    arrived(R.gx, gx_sem)
    R.g1[...] = R.gst[...] + R.gx[0] + R.gx[1] + R.gx[2]
    gy_sem = new()
    R.gyr[2 * y + k] = R.g1[...]
    for j in range(1, 8):
        put(R.g1, R.gyr.at[2 * y + k], dev(x, z, plus(y, j // 2), flip(j)), gy_sem)
    qk_second(0)
    v_second(0)
    W[0].o = cross_second(L[0].cwo, L[0].wout, W[0].o)
    arrived(R.gyr.at[0:7], gy_sem)
    for i in range(2):
        R.gz[z, i] = R.gyr[4 * i] + R.gyr[4 * i + 1] + R.gyr[4 * i + 2] + R.gyr[4 * i + 3]
    gz_sem = to_z(R.gz.at[z], R.gz.at[z])
    spread_rest(R.hin, in_sems)
    normed, _ = normalize(full(R.hin).astype(F32))
    R.normed[...] = normed
    for i in streams:
        S[0].h[i] = R.hin[i, t]
    gate_start(0)
    arrived(R.gz.at[0:3], gz_sem)
    R.gains[...] = jnp.concatenate([R.gz[i // 2, i % 2] for i in range(8)], axis=1)
    S[0].a[...] = (normed * gain_row(0)).astype(BF).reshape(2, 8, 16, 1024)
    W[0].o = cross_third(L[0].wout, W[0].o)
    W[0].d = cross_second(L[0].cwd, L[0].wdn, W[0].d)
    cot_sems = []

    def after_keys_0():
        ring_relay(W[0].gate)
        up_start(0)
        down_start(0)
        att_first(1)
        ff_first(1)

    def in_gather_0():
        ring_relay(W[0].up)
        ring_relay(W[0].d)

    def in_ff_0():
        qk_second(1)
        v_second(1)

    def after_ff_0():
        W[1].o = cross_second(L[1].cwo, L[1].wout, W[1].o)
        gate_start(1)
        W[1].d = cross_second(L[1].cwd, L[1].wdn, W[1].d)

    def in_gather_1():
        W[1].o = cross_third(L[1].wout, W[1].o)

    def after_keys_1():
        ring_relay(W[1].gate)
        up_start(1)
        down_start(1)

    def after_att_1():
        cot_sems.append(spread_tokens(R.cot, S[3].gb))

    def in_gather_2():
        ring_relay(W[1].up)
        ring_relay(W[1].d)

    def take_cotangent():
        spread_rest(S[3].gb, cot_sems[0])
        for i in streams:
            S[3].gr[i] = S[3].gb[i, t]

    landed = SimpleNamespace(out=new(), ing=new(), gx=new())

    def finish_outputs():
        for i in streams:
            rows = (S[3].h[i].astype(F32) + rs_end(3, i)).astype(BF)
            to_owners(i, rows, R.outst, R.outrv, landed.out)

    none = (None, None)
    attention_forward(0, none, after_keys_0, nothing)
    feedforward_forward(0, next_rows(0, in_gather_0), in_ff_0, after_ff_0)
    attention_forward(1, next_rows(1, in_gather_1), after_keys_1, after_att_1)
    feedforward_forward(1, next_rows(2, in_gather_2), nothing, take_cotangent)

    def ff_grads(l):
        gu_grad_second(l)
        down_second(l)

    def att_grads():
        out_second(1)
        k_second(1)
        v_grad_second(1)

    def last_grads():
        ff_grads(0)

    def after_grads_1():
        att_grads()
        ff_grads(1)

    def after_grads_0():
        last_grads()
        att_end(1)
        down_third(1)
        gu_end(1)

    feedforward_backward(1, none, finish_outputs)
    attention_backward(1, hand_back(3), lambda: ff_push(1))
    states = hand_back(2)
    feedforward_backward(0, states, after_grads_1)
    states = hand_back(1, lambda: ff_push(0))
    out_third(1)
    attention_backward(0, states, after_grads_0)
    arrived(R.ggx, landed.gx)
    gg = R.gg[...] + R.ggx[0] + R.ggx[1] + R.ggx[2]
    for i in range(4):
        R.ggz[i] = gg[:, 256 * i : 256 * i + 256]
    gg_sem = new()
    for j in (1, 3, 2):
        zd = plus(z, j)
        put(R.ggz.at[zd], R.ggzr.at[j - 1], dev(x, zd, y, k), gg_sem)
    for i in streams:
        to_owners(i, norm_backward(0, i), R.ingst, R.ingrv, landed.ing)
    arrived(R.ggzr, gg_sem)
    gg = R.ggz[z] + R.ggzr[0] + R.ggzr[1] + R.ggzr[2]
    R.ggy[0] = gg[:, 0:128]
    R.ggy[1] = gg[:, 128:256]
    gg_sem = new()
    R.ggyr[0] = R.ggy[s]
    for j in range(1, 8):
        yd = plus(y, j // 2)
        put(R.ggy.at[lax.div(yd, 2)], R.ggyr.at[j], dev(x, z, yd, flip(j)), gg_sem)
    k_second(0)
    v_grad_second(0)
    out_second(0)
    down_third(0)
    out_third(0)
    out_end(1)
    down_end(1)
    gu_end(0)
    arrived(R.outrv, landed.out)
    R.out[...] = R.outrv[...].reshape(2, 1, 64, 256)
    leave(R.out, far_r.out)
    arrived(R.ingrv, landed.ing)
    R.ing[...] = R.ingrv[...].reshape(2, 1, 64, 256)
    leave(R.ing, far_r.ing)
    att_end(0)
    out_end(0)
    down_end(0)
    arrived(R.ggyr.at[1:8], gg_sem)
    gg = R.ggyr[0]
    for j in range(1, 8):
        gg = gg + R.ggyr[j]
    gg = jnp.sum(jnp.where(lax.broadcasted_iota(I32, (8, 128), 0) == x, gg, 0.0), axis=0, keepdims=True)
    part = lax.rem(c, 4)
    gain = jnp.zeros((1, 32), F32)
    for i in range(4):
        gain += jnp.where(part == i, gg[:, 32 * i : 32 * i + 32], 0.0)
    R.ogg[...] = gain
    wait_for(leaving)
    for copy in pending:
        copy.wait_send()
    for mine, copy in kept:

        @pl.when(jnp.logical_not(mine))
        def _(copy=copy):
            copy.wait_send()

    assert used[0] <= N_SEM, used


def call(*args):
    arguments, results, scratch = groups()
    return pl.pallas_call(
        kernel,
        out_shape=[jax.ShapeDtypeStruct(shape, dtype) for shape, dtype in specs_of(results)],
        in_specs=blocks_of(arguments),
        out_specs=blocks_of(results),
        scratch_shapes=[pltpu.VMEM(shape, dtype) for shape, dtype in specs_of(scratch)]
        + [pltpu.SemaphoreType.DMA((N_SEM,))],
        compiler_params=pltpu.CompilerParams(
            collective_id=0, has_side_effects=True, vmem_limit_bytes=62 * 1024 * 1024
        ),
    )(*args)


def hand_out(*refs):
    n = len(refs) // 2
    copies = [pltpu.make_async_copy(refs[i], refs[n + i], refs[-1].at[i]) for i in range(n)]
    for copy in copies:
        copy.start()
    for copy in copies:
        copy.wait()


def body(inputs, cotangent, segment_ids, gains, *weights):
    first = (inputs.reshape(2, 4, 16, 1024), cotangent.reshape(2, 4, 16, 1024), segment_ids, gains)
    results = call(*first, *weights)
    anywhere = pl.BlockSpec(memory_space=pl.ANY)
    return tuple(
        pl.pallas_call(
            hand_out,
            out_shape=[jax.ShapeDtypeStruct(r.shape, r.dtype) for r in results],
            in_specs=[pl.BlockSpec(memory_space=pltpu.VMEM)] * len(results),
            out_specs=[anywhere] * len(results),
            scratch_shapes=[pltpu.SemaphoreType.DMA((len(results),))],
        )(*results)
    )


def solution(mesh):
    tokens = P(None, None, "ctx", None)
    weight = P("ctx", "section")
    return jax.shard_map(
        body,
        mesh=mesh,
        in_specs=(tokens, tokens, P(), P("section", "ctx")) + (weight,) * 14,
        out_specs=(P(None, None, "ctx", "section"),) * 2 + (P("section", "ctx"),) + (weight,) * 14,
        check_vma=False,
    )
```

```python
from types import SimpleNamespace

import jax
import jax.numpy as jnp
from jax import lax
from jax.experimental import pallas as pl
from jax.experimental.pallas import tpu as pltpu
from jax.sharding import PartitionSpec as P

MESH = pl.DeviceIdType.MESH
BF = jnp.bfloat16
F32 = jnp.float32
I32 = jnp.int32
EPS = 1e-06
MASKED = -1e30


def spec(dtype, *shape):
    return shape, dtype


FAR_IN = dict(xin=spec(BF, 2, 4, 16, 1024), cot=spec(BF, 2, 4, 16, 1024))
NEAR_IN = dict(seg=spec(I32, 2, 1, 2048), gains_in=spec(BF, 1, 32))
FAR_LAYER_IN = dict(
    wq=spec(BF, 32, 256),
    wk=spec(BF, 32, 256),
    wv=spec(BF, 32, 256),
    wo=spec(BF, 32, 256),
    wg=spec(BF, 32, 704),
    wu=spec(BF, 32, 704),
)
NEAR_LAYER_IN = dict(wd=spec(BF, 88, 256))
FAR_OUT = dict(out=spec(BF, 2, 1, 64, 256), ing=spec(BF, 2, 1, 64, 256))
NEAR_OUT = dict(ogg=spec(F32, 1, 32))
FAR_LAYER_OUT = dict(
    oq=spec(F32, 32, 256),
    ok=spec(F32, 32, 256),
    ov=spec(F32, 32, 256),
    oo=spec(F32, 32, 256),
    og=spec(F32, 32, 704),
    ou=spec(F32, 32, 704),
    od=spec(F32, 88, 256),
)
COMMON = dict(
    hin=spec(BF, 2, 8, 16, 1024),
    pick=spec(BF, 704, 768),
    gst=spec(F32, 8, 128),
    gx=spec(F32, 3, 8, 128),
    g1=spec(F32, 8, 128),
    gyr=spec(F32, 8, 8, 128),
    gz=spec(F32, 4, 2, 8, 128),
    gains=spec(F32, 8, 1024),
    normed=spec(F32, 256, 1024),
    gg=spec(F32, 8, 1024),
    ggx=spec(F32, 3, 8, 1024),
    ggz=spec(F32, 4, 8, 256),
    ggzr=spec(F32, 3, 8, 256),
    ggy=spec(F32, 2, 8, 128),
    ggyr=spec(F32, 8, 8, 128),
    scores=spec(F32, 16, 128, 512),
    outst=spec(BF, 2, 4, 16, 256),
    ingst=spec(BF, 2, 4, 16, 256),
    outrv=spec(BF, 2, 64, 256),
    ingrv=spec(BF, 2, 64, 256),
    dmh=spec(BF, 256, 128),
    ds=spec(BF, 4, 512, 512),
    do2=spec(BF, 512, 128),
    dgu=spec(BF, 2, 128, 768),
)
LAYER = dict(
    qkst=spec(BF, 2, 32, 256),
    vst=spec(BF, 2, 32, 128),
    gus=spec(BF, 2, 32, 768),
    wds=spec(BF, 96, 256),
    cwo=spec(BF, 32, 256),
    cwd=spec(BF, 96, 256),
    wqk=spec(BF, 4, 8, 32, 256),
    wval=spec(BF, 4, 4, 2, 32, 128),
    wout=spec(BF, 4, 4, 32, 256),
    wgu=spec(BF, 4, 4, 2, 32, 768),
    wdn=spec(BF, 4, 4, 96, 256),
    kv=spec(BF, 4, 2, 2, 128, 256),
    q2=spec(BF, 512, 128),
    prob=spec(BF, 16, 128, 512),
    ot=spec(F32, 128, 256),
    gu=spec(F32, 256, 768),
    hid=spec(BF, 256, 384),
    dkv=spec(BF, 4, 2, 256, 256),
    dkvab=spec(BF, 2, 2, 256, 256),
    dkvc=spec(BF, 256, 256),
    dkvds=spec(BF, 256, 256),
    dkvd=spec(BF, 256, 256),
    dkves=spec(BF, 256, 256),
    dkve=spec(BF, 256, 256),
    gwk=spec(BF, 4, 8, 32, 128),
    gwv=spec(BF, 4, 4, 2, 32, 256),
    gwout=spec(BF, 4, 4, 32, 256),
    gwgu=spec(BF, 4, 4, 2, 32, 768),
    gwdn=spec(BF, 4, 4, 96, 256),
    rzk=spec(BF, 3, 8, 32, 128),
    ryv=spec(BF, 3, 4, 2, 32, 256),
    rzout=spec(BF, 3, 4, 32, 256),
    hygu=spec(BF, 2, 2, 2, 32, 768),
    bygu=spec(BF, 2, 4, 2, 32, 768),
    hzdn=spec(BF, 2, 2, 96, 256),
    bzdn=spec(BF, 2, 4, 96, 256),
    share=spec(F32, 8, 512),
    sk=spec(BF, 8, 32, 128),
    sv=spec(BF, 4, 2, 32, 256),
    sout=spec(BF, 4, 32, 256),
    sgu=spec(BF, 4, 2, 32, 768),
    sdn=spec(BF, 4, 96, 256),
    fk=spec(BF, 8, 32, 128),
    fv=spec(BF, 8, 32, 256),
    fgu=spec(BF, 8, 32, 768),
    yout=spec(BF, 4, 32, 256),
    ydn=spec(BF, 4, 96, 256),
    cout=spec(BF, 32, 256),
    cdn=spec(BF, 96, 256),
    fout=spec(BF, 32, 256),
    fdn=spec(BF, 96, 256),
)
SUB = dict(
    a=spec(BF, 2, 8, 16, 1024),
    h=spec(BF, 2, 16, 1024),
    gr=spec(BF, 2, 16, 1024),
    gb=spec(BF, 2, 8, 16, 1024),
)
EXCHANGE = dict(
    pb=spec(BF, 2, 2, 4, 16, 1024),
    sib=spec(BF, 2, 4, 16, 1024),
    xs=spec(BF, 2, 3, 16, 1024),
    xr=spec(BF, 2, 3, 16, 1024),
)
N_SEM = 282
N_LAYERS, N_SUB, N_EXCHANGE = 2, 4, 8


def groups():
    arguments = [(4, 0, FAR_IN), (0, 0, NEAR_IN)]
    results = [(4, 0, FAR_OUT), (0, 0, NEAR_OUT)]
    scratch = [(0, 0, COMMON), (0, 0, FAR_IN), (0, 0, FAR_OUT)]
    for l in range(N_LAYERS):
        arguments += [(5, l, FAR_LAYER_IN), (1, l, NEAR_LAYER_IN)]
        results += [(5, l, FAR_LAYER_OUT)]
        scratch += [(1, l, LAYER), (1, l, FAR_LAYER_IN), (1, l, FAR_LAYER_OUT)]
    scratch += [(2, i, SUB) for i in range(N_SUB)] + [(3, n, EXCHANGE) for n in range(N_EXCHANGE)]
    return arguments, results, scratch


def named(refs):
    spaces = [[SimpleNamespace() for _ in range(n)] for n in (1, N_LAYERS, N_SUB, N_EXCHANGE, 1, N_LAYERS)]
    left = list(refs)
    for group in groups():
        for kind, index, specs in group:
            for name in specs:
                setattr(spaces[kind][index], name, left.pop(0))
    return spaces[0][0], spaces[1], spaces[2], spaces[3], spaces[4][0], spaces[5]


def specs_of(group):
    return [entry for _, _, specs in group for entry in specs.values()]


def blocks_of(group):
    spaces = [pl.ANY if kind >= 4 else pltpu.VMEM for kind, _, specs in group for _ in specs]
    return [pl.BlockSpec(memory_space=space) for space in spaces]


def nn(a, b):
    return lax.dot_general(a, b, (((1,), (0,)), ((), ())), preferred_element_type=F32)


def nt(a, b):
    return lax.dot_general(a, b, (((1,), (1,)), ((), ())), preferred_element_type=F32)


def tn(a, b):
    return lax.dot_general(a, b, (((0,), (0,)), ((), ())), preferred_element_type=F32)


def normalize(h):
    inverse = lax.rsqrt(jnp.mean(h * h, axis=-1, keepdims=True) + EPS)
    return h * inverse, inverse


def kernel(*refs):
    R, L, S, X, far_r, far_l = named(refs[:-1])
    sems = refs[-1]
    used = [0]
    pending, kept = [], []
    outgoing = []

    def new():
        used[0] += 1
        return sems.at[used[0] - 1]

    x = lax.axis_index("section")
    c = lax.axis_index("ctx")
    z, y, k = lax.div(c, 8), lax.rem(lax.div(c, 2), 4), lax.rem(c, 2)
    t = 2 * x + k
    s = lax.div(y, 2)
    yy = lax.rem(y, 2)
    other = 1 - k

    def plus(v, j):
        return lax.rem(v + j, 4)

    def dev(xd, zd, yd, kd):
        return {"section": xd, "ctx": zd * 8 + yd * 2 + kd}

    def flip(j):
        return k if j % 2 == 0 else other

    sibling = dev(x, z, y, other)

    def put(src, dst, to, rsem):
        if len(pending) % 32 == 0:
            outgoing.append(new())
        copy = pltpu.make_async_remote_copy(
            src_ref=src, dst_ref=dst, send_sem=outgoing[-1], recv_sem=rsem, device_id=to, device_id_type=MESH
        )
        copy.start()
        pending.append(copy)

    def put_or_keep(mine, src, dst, to, rsem):
        copy = pltpu.make_async_remote_copy(
            src_ref=src, dst_ref=dst, send_sem=new(), recv_sem=rsem, device_id=to, device_id_type=MESH
        )

        @pl.when(mine)
        def _():
            pltpu.make_async_copy(src, dst, rsem).start()

        @pl.when(jnp.logical_not(mine))
        def _():
            copy.start()

        kept.append((mine, copy))

    def arrived(ref, sem):
        pltpu.make_async_copy(ref, ref, sem).wait()

    barrier = pltpu.get_barrier_semaphore()

    def greet(d):
        pl.semaphore_signal(barrier, inc=1, device_id=d, device_id_type=MESH)

    count = 0
    for j in range(4):
        for i in range(2):
            if (j, i) != (0, 0):
                greet(dev(plus(x, j), z, y, flip(i)))
                count += 1
            if j:
                greet(dev(x, z, plus(y, j), flip(i)))
                greet(dev(x, plus(z, j), y, flip(i)))
                count += 2
            greet(dev(plus(x, j), 3 - z, 3 - y, flip(i)))
            count += 1
    crossing = jnp.where(x == z, 0, 1)

    @pl.when(x != z)
    def _():
        greet(dev(z, x, y, k))

    def fetch(src, dst):
        copy = pltpu.make_async_copy(src, dst, new())
        copy.start()
        return copy

    def fetch_att(l):
        ends = ((far_l[l].wq, L[l].wq), (far_l[l].wk, L[l].wk), (far_l[l].wv, L[l].wv), (far_l[l].wo, L[l].wo))
        return [fetch(src, dst) for src, dst in ends]

    def wait_for(copies):
        for copy in copies:
            copy.wait()

    coming = fetch_att(0)
    xin_coming = fetch(far_r.xin, R.xin)
    later = fetch_att(1) + [fetch(far_r.cot, R.cot)]
    for l in range(2):
        later += [fetch(far_l[l].wg, L[l].wg), fetch(far_l[l].wu, L[l].wu)]
    leaving = []

    def leave(src, dst):
        leaving.append(fetch(src, dst))

    def pack_att(l):
        for i in range(2):
            L[l].qkst[i, :, 0:128] = L[l].wq[:, 128 * i : 128 * i + 128]
            L[l].qkst[i, :, 128:256] = L[l].wk[:, 128 * i : 128 * i + 128]
            L[l].vst[i] = L[l].wv[:, 128 * i : 128 * i + 128]

    def pack_rest():
        lane = lax.broadcasted_iota(I32, (1, 768), 1)
        half = (lane >= 384).astype(I32)
        place = lane - 384 * half
        group = (place >= 96).astype(I32) + (place >= 192).astype(I32) + (place >= 288).astype(I32)
        place = place - 96 * group
        unit = jnp.where(place < 88, 352 * half + 88 * group + place, -1)
        R.pick[...] = (lax.broadcasted_iota(I32, (704, 768), 0) == unit).astype(F32).astype(BF)
        stacked = jnp.concatenate([w[...] for l in range(2) for w in (L[l].wg, L[l].wu)], axis=0)
        stacked = nn(stacked, R.pick[...]).astype(BF)
        for l in range(2):
            for i in range(2):
                for n in range(2):
                    rows = stacked[64 * l + 32 * n : 64 * l + 32 * n + 32, 384 * i : 384 * i + 384]
                    L[l].gus[i, :, 384 * n : 384 * n + 384] = rows
            L[l].wds[0:88, :] = L[l].wd[...]
            L[l].wds[88:96, :] = jnp.zeros((8, 256), BF)
        pack_att(1)
        R.gg[...] = jnp.zeros((8, 1024), F32)

    wait_for(coming)
    pack_att(0)
    column = lax.broadcasted_iota(I32, (32, 128), 1) - 32 * lax.rem(c, 4)
    spot = (lax.broadcasted_iota(I32, (32, 128), 0) == column).astype(F32).astype(BF)
    piece = nn(jnp.broadcast_to(R.gains_in[...].astype(F32), (8, 32)).astype(BF), spot)
    R.gst[...] = jnp.where(lax.broadcasted_iota(I32, (8, 128), 0) == x, piece, 0.0)
    pl.semaphore_wait(barrier, count + crossing)

    W = [SimpleNamespace(), SimpleNamespace()]
    G = [SimpleNamespace(), SimpleNamespace()]
    partner = dev(x, z, y + 1 - 2 * yy, k)
    mate = 1 - yy
    slot_m = 2 * yy + k

    def keep(src, dst, sem):
        pltpu.make_async_copy(src, dst, sem).start()

    def to_z(src, dst, js=(1, 3, 2)):
        sem = new()
        for j in js:
            put(src, dst, dev(x, plus(z, j), y, k), sem)
        return sem

    def to_y(src, dst, js=(1, 3, 2)):
        sem = new()
        for j in js:
            put(src, dst, dev(x, z, plus(y, j), k), sem)
        return sem

    def qk_first(l):
        src, dst = L[l].qkst, L[l].wqk.at[z, 2 * y + k]
        sem = W[l].qk = new()
        keep(src.at[k], dst, sem)
        for j in (2, 6, 4, 3, 7, 5, 1):
            put(src.at[flip(j)], dst, dev(x, z, plus(y, j // 2), flip(j)), sem)

    def qk_second(l):
        w = L[l].wqk
        arrived(w.at[z], W[l].qk)
        keys, queries = w.at[z, :, :, 128:256], w.at[z, :, :, 0:128]
        W[l].k = to_z(keys, keys)
        W[l].q = to_z(queries, queries)

    def z_first(src, w):
        sem, dst = new(), w.at[z, y, k]
        keep(src.at[k], dst, sem)
        for j in (2, 6, 4, 3, 7, 5, 1):
            put(src.at[flip(j)], dst, dev(x, plus(z, j // 2), y, flip(j)), sem)
        return sem

    def v_second(l):
        w = L[l].wval
        arrived(w.at[:, y], W[l].v)
        W[l].v = to_y(w.at[:, y], w.at[:, y])

    def at_y(j):
        return dev(x, z, plus(y, j), k)

    def at_z(j):
        return dev(x, plus(z, j), y, k)

    def ring_start(block, v, at, direct=False):
        sems_ = [new() for _ in range(4)]
        put(block(v), block(v), at(1), sems_[0])
        put(block(v), block(v), at(3), sems_[1])
        if direct:
            put(block(v), block(v), at(2), sems_[2])
        return block, v, at, sems_, direct

    def ring_relay(state):
        block, v, at, sems_, direct = state
        if direct:
            return
        before, after = plus(v, 3), plus(v, 1)
        arrived(block(before), sems_[0])
        put(block(before, 0), block(before, 0), at(1), sems_[2])
        arrived(block(after), sems_[1])
        put(block(after, 1), block(after, 1), at(3), sems_[3])

    def ring_end(state):
        block, v, at, sems_, direct = state
        far = plus(v, 2)
        if direct:
            arrived(block(plus(v, 3)), sems_[0])
            arrived(block(plus(v, 1)), sems_[1])
            arrived(block(far), sems_[2])
            return
        arrived(block(far, 0), sems_[2])
        arrived(block(far, 1), sems_[3])

    def halved(h):
        return slice(None) if h is None else slice(2 * h, 2 * h + 2)

    def gate_start(l):
        arrived(L[l].wgu.at[:, y], W[l].gu)
        W[l].gate = ring_start(lambda v, h=None: L[l].wgu.at[halved(h), v, :, :, 0:384], y, at_y)

    def up_start(l):
        W[l].up = ring_start(lambda v, h=None: L[l].wgu.at[halved(h), v, :, :, 384:768], y, at_y)

    def down_start(l):
        arrived(L[l].wdn.at[z], W[l].d)
        W[l].d = ring_start(lambda v, h=None: L[l].wdn.at[v, halved(h)], z, at_z, True)

    def cross_first(src, dst):
        sem = new()
        put_or_keep(x == z, src, dst, dev(z, x, y, k), sem)
        return sem

    def cross_second(src, w, sem):
        arrived(src, sem)
        sem, dst = new(), w.at[z, slot_m]
        put_or_keep(s == k, src, dst, dev(x, z, y, s), sem)
        for j in (1, 3, 2):
            put(src, dst, dev(x, z, plus(y, j), s), sem)
        return sem

    def cross_third(w, sem):
        arrived(w.at[z], sem)
        return to_z(w.at[z], w.at[z])

    streams = (0, 1)
    sums = {}

    def rs_start(n, i, part):
        pb, sib = X[n].pb, X[n].sib
        for r in range(8):
            pb[i, r % 2, r // 2] = part[16 * r : 16 * r + 16].astype(BF)
        sem = sums[n, i] = new()
        for j in (1, 3, 2, 0):
            xd = plus(x, j)
            put(pb.at[i, other, xd], sib.at[i, xd], sibling, sem)

    def rs_mid(n, i):
        pb, sib, xs, xr = X[n].pb, X[n].sib, X[n].xs, X[n].xr
        arrived(sib.at[i], sums[n, i])
        sem = sums[n, i] = new()
        for j in (1, 3, 2):
            xd = plus(x, j)
            xs[i, j - 1] = (pb[i, k, xd].astype(F32) + sib[i, xd].astype(F32)).astype(BF)
            put(xs.at[i, j - 1], xr.at[i, j - 1], dev(xd, z, y, k), sem)

    def rs_end(n, i):
        pb, sib, xr = X[n].pb, X[n].sib, X[n].xr
        total = pb[i, k, x].astype(F32) + sib[i, x].astype(F32)
        arrived(xr.at[i], sums[n, i])
        for j in (1, 3, 2):
            total += xr[i, j - 1].astype(F32)
        return total

    def gather_start(buf, i, block):
        buf[i, t] = block
        mine = buf.at[i, t]
        rx = {j: new() for j in (1, 3, 2)}
        rk = new()
        for j in (1, 3, 2):
            put(mine, mine, dev(plus(x, j), z, y, k), rx[j])
        put(mine, mine, sibling, rk)
        return buf, i, rx, rk

    def gather_forward(state):
        if state is not None:
            buf, i, rx, rk = state
            for j in (1, 3, 2):
                slot = buf.at[i, 2 * plus(x, 4 - j) + k]
                arrived(slot, rx[j])
                put(slot, slot, sibling, rk)

    def gather_finish(state):
        if state is not None:
            buf, i, rx, rk = state
            arrived(buf.at[i, 0:4], rk)

    def nothing():
        pass

    def opened(states, n, work, early=nothing):
        gather_finish(states[0])
        work(0)
        gather_forward(states[1])
        rs_mid(n, 0)
        early()
        gather_finish(states[1])
        work(1)
        rs_mid(n, 1)

    def closed(rows_of, buf, between):
        first = gather_start(buf, 0, rows_of(0))
        second = gather_start(buf, 1, rows_of(1))
        between()
        gather_forward(first)
        return first, second

    def to_owners(i, rows, stage, landing, sem):
        for r in range(4):
            stage[i, r] = rows[:, 256 * r : 256 * r + 256]
        zd, yd = (z, y) if i == 0 else (3 - z, 3 - y)
        kd = lax.div(x, 2)
        first_row = pl.multiple_of(16 * (2 * lax.rem(x, 2) + k), 16)
        dst = landing.at[s, pl.ds(first_row, 16)]
        for j in range(4):
            xd = plus(x, j)
            if i == 0 and j == 0:
                put_or_keep(kd == k, stage.at[i, xd], dst, dev(xd, zd, yd, kd), sem)
            else:
                put(stage.at[i, xd], dst, dev(xd, zd, yd, kd), sem)

    def spread_tokens(src, dst):
        rows = pl.ds(4 * k, 4)
        close, mirrored = new(), new()
        put(src.at[1 - s], dst.at[1, rows], dev(x, 3 - z, 3 - y, k), mirrored)
        put(src.at[s], dst.at[0, rows], sibling, close)
        dst[0, rows] = src[s]
        return close, mirrored

    def spread_rest(dst, sems_):
        close, mirrored = sems_
        far = dst.at[1, pl.ds(4 * k, 4)]
        arrived(far, mirrored)
        put(far, far, sibling, close)
        arrived(dst.at[0], close)

    lane = lax.broadcasted_iota(I32, (1, 512), 1)
    own_block = 4 * z + y
    query_pos = 128 * jnp.where(lane < 256, own_block, 15 - own_block) + lax.rem(lane, 128)
    ids = R.seg[s]

    def tokens_to(n):
        return jnp.sum(jnp.where(ids <= n, 1.0, 0.0), axis=1, keepdims=True).astype(I32)

    first, second = tokens_to(0), tokens_to(1)
    query_start = jnp.where(query_pos < first, 0, jnp.where(query_pos < second, first, second))
    head_lane = lax.broadcasted_iota(I32, (128, 128), 1) < 64

    def two_heads(v):
        zero = jnp.zeros_like(v)
        return jnp.concatenate([jnp.where(head_lane, v, zero), jnp.where(head_lane, zero, v)], axis=0)

    def own_heads(vt):
        return jnp.concatenate([vt[0:64, 0:128], vt[64:128, 128:256]], axis=0)

    def gain_row(i):
        return R.gains[i : i + 1, :]

    def full(ref):
        return ref[...].reshape(256, 1024)

    def keys_of(l, zz):
        return L[l].kv[zz, :, :, :, 0:128].reshape(512, 128)

    def values_of(l, zz):
        return L[l].kv[zz, :, :, :, 128:256].reshape(512, 128)

    def attention_forward(l, states, hook, late, sent=nothing):
        kv = L[l].kv
        direct, relayed = ([{j: new() for j in (1, 2, 3)} for _ in streams] for _ in range(2))
        from_mate = [new() for _ in streams]
        for i in streams:
            if i == 1:
                gather_forward(states[1])
            gather_finish(states[i])
            a = S[2 * l].a[i].reshape(128, 1024)
            w = L[l].wqk
            if i == 0:
                arrived(w.at[0:3, :, :, 128:256], W[l].k)
            keys = nn(a, w[:, :, :, 128:256].reshape(1024, 128))
            w = L[l].wval
            if i == 0:
                arrived(w.at[0:3], W[l].v)
            u = nn(a, w[...].reshape(1024, 128))
            if l == 0:
                values = u.astype(BF)
            else:
                values = (0.5 * u + 0.5 * L[0].kv[z, yy, i, :, 128:256].astype(F32)).astype(BF)
            kv[z, yy, i, :, 0:128] = keys.astype(BF)
            kv[z, yy, i, :, 128:256] = values
            own = kv.at[z, yy, i]
            for j in (1, 3):
                put(own, own, dev(x, plus(z, j), y, k), direct[i][j])
            put(own, own, partner, from_mate[i])
            put(own, own, dev(x, plus(z, 2), y, k), direct[i][2])
        sent()
        for i in streams:
            near = kv.at[z, mate, i]
            arrived(near, from_mate[i])
            for j in (1, 3):
                put(near, near, dev(x, plus(z, j), y, k), relayed[i][j])
        w = L[l].wqk
        arrived(w.at[0:3, :, :, 0:128], W[l].q)
        for i in streams:
            q = nn(S[2 * l].a[i].reshape(128, 1024), w[:, :, :, 0:128].reshape(1024, 128)).astype(BF)
            L[l].q2[256 * i : 256 * i + 256, :] = two_heads((q * 0.125).astype(BF))
        scores = R.scores
        top = jnp.full((1, 512), MASKED, F32)
        for j in (0, 3, 1, 2):
            zz = plus(z, j)
            for i in streams:
                if j % 2:
                    arrived(kv.at[zz, yy, i], direct[i][4 - j])
                    arrived(kv.at[zz, mate, i], relayed[i][4 - j])
                elif j:
                    arrived(kv.at[zz, mate, i], relayed[i][2])
            if j == 1:
                hook()
            scores[4 * j : 4 * j + 4] = nt(keys_of(l, zz), L[l].q2[...]).reshape(4, 128, 512)

            def mask(i, top, j=j, zz=zz):
                block = 4 * zz + 2 * s + lax.div(i, 2)
                base = 128 * (block + lax.rem(i, 2) * (15 - 2 * block))
                row = lax.broadcasted_iota(I32, (128, 512), 0)
                seen = (row >= query_start - base) & (row <= query_pos - base)
                v = jnp.where(seen, scores[4 * j + i], MASKED)
                scores[4 * j + i] = v
                return jnp.maximum(top, jnp.max(v, axis=0, keepdims=True))

            top = lax.fori_loop(0, 4, mask, top)
            if j == 0:
                for i in streams:
                    opposite = kv.at[plus(z, 2), yy, i]
                    arrived(opposite, direct[i][2])
                    put(opposite, opposite, partner, relayed[i][2])
        prob = L[l].prob
        for i in streams:
            lanes = slice(256 * i, 256 * i + 256)
            high = top[:, lanes]

            def expo(r, total):
                v = jnp.exp(scores[r, :, lanes] - high)
                prob[r, :, lanes] = v.astype(BF)
                return total + jnp.sum(v, axis=0, keepdims=True)

            share = 1.0 / lax.fori_loop(0, 16, expo, jnp.zeros((1, 256), F32))
            L[l].share[0:1, lanes] = share
            ot = jnp.zeros((128, 256), F32)
            for j in range(4):
                ot += tn(values_of(l, plus(z, j)), prob[4 * j : 4 * j + 4, :, lanes].reshape(512, 256))
            ot = ot * share
            ot = own_heads(ot)
            L[l].ot[:, 128 * i : 128 * i + 128] = ot
            o = jnp.transpose(ot).astype(BF)
            if i == 0:
                arrived(L[l].wout.at[0:3], W[l].o)
            part = jnp.concatenate([nn(o, L[l].wout[r].reshape(128, 256)) for r in range(4)], axis=1)
            rs_start(2 * l, i, part)
        for i in streams:
            rs_mid(2 * l, i)
        late()

    def feedforward_forward(l, states, early, hook):
        w = L[l].wgu

        def work(i):
            a = S[2 * l + 1].a[i].reshape(128, 1024)
            if i == 0:
                ring_end(W[l].gate)
            gate = nn(a, w[:, :, :, :, 0:384].reshape(1024, 384))
            if i == 0:
                ring_end(W[l].up)
            up = nn(a, w[:, :, :, :, 384:768].reshape(1024, 384))
            rows = slice(128 * i, 128 * i + 128)
            L[l].gu[rows, 0:384] = gate
            L[l].gu[rows, 384:768] = up
            hidden = (gate * jax.nn.sigmoid(gate) * up).astype(BF)
            L[l].hid[rows, :] = hidden
            if i == 0:
                ring_end(W[l].d)
            part = jnp.concatenate([nn(hidden, L[l].wdn[r].reshape(384, 256)) for r in range(4)], axis=1)
            rs_start(2 * l + 1, i, part)

        opened(states, 2 * l + 1, work, early)
        hook()

    def next_rows(n, between=nothing):
        def rows_of(i):
            rows = (S[n].h[i].astype(F32) + rs_end(n, i)).astype(BF)
            S[n + 1].h[i] = rows
            normed, _ = normalize(rows.astype(F32))
            return (normed * gain_row(n + 1)).astype(BF)

        return closed(rows_of, S[n + 1].a, between)

    def norm_backward(n, i):
        da = rs_end(4 + n, i)
        normed, inverse = normalize(S[n].h[i].astype(F32))
        gain_part = jnp.sum(da * normed, axis=0, keepdims=True)
        if n == 0:
            pass
        elif i == 0:
            R.gg[n : n + 1, :] = gain_part
        else:
            R.gg[n : n + 1, :] += gain_part
        scaled = da * gain_row(n)
        mixed = scaled - normed * jnp.mean(scaled * normed, axis=-1, keepdims=True)
        return (S[n].gr[i].astype(F32) + inverse * mixed).astype(BF)

    def hand_back(n, between=nothing):
        def rows_of(i):
            rows = norm_backward(n, i)
            S[n - 1].gr[i] = rows
            return rows

        return closed(rows_of, S[n - 1].gb, between)

    def send_z(g, landing):
        sem = new()
        for j in (1, 3, 2):
            zd = plus(z, j)
            put(g.at[zd], landing.at[j - 1], dev(x, zd, y, k), sem)
        return sem

    def send_y(g, landing):
        sem = new()
        for j in (1, 3, 2):
            yd = plus(y, j)
            put(g.at[:, yd], landing.at[j - 1], dev(x, z, yd, k), sem)
        return sem

    def attention_backward(l, states, hook):
        n = 2 * l
        wo, dkv, prob = L[l].wout, L[l].dkv, L[l].prob
        ab, own_ab, c_sem = {j: new() for j in (1, 3)}, {j: new() for j in (1, 3)}, new()
        dq = []
        for i in streams:
            if i == 1:
                gather_forward(states[1])
            gather_finish(states[i])
            gb = S[n].gb[i].reshape(128, 1024)
            dot_ = nt(wo[0].reshape(128, 256), gb[:, 0:256])
            for r in range(1, 4):
                dot_ += nt(wo[r].reshape(128, 256), gb[:, 256 * r : 256 * r + 256])
            dot_ = dot_.astype(BF).astype(F32)
            do2 = two_heads(jnp.transpose(dot_).astype(BF))
            share = L[l].share[0:1, 256 * i : 256 * i + 256]
            head_row = lax.broadcasted_iota(I32, (128, 128), 0) < 64
            scaled = dot_ * jnp.where(head_row, share[:, 0:128], share[:, 128:256])
            R.do2[256 * i : 256 * i + 256, :] = two_heads(jnp.transpose(scaled).astype(BF))
            prod = dot_ * L[l].ot[:, 128 * i : 128 * i + 128]
            delta = jnp.concatenate(
                [jnp.sum(prod[0:64], axis=0, keepdims=True), jnp.sum(prod[64:128], axis=0, keepdims=True)], axis=1
            )
            lanes = slice(256 * i, 256 * i + 256)
            dqt = jnp.zeros((128, 256), F32)
            for j in (2, 1, 3, 0):
                zz = plus(z, j)
                p = prob[4 * j : 4 * j + 4, :, lanes].reshape(512, 256)
                dp = nt(values_of(l, zz), do2)
                ds = (p.astype(F32) * ((dp - delta) * share)).astype(BF)
                R.ds[j, :, lanes] = ds
                if i == 1:
                    p = prob[4 * j : 4 * j + 4].reshape(512, 512)
                    dkv[zz, :, :, 0:128] = nn(R.ds[j], L[l].q2[...]).astype(BF).reshape(2, 256, 128)
                    dkv[zz, :, :, 128:256] = nn(p, R.do2[...]).astype(BF).reshape(2, 256, 128)
                    if j % 2:
                        put(dkv.at[zz, mate], L[l].dkvab.at[j // 2, mate], dev(x, zz, y, k), ab[j])
                    elif j:
                        put(dkv.at[zz, mate], L[l].dkvc, partner, c_sem)
                dqt += tn(keys_of(l, zz), ds)
                if i == 1 and j == 3:
                    for r in (1, 3):
                        put(dkv.at[plus(z, r), yy], L[l].dkvab.at[r // 2, yy], dev(x, plus(z, r), y, k), own_ab[r])
            dq.append(jnp.transpose(own_heads(dqt) * 0.125).astype(BF))
        dq = jnp.concatenate(dq, axis=0)
        gb = full(S[n].gb)
        arrived(L[l].dkvc, c_sem)
        far = plus(z, 2)
        L[l].dkvds[...] = (dkv[far, yy].astype(F32) + L[l].dkvc[...].astype(F32)).astype(BF)
        d_sem, e_sem = new(), new()
        put(L[l].dkvds, L[l].dkvd, dev(x, far, y, k), d_sem)
        got = L[l].dkvab
        arrived(got.at[0, mate], ab[1])
        arrived(got.at[1, mate], ab[3])
        L[l].dkves[...] = (dkv[z, mate].astype(F32) + got[0, mate].astype(F32) + got[1, mate].astype(F32)).astype(BF)
        put(L[l].dkves, L[l].dkve, partner, e_sem)
        gw = L[l].gwout
        otb = L[l].ot[...].astype(BF)
        for i in range(4):
            gw[i] = nn(otb, gb[:, 256 * i : 256 * i + 256]).astype(BF).reshape(4, 32, 256)
        at = jnp.transpose(full(S[n].a))
        if l == 0:
            G[l].o = send_z(L[l].gwout, L[l].rzout)
        arrived(got.at[0, yy], own_ab[1])
        arrived(got.at[1, yy], own_ab[3])
        tot = dkv[z, yy].astype(F32) + got[0, yy].astype(F32) + got[1, yy].astype(F32)
        arrived(L[l].dkvd, d_sem)
        arrived(L[l].dkve, e_sem)
        tot = tot + L[l].dkvd[...].astype(F32) + L[l].dkve[...].astype(F32)
        dk = tot[:, 0:128].astype(BF)
        dvals = tot[:, 128:256]
        if l == 1:
            half = 0.5 * dvals.astype(BF).astype(F32)
            du = half.astype(BF)
            R.dmh[...] = du
        else:
            du = (dvals + R.dmh[...].astype(F32)).astype(BF)
        def send_grads():
            grads = nn(at, jnp.concatenate([dq, du, dk], axis=1)).astype(BF)
            L[l].gwv[...] = grads[:, 0:256].reshape(4, 4, 2, 32, 256)
            L[l].gwk[...] = grads[:, 256:384].reshape(4, 8, 32, 128)
            G[l].k = send_z(L[l].gwk, L[l].rzk)
            G[l].v = send_y(L[l].gwv, L[l].ryv)

        if l == 0:
            send_grads()
        for i in streams:
            rows = slice(128 * i, 128 * i + 128)
            da = nt(jnp.concatenate([dq[rows], dk[rows]], axis=1), L[l].wqk[...].reshape(1024, 256))
            da += nt(du[rows], L[l].wval[...].reshape(1024, 128))
            rs_start(4 + n, i, da)
            if l == 0:
                gain_part = jnp.sum(da * R.normed[rows, :], axis=0, keepdims=True)
                if i == 0:
                    R.gg[0:1, :] = gain_part
                else:
                    R.gg[0:1, :] += gain_part
        if l == 0:
            for j in (1, 3, 2):
                put(R.gg, R.ggx.at[j - 1], dev(plus(x, j), z, y, k), landed.gx)
        for i in streams:
            rs_mid(4 + n, i)
        if l == 1:
            send_grads()
        if l == 1:
            G[l].o = send_z(L[l].gwout, L[l].rzout)
        hook()

    def feedforward_backward(l, states, hook):
        n = 2 * l + 1

        def work(i):
            gb = S[n].gb[i].reshape(128, 1024)
            wd = L[l].wdn
            dhid = nt(gb[:, 0:256], wd[0].reshape(384, 256))
            for r in range(1, 4):
                dhid += nt(gb[:, 256 * r : 256 * r + 256], wd[r].reshape(384, 256))
            gu = L[l].gu[128 * i : 128 * i + 128, :]
            gate, up = gu[:, 0:384], gu[:, 384:768]
            sig = jax.nn.sigmoid(gate)
            dgate = dhid * up * sig * (1.0 + gate * (1.0 - sig))
            dup = dhid * (gate * sig)
            dgu = jnp.concatenate([dgate.astype(BF), dup.astype(BF)], axis=1)
            R.dgu[i] = dgu
            rs_start(4 + n, i, nt(dgu, L[l].wgu[...].reshape(1024, 768)))

        opened(states, 4 + n, work)
        at = jnp.transpose(full(S[n].a))
        gw = L[l].gwgu
        gw[...] = nn(at, R.dgu[...].reshape(256, 768)).astype(BF).reshape(4, 4, 2, 32, 768)
        far = plus(y, 2)
        G[l].g = [new() for _ in range(4)]
        put(gw.at[0:2, far], L[l].hygu.at[0], at_y(1), G[l].g[0])
        put(gw.at[2:4, far], L[l].hygu.at[1], at_y(3), G[l].g[1])
        gb = full(S[n].gb)
        ht = jnp.transpose(L[l].hid[...])
        gw = L[l].gwdn
        for i in range(4):
            gw[i] = nn(ht, gb[:, 256 * i : 256 * i + 256]).astype(BF).reshape(4, 96, 256)
        far = plus(z, 2)
        G[l].d = [new() for _ in range(4)]
        put(gw.at[far, 0:2], L[l].hzdn.at[0], at_z(1), G[l].d[0])
        put(gw.at[far, 2:4], L[l].hzdn.at[1], at_z(3), G[l].d[1])
        hook()

    def ff_push(l):
        gu, dn, hg, hd = L[l].gwgu, L[l].gwdn, L[l].hygu, L[l].hzdn
        for h, j in ((0, 1), (1, 3)):
            yd, zd, half = plus(y, j), plus(z, j), slice(2 * h, 2 * h + 2)
            arrived(hg.at[h], G[l].g[h])
            gu[half, yd] = (gu[half, yd].astype(F32) + hg[h].astype(F32)).astype(BF)
            put(gu.at[:, yd], L[l].bygu.at[h], at_y(j), G[l].g[2 + h])
            arrived(hd.at[h], G[l].d[h])
            dn[zd, half] = (dn[zd, half].astype(F32) + hd[h].astype(F32)).astype(BF)
            put(dn.at[zd], L[l].bzdn.at[h], at_z(j), G[l].d[2 + h])

    def summed(own, got):
        return own.astype(F32) + got[0].astype(F32) + got[1].astype(F32) + got[2].astype(F32)

    def rows_back(st, land):
        sem = new()
        for j in range(4):
            m = plus(slot_m, j)
            to = dev(x, z, 2 * k + lax.div(m, 2), lax.rem(m, 2))
            if j == 0:
                put_or_keep(s == k, st.at[m], land.at[y], to, sem)
            else:
                put(st.at[m], land.at[y], to, sem)
        return sem

    def four(land):
        return land[0].astype(F32) + land[1].astype(F32) + land[2].astype(F32) + land[3].astype(F32)

    def out_second(l):
        arrived(L[l].rzout, G[l].o)
        L[l].sout[...] = summed(L[l].gwout[z], L[l].rzout).astype(BF)
        G[l].o = rows_back(L[l].sout, L[l].yout)

    def out_third(l):
        arrived(L[l].yout, G[l].o)
        L[l].cout[...] = four(L[l].yout).astype(BF)
        G[l].o = cross_first(L[l].cout, L[l].fout)

    def out_end(l):
        arrived(L[l].fout, G[l].o)
        L[l].oo[...] = L[l].fout[...].astype(F32)
        leave(L[l].oo, far_l[l].oo)

    def down_second(l):
        got = L[l].bzdn
        arrived(got.at[0], G[l].d[2])
        arrived(got.at[1], G[l].d[3])
        L[l].sdn[...] = (L[l].gwdn[z].astype(F32) + got[0].astype(F32) + got[1].astype(F32)).astype(BF)
        G[l].d = rows_back(L[l].sdn, L[l].ydn)

    def down_third(l):
        arrived(L[l].ydn, G[l].d)
        L[l].cdn[...] = four(L[l].ydn).astype(BF)
        G[l].d = cross_first(L[l].cdn, L[l].fdn)

    def down_end(l):
        arrived(L[l].fdn, G[l].d)
        L[l].od[...] = L[l].fdn[0:88, :].astype(F32)
        leave(L[l].od, far_l[l].od)

    def rows_y(g, got, st, land, sem):
        arrived(got, sem)
        st[...] = summed(g[z], got).astype(BF)
        sem = new()
        land[0] = st[2 * y + k]
        for j in (2, 6, 4, 3, 7, 5, 1):
            yd, kd = plus(y, j // 2), flip(j)
            put(st.at[2 * yd + kd], land.at[j], dev(x, z, yd, kd), sem)
        return sem

    def rows_z(st, land):
        sem = new()
        land[0] = st[z, k]
        for j in (2, 6, 4, 3, 7, 5, 1):
            zd, kd = plus(z, j // 2), flip(j)
            put(st.at[zd, kd], land.at[j], dev(x, zd, y, kd), sem)
        return sem

    def halves(land, sem):
        if sem is not None:
            arrived(land.at[1:8], sem)
        own = land[0].astype(F32) + land[2].astype(F32) + land[4].astype(F32) + land[6].astype(F32)
        far = land[1].astype(F32) + land[3].astype(F32) + land[5].astype(F32) + land[7].astype(F32)
        return jnp.where(k == 0, own, far), jnp.where(k == 0, far, own)

    def k_second(l):
        G[l].k = rows_y(L[l].gwk, L[l].rzk, L[l].sk, L[l].fk, G[l].k)

    def v_grad_second(l):
        g, got, st = L[l].gwv, L[l].ryv, L[l].sv
        arrived(got, G[l].v)
        for i in range(4):
            own = g[i, y].astype(F32) + got[0, i].astype(F32) + got[1, i].astype(F32) + got[2, i].astype(F32)
            st[i] = own.astype(BF)
        G[l].v = rows_z(st, L[l].fv)

    def gu_grad_second(l):
        g, got, st = L[l].gwgu, L[l].bygu, L[l].sgu
        arrived(got.at[0], G[l].g[2])
        arrived(got.at[1], G[l].g[3])
        for i in range(4):
            st[i] = (g[i, y].astype(F32) + got[0, i].astype(F32) + got[1, i].astype(F32)).astype(BF)
        G[l].g = rows_z(st, L[l].fgu)

    def att_end(l):
        f = far_l[l]
        arrived(L[l].fv.at[1:8], G[l].v)
        for land, result, sem, to in (
            (L[l].fk, L[l].ok, G[l].k, f.ok),
            (L[l].fv.at[:, :, 0:128], L[l].oq, None, f.oq),
            (L[l].fv.at[:, :, 128:256], L[l].ov, None, f.ov),
        ):
            low, high = halves(land, sem)
            result[:, 0:128] = low
            result[:, 128:256] = high
            leave(result, to)

    def gu_end(l):
        low, high = halves(L[l].fgu, G[l].g)
        both = jnp.concatenate(
            [
                jnp.concatenate([low[:, 0:384], high[:, 0:384]], axis=1),
                jnp.concatenate([low[:, 384:768], high[:, 384:768]], axis=1),
            ],
            axis=0,
        )
        main = both.astype(BF)
        rest = (both - main.astype(F32)).astype(BF)
        both = nt(main, R.pick[...]) + nt(rest, R.pick[...])
        L[l].og[...] = both[0:32]
        L[l].ou[...] = both[32:64]
        leave(L[l].og, far_l[l].og)
        leave(L[l].ou, far_l[l].ou)

    def nothing():
        pass

    def att_first(l):
        qk_first(l)
        W[l].v = z_first(L[l].vst, L[l].wval)
        W[l].o = cross_first(L[l].wo, L[l].cwo)

    def ff_first(l):
        W[l].gu = z_first(L[l].gus, L[l].wgu)
        W[l].d = cross_first(L[l].wds, L[l].cwd)

    qk_first(0)
    W[0].v = z_first(L[0].vst, L[0].wval)
    xin_coming.wait()
    in_sems = spread_tokens(R.xin, R.hin)
    gx_sem = new()
    for j in (1, 3, 2):
        put(R.gst, R.gx.at[j - 1], dev(plus(x, j), z, y, k), gx_sem)
    W[0].o = cross_first(L[0].wo, L[0].cwo)
    wait_for(later)
    pack_rest()
    ff_first(0)
    arrived(R.gx, gx_sem)
    R.g1[...] = R.gst[...] + R.gx[0] + R.gx[1] + R.gx[2]
    gy_sem = new()
    R.gyr[2 * y + k] = R.g1[...]
    for j in range(1, 8):
        put(R.g1, R.gyr.at[2 * y + k], dev(x, z, plus(y, j // 2), flip(j)), gy_sem)
    qk_second(0)
    v_second(0)
    W[0].o = cross_second(L[0].cwo, L[0].wout, W[0].o)
    arrived(R.gyr.at[0:7], gy_sem)
    for i in range(2):
        R.gz[z, i] = R.gyr[4 * i] + R.gyr[4 * i + 1] + R.gyr[4 * i + 2] + R.gyr[4 * i + 3]
    gz_sem = to_z(R.gz.at[z], R.gz.at[z])
    spread_rest(R.hin, in_sems)
    normed, _ = normalize(full(R.hin).astype(F32))
    R.normed[...] = normed
    for i in streams:
        S[0].h[i] = R.hin[i, t]
    gate_start(0)
    arrived(R.gz.at[0:3], gz_sem)
    R.gains[...] = jnp.concatenate([R.gz[i // 2, i % 2] for i in range(8)], axis=1)
    S[0].a[...] = (normed * gain_row(0)).astype(BF).reshape(2, 8, 16, 1024)
    cot_sems = []

    def after_sends_0():
        W[0].o = cross_third(L[0].wout, W[0].o)
        W[0].d = cross_second(L[0].cwd, L[0].wdn, W[0].d)

    def after_keys_0():
        ring_relay(W[0].gate)
        up_start(0)
        down_start(0)
        att_first(1)
        ff_first(1)

    def in_gather_0():
        ring_relay(W[0].up)
        ring_relay(W[0].d)

    def in_ff_0():
        qk_second(1)
        v_second(1)

    def after_ff_0():
        W[1].o = cross_second(L[1].cwo, L[1].wout, W[1].o)
        gate_start(1)
        W[1].d = cross_second(L[1].cwd, L[1].wdn, W[1].d)

    def in_gather_1():
        W[1].o = cross_third(L[1].wout, W[1].o)

    def after_keys_1():
        ring_relay(W[1].gate)
        up_start(1)
        down_start(1)

    def after_att_1():
        cot_sems.append(spread_tokens(R.cot, S[3].gb))

    def in_gather_2():
        ring_relay(W[1].up)
        ring_relay(W[1].d)

    def take_cotangent():
        spread_rest(S[3].gb, cot_sems[0])
        for i in streams:
            S[3].gr[i] = S[3].gb[i, t]

    landed = SimpleNamespace(out=new(), ing=new(), gx=new())

    def finish_outputs():
        for i in streams:
            rows = (S[3].h[i].astype(F32) + rs_end(3, i)).astype(BF)
            to_owners(i, rows, R.outst, R.outrv, landed.out)

    none = (None, None)
    attention_forward(0, none, after_keys_0, nothing, after_sends_0)
    feedforward_forward(0, next_rows(0, in_gather_0), in_ff_0, after_ff_0)
    attention_forward(1, next_rows(1, in_gather_1), after_keys_1, after_att_1)
    feedforward_forward(1, next_rows(2, in_gather_2), nothing, take_cotangent)

    def ff_grads(l):
        gu_grad_second(l)
        down_second(l)

    def att_grads():
        out_second(1)
        k_second(1)
        v_grad_second(1)

    def last_grads():
        ff_grads(0)

    def after_grads_1():
        att_grads()
        ff_grads(1)

    def after_grads_0():
        last_grads()
        att_end(1)
        down_third(1)
        gu_end(1)

    feedforward_backward(1, none, finish_outputs)
    attention_backward(1, hand_back(3), lambda: ff_push(1))
    states = hand_back(2)
    feedforward_backward(0, states, after_grads_1)
    states = hand_back(1, lambda: ff_push(0))
    out_third(1)
    attention_backward(0, states, after_grads_0)
    arrived(R.ggx, landed.gx)
    gg = R.gg[...] + R.ggx[0] + R.ggx[1] + R.ggx[2]
    for i in range(4):
        R.ggz[i] = gg[:, 256 * i : 256 * i + 256]
    gg_sem = new()
    for j in (1, 3, 2):
        zd = plus(z, j)
        put(R.ggz.at[zd], R.ggzr.at[j - 1], dev(x, zd, y, k), gg_sem)
    for i in streams:
        to_owners(i, norm_backward(0, i), R.ingst, R.ingrv, landed.ing)
    arrived(R.ggzr, gg_sem)
    gg = R.ggz[z] + R.ggzr[0] + R.ggzr[1] + R.ggzr[2]
    R.ggy[0] = gg[:, 0:128]
    R.ggy[1] = gg[:, 128:256]
    gg_sem = new()
    R.ggyr[0] = R.ggy[s]
    for j in range(1, 8):
        yd = plus(y, j // 2)
        put(R.ggy.at[lax.div(yd, 2)], R.ggyr.at[j], dev(x, z, yd, flip(j)), gg_sem)
    k_second(0)
    v_grad_second(0)
    out_second(0)
    down_third(0)
    out_third(0)
    out_end(1)
    down_end(1)
    gu_end(0)
    arrived(R.outrv, landed.out)
    R.out[...] = R.outrv[...].reshape(2, 1, 64, 256)
    leave(R.out, far_r.out)
    arrived(R.ingrv, landed.ing)
    R.ing[...] = R.ingrv[...].reshape(2, 1, 64, 256)
    leave(R.ing, far_r.ing)
    att_end(0)
    out_end(0)
    down_end(0)
    arrived(R.ggyr.at[1:8], gg_sem)
    gg = R.ggyr[0]
    for j in range(1, 8):
        gg = gg + R.ggyr[j]
    gg = jnp.sum(jnp.where(lax.broadcasted_iota(I32, (8, 128), 0) == x, gg, 0.0), axis=0, keepdims=True)
    part = lax.rem(c, 4)
    gain = jnp.zeros((1, 32), F32)
    for i in range(4):
        gain += jnp.where(part == i, gg[:, 32 * i : 32 * i + 32], 0.0)
    R.ogg[...] = gain
    wait_for(leaving)
    for copy in pending:
        copy.wait_send()
    for mine, copy in kept:

        @pl.when(jnp.logical_not(mine))
        def _(copy=copy):
            copy.wait_send()

    assert used[0] <= N_SEM, used


def call(*args):
    arguments, results, scratch = groups()
    return pl.pallas_call(
        kernel,
        out_shape=[jax.ShapeDtypeStruct(shape, dtype) for shape, dtype in specs_of(results)],
        in_specs=blocks_of(arguments),
        out_specs=blocks_of(results),
        scratch_shapes=[pltpu.VMEM(shape, dtype) for shape, dtype in specs_of(scratch)]
        + [pltpu.SemaphoreType.DMA((N_SEM,))],
        compiler_params=pltpu.CompilerParams(
            collective_id=0, has_side_effects=True, vmem_limit_bytes=62 * 1024 * 1024
        ),
    )(*args)


def hand_out(*refs):
    n = len(refs) // 2
    copies = [pltpu.make_async_copy(refs[i], refs[n + i], refs[-1].at[i]) for i in range(n)]
    for copy in copies:
        copy.start()
    for copy in copies:
        copy.wait()


def body(inputs, cotangent, segment_ids, gains, *weights):
    first = (inputs.reshape(2, 4, 16, 1024), cotangent.reshape(2, 4, 16, 1024), segment_ids, gains)
    results = call(*first, *weights)
    anywhere = pl.BlockSpec(memory_space=pl.ANY)
    return tuple(
        pl.pallas_call(
            hand_out,
            out_shape=[jax.ShapeDtypeStruct(r.shape, r.dtype) for r in results],
            in_specs=[pl.BlockSpec(memory_space=pltpu.VMEM)] * len(results),
            out_specs=[anywhere] * len(results),
            scratch_shapes=[pltpu.SemaphoreType.DMA((len(results),))],
        )(*results)
    )


def solution(mesh):
    tokens = P(None, None, "ctx", None)
    weight = P("ctx", "section")
    return jax.shard_map(
        body,
        mesh=mesh,
        in_specs=(tokens, tokens, P(), P("section", "ctx")) + (weight,) * 14,
        out_specs=(P(None, None, "ctx", "section"),) * 2 + (P("section", "ctx"),) + (weight,) * 14,
        check_vma=False,
    )
```
